32 devices in a mesh: rep: 4 (over y, x), shard: 8 (over z, core).
Axes of the slice: x: 2, y: 2, z: 4, core: 2. Of those that a mesh axis runs over, the one named last changes fastest.
Arguments:
- streams: bfloat16 [5120, 4, 2048], P(('rep', 'shard')), may hold values from -6 to 6
- cotangent: bfloat16 [5120, 4, 2048], P(('rep', 'shard')), may hold values from -6 to 6
- lengths: int32 [4, 2], P('rep'), may hold values from 1 to 1024, 1280 in all within a row
- packed_at: int32 [4, 1280], P('rep'), may hold values from 0 to 1279, each once within a row
- query_weight: bfloat16 [2048, 2048], P('shard'), may hold values from -0.125 to 0.125
- key_weight: bfloat16 [2048, 2048], P('shard'), may hold values from -0.125 to 0.125
- value_weight: bfloat16 [2048, 2048], P('shard'), may hold values from -0.125 to 0.125
- output_weight: bfloat16 [2048, 2048], P('shard'), may hold values from -0.5 to 0.5
- gate_weight: bfloat16 [2048, 8192], P('shard'), may hold values from -0.125 to 0.125
- up_weight: bfloat16 [2048, 8192], P('shard'), may hold values from -0.125 to 0.125
- down_weight: bfloat16 [8192, 2048], P('shard'), may hold values from -0.0625 to 0.0625
- mixing_weight: bfloat16 [2, 2048, 6], P(None, 'shard'), may hold values from -0.125 to 0.125
- mixing_static: float32 [2, 4, 6], replicated, may hold values from -0.5 to 0.5
Outputs:
- streams_out: bfloat16 [5120, 4, 2048], P(('rep', 'shard'))
- grad_streams: float32 [5120, 4, 2048], P(('rep', 'shard'))
- grad_query: float32 [2048, 2048], P('shard')
- grad_key: float32 [2048, 2048], P('shard')
- grad_value: float32 [2048, 2048], P('shard')
- grad_output: float32 [2048, 2048], P('shard')
- grad_gate: float32 [2048, 8192], P('shard')
- grad_up: float32 [2048, 8192], P('shard')
- grad_down: float32 [8192, 2048], P('shard')
- grad_mixing: float32 [2, 2048, 6], P(None, 'shard')
- grad_static: float32 [2, 4, 6], replicated
The draws below stay inside these ranges and needn't reach their ends.
Inputs may be any that keep to these rules, and one draw needn't show every extreme that they name: `lengths`: each row sums to 1280. `packed_at`: each row is a permutation of 0 to 1279.
All inputs are finite; a program needn't handle non-finite values.
Results may differ from the reference program's by a relative error of at most 0.024.
Values may be sent and summed in bfloat16 or wider, within the bound.
No kernel may reach another device: no remote copies, remote signals or barrier semaphores. Data moves between devices by JAX's collectives and lax.ppermute only.
A program may use at most 576 MiB of HBM per device.

```python
import math
import jax
import jax.numpy as jnp
import numpy as np
from jax import lax

D = 2048
HEADS = 16
FF = 8192
HEAD_DIM = 128
STREAMS = 4
MIX_COLS = 6
MAXLEN = 1024
GROUP_TOK = 1280
NSEQ = 2
TOKENS = 5120
N_REP = 4


def steps_of(rng, shape, shards, low, largest):
    def one(dim, parts):
        steps = jax.random.uniform(jax.random.fold_in(jax.random.fold_in(rng, 6), dim), (parts,), jnp.float32, low / len(shards), largest / len(shards))
        return jnp.repeat(jnp.exp(steps), shape[dim] // parts).reshape((-1,) + (1,) * (len(shape) - dim - 1))

    gain = one(*shards[0])
    for cut in shards[1:]:
        gain = gain * one(*cut)
    return gain


def length_profile(amount, total, limit, skew):
    weights = [(1 << 20) // math.isqrt(rank ** skew) + 1 for rank in range(2, amount + 1)]
    surplus, holding = total - limit - (amount - 1), [1] * (amount - 1)
    while surplus > 0:
        candidates = [i for i in range(amount - 1) if holding[i] < limit]
        whole, left = sum([weights[i] for i in candidates]), surplus
        for i in candidates:
            addition = min(limit - holding[i], max(1, left * weights[i] // whole), surplus)
            holding[i] = holding[i] + addition
            surplus = surplus - addition
    return np.array([limit] + holding)


def ragged(own_key, number_of, total, reach, skew):
    if number_of == 2:
        one = jax.random.randint(own_key, (), max(1, total - reach), min(reach, total - 1) + 1)
        return jnp.stack([one, total - one])
    sizes = jnp.asarray(length_profile(number_of, total, reach, skew), jnp.int32)
    pairs = (number_of - 1) // 2
    donor, sink = sizes[1:1 + 2 * pairs:2], sizes[2:2 + 2 * pairs:2]
    room = jnp.minimum(donor - 1, reach - sink)
    passed = jax.random.randint(jax.random.fold_in(own_key, 1), (pairs,), 0, 1 << 20) % (room + 1)
    sizes = sizes.at[1:1 + 2 * pairs:2].set(donor - passed).at[2:2 + 2 * pairs:2].set(sink + passed)
    return sizes[jax.random.permutation(jax.random.fold_in(own_key, 2), number_of)]


def noise(rng, dims, deviation, most, split=(), held_as=jnp.bfloat16):
    values = jax.random.normal(rng, dims, jnp.float32) * deviation
    if len(split) > 0:
        values = steps_of(rng, dims, split, -0.22, 0.18) * values
    return jnp.clip(values, min=-most, max=most).astype(held_as)


def setup_inputs(seed: int = 0) -> dict:
    arg_keys = jax.random.split(jax.random.key(seed), 14)
    return {
        "streams": noise(arg_keys[0], (TOKENS, STREAMS, D), 1.0, 6.0, ((0, 32),)),
        "cotangent": noise(arg_keys[1], (TOKENS, STREAMS, D), 1.0, 6.0, ((0, 32),)),
        "lengths": jax.vmap(lambda own: ragged(own, NSEQ, GROUP_TOK, MAXLEN, 2))(jax.random.split(arg_keys[2], N_REP)).reshape((N_REP, NSEQ)).astype(jnp.int32),
        "packed_at": jax.vmap(lambda own: jax.random.permutation(own, GROUP_TOK))(jax.random.split(arg_keys[3], N_REP)).reshape((N_REP, GROUP_TOK)).astype(jnp.int32),
        "query_weight": noise(arg_keys[4], (D, D), D ** -0.5, 0.125, ((0, 8),)),
        "key_weight": noise(arg_keys[5], (D, D), D ** -0.5, 0.125, ((0, 8),)),
        "value_weight": noise(arg_keys[6], (D, D), D ** -0.5, 0.125, ((0, 8),)),
        "output_weight": noise(arg_keys[7], (D, D), (D // 16) ** -0.5, 0.5, ((0, 8),)),
        "gate_weight": noise(arg_keys[8], (D, FF), D ** -0.5, 0.125, ((0, 8),)),
        "up_weight": noise(arg_keys[9], (D, FF), D ** -0.5, 0.125, ((0, 8),)),
        "down_weight": noise(arg_keys[10], (FF, D), FF ** -0.5, 0.0625, ((0, 8),)),
        "mixing_weight": noise(arg_keys[11], (2, D, MIX_COLS), D ** -0.5, 0.125, ((1, 8),)),
        "mixing_static": jnp.clip(jax.random.uniform(arg_keys[12], (2, STREAMS, MIX_COLS), jnp.float32, -0.5, 0.5), -0.5, 0.5),
    }


EPSILON = 1e-05
NEGATIVE = -1e+30
HIGHEST = lax.Precision.HIGHEST

@jax.custom_vjp
def low(v):
    return lax.optimization_barrier(v.astype(jnp.bfloat16)).astype(jnp.float32)

@jax.custom_vjp
def low_back(v):
    return v

def low_keep(v):
    return (low(v), None)

def low_pass(kept, grad):
    return (grad,)

def back_keep(v):
    return (v, None)

def back_low(kept, grad):
    return (low(grad),)
low.defvjp(low_keep, low_pass)
low_back.defvjp(back_keep, back_low)

def layer_norm(values):
    centred = values - lax.optimization_barrier(jnp.mean(values, axis=-1, keepdims=True))
    spread = lax.optimization_barrier(jnp.mean(centred * centred, axis=-1, keepdims=True))
    return centred * lax.rsqrt(spread + EPSILON)

def mixing(stream_values, weight, static):
    normed = layer_norm(stream_values)
    coefficients = static + jnp.tanh(jnp.einsum('tnd,dc->tnc', normed, weight, precision=HIGHEST))
    entering = jnp.einsum('tn,tnd->td', coefficients[:, :, 0], stream_values, precision=HIGHEST)
    carried = jnp.einsum('tnj,tnd->tjd', coefficients[:, :, 1:-1], stream_values, precision=HIGHEST)
    return (layer_norm(entering), carried, coefficients[:, :, -1])

def sequence_meta(ordering, lengths):
    ending = jnp.cumsum(lengths).astype(jnp.int32)
    segment = lax.optimization_barrier(jnp.sum((ordering[:, None] >= ending[None, :]).astype(jnp.int32), axis=1)).astype(jnp.int32)
    opening = (ending - lengths).astype(jnp.int32)
    chosen = segment[:, None] == jnp.arange(lengths.shape[0], dtype=jnp.int32)[None, :]
    first_place = lax.optimization_barrier(jnp.sum(jnp.where(chosen, opening[None, :], 0), axis=1)).astype(jnp.int32)
    return (segment, (ordering - first_place).astype(jnp.int32))

def rope_tables(position, head_width):
    middle = head_width // 2
    frequency = jnp.exp(jnp.arange(middle, dtype=jnp.float32) * (-2.0 * math.log(10000.0) / head_width))
    angles = position.astype(jnp.float32)[:, None] * frequency[None, :]
    angles = jnp.concatenate([angles, angles], axis=1)
    return (jnp.cos(angles), jnp.sin(angles))

def rotate(values, cosine, sine_part):
    middle = values.shape[-1] // 2
    turned = jnp.concatenate([-values[..., middle:], values[..., :middle]], axis=-1)
    return values * cosine + turned * sine_part

def attend_group(query_rows, key_rows, value_rows, ordering, lengths):
    segment, position = sequence_meta(ordering, lengths)
    cosine, sine_part = rope_tables(position, HEAD_DIM)
    allowed = (segment[:, None] == segment[None, :]) & (ordering[None, :] <= ordering[:, None])
    score_scale = HEAD_DIM ** (-0.5)

    def one_head(operands):
        query_head, key_head, value_head = operands
        query_rot = low(rotate(query_head, cosine, sine_part))
        key_rot = low(rotate(key_head, cosine, sine_part))
        scores = low_back(jnp.dot(query_rot, key_rot.T, precision=HIGHEST, preferred_element_type=jnp.float32) * score_scale)
        scores = jnp.where(allowed, scores, NEGATIVE)
        highest_score = lax.optimization_barrier(jnp.max(scores, axis=-1, keepdims=True))
        raised = jnp.exp(scores - highest_score)
        weights = raised / lax.optimization_barrier(jnp.sum(raised, axis=-1, keepdims=True))
        return jnp.dot(low(weights), value_head, precision=HIGHEST, preferred_element_type=jnp.float32)
    stacked = lax.map(jax.checkpoint(one_head), (query_rows.transpose(1, 0, 2), key_rows.transpose(1, 0, 2), value_rows.transpose(1, 0, 2)))
    return stacked.transpose(1, 0, 2)

def attend_all(query_rows, key_rows, value_rows, packed_at, lengths):

    def one_group(operands):
        return attend_group(operands[0], operands[1], operands[2], operands[3], operands[4])
    shaped = tuple((values.reshape(N_REP, GROUP_TOK, HEADS, HEAD_DIM) for values in (query_rows, key_rows, value_rows)))
    attended = lax.map(one_group, shaped + (packed_at, lengths))
    return attended.reshape(N_REP * GROUP_TOK, HEADS * HEAD_DIM)

def forward(stream_values, query_weight, key_weight, value_weight, output_weight, gate_weight, up_weight, down_weight, mixing_weight, mixing_static, packed_at, lengths):
    normed, carried, beta_first = mixing(stream_values, mixing_weight[0], mixing_static[0])
    attention_in = low(normed)
    query_rows = low_back(low(jnp.dot(attention_in, query_weight, precision=HIGHEST)))
    key_rows = low_back(low(jnp.dot(attention_in, key_weight, precision=HIGHEST)))
    value_rows = low_back(low(jnp.dot(attention_in, value_weight, precision=HIGHEST)))
    attended = attend_all(query_rows, key_rows, value_rows, packed_at, lengths)
    attended = low_back(low(attended))
    branch = low_back(jnp.dot(attended, output_weight, precision=HIGHEST))
    middle = carried + beta_first[:, :, None] * branch[:, None, :]
    normed_second, carried_second, beta_second = mixing(middle, mixing_weight[1], mixing_static[1])
    ffn_in = low(normed_second)
    gate_pre = low_back(jnp.dot(ffn_in, gate_weight, precision=HIGHEST))
    up_pre = low_back(jnp.dot(ffn_in, up_weight, precision=HIGHEST))
    activated = low(gate_pre * jax.nn.sigmoid(gate_pre) * up_pre)
    ffn_out = low_back(jnp.dot(activated, down_weight, precision=HIGHEST))
    return carried_second + beta_second[:, :, None] * ffn_out[:, None, :]

def reference(streams, cotangent, lengths, packed_at, query_weight, key_weight, value_weight, output_weight, gate_weight, up_weight, down_weight, mixing_weight, mixing_static):
    floats = tuple((array.astype(jnp.float32) for array in (streams, query_weight, key_weight, value_weight, output_weight, gate_weight, up_weight, down_weight, mixing_weight, mixing_static)))

    def run_block(*operands):
        return forward(*operands, packed_at, lengths)
    result, pull_back = jax.vjp(run_block, *floats)
    gradients = pull_back(cotangent.astype(jnp.float32))
    return (result.astype(jnp.bfloat16), gradients[0], gradients[1], gradients[2], gradients[3], gradients[4], gradients[5], gradients[6], gradients[7], gradients[8], gradients[9])
```

```python
import functools
import math

import jax
import jax.numpy as jnp
from jax import lax
from jax.experimental import pallas as pl
from jax.experimental.pallas import tpu as pltpu
from jax.sharding import PartitionSpec as P

HEADS = 16
EPSILON = 1e-05
NEGATIVE = -1e30
LANES = 128
LOG2E = 1.4426950408889634
F32 = jnp.float32
BF16 = jnp.bfloat16
NO_COST = pl.CostEstimate(flops=0, bytes_accessed=0, transcendentals=0)
NN = (((1,), (0,)), ((), ()))
NT = (((1,), (1,)), ((), ()))
TN = (((0,), (0,)), ((), ()))


def dot(a, b, dims=NN):
    return lax.dot_general(a, b, dims, preferred_element_type=F32)


def params(mib):
    return pltpu.CompilerParams(vmem_limit_bytes=mib << 20)


def after(value, *events):
    return lax.optimization_barrier((value, *events))[0] if events else value


def assemble_kernel(line, x_ref, *refs):
    rights, lefts, out_ref = refs[: line - 1], refs[line - 1 : -1], refs[-1]
    out_ref[0] = x_ref[...]
    for k in range(1, line):
        out_ref[k] = lefts[k - 1][...] + rights[line - k - 1][...]


class Task:
    def __init__(self, steps):
        self.steps, self.value, self.over, self.arrived = steps, None, False, []
        self.advance(None)

    def advance(self, arrived):
        self.arrived += arrived or []
        try:
            self.sends = list(self.steps.send(arrived))
            self.left = list(range(len(self.sends)))
            self.got = [None] * len(self.sends)
        except StopIteration as stop:
            self.value, self.over, self.left = stop.value, True, []


class Rounds:
    def __init__(self):
        self.base, self.fence, self.last = (), (), ()

    def hold(self, *values):
        self.fence += values

    def tie(self, value):
        return after(value, *self.fence)

    def run(self, *jobs):
        self.base, self.fence = self.fence, ()
        self.last = self.base
        self.send(jobs, self.base)

    def also(self, *jobs):
        self.last = self.send(jobs, self.base)

    def then(self, *jobs):
        self.last = self.send(jobs, self.last)

    def send(self, jobs, events):
        sends = []
        for job in jobs:
            task, pairs = job if isinstance(job, tuple) else (job, len(job.left))
            sends += [(task, i) for i in task.left[: 2 * pairs]]
        out = tuple(t.sends[i][0](after(t.sends[i][1], *events)) for t, i in sends)
        self.fence += out
        for (t, i), v in zip(sends, out):
            t.got[i] = v
            t.left.remove(i)
        for t in {id(t): t for t, _ in sends}.values():
            if not t.left:
                t.advance(t.got)
        return out

    def finish(self, *tasks):
        while any(not t.over for t in tasks):
            self.run(*tasks)


def sender(axis, pairs):
    return lambda x: lax.ppermute(x, axis, pairs)


def assemble_kernel(line, x_ref, *refs):
    rights, lefts, out_ref = refs[: line - 1], refs[line - 1 : -1], refs[-1]
    out_ref[0] = x_ref[...]
    for k in range(1, line):
        out_ref[k] = lefts[k - 1][...] + rights[line - k - 1][...]


def line_gather(x):
    line = lax.axis_size("shard") // 2
    right = left = x
    rights, lefts = [], []
    for step in range(line - 1):
        right, left = yield [
            (sender("shard", [(2 * p + c, 2 * p + 2 + c) for p in range(step, line - 1) for c in range(2)]), right),
            (sender("shard", [(2 * p + c, 2 * p - 2 + c) for p in range(1, line - step) for c in range(2)]), left),
        ]
        rights.append(right)
        lefts.append(left)
    rows, width = x.shape
    (mine,) = token_call(
        functools.partial(assemble_kernel, line), rows, [x, *rights, *lefts],
        [jax.ShapeDtypeStruct((line, rows, width), x.dtype)],
    )
    return mine.reshape(line * rows, width)


def other_core(x):
    size = lax.axis_size("shard")
    (other,) = yield [(sender("shard", [(i, i ^ 1) for i in range(size)]), x)]
    return other


def line_shift(k):
    line = lax.axis_size("shard") // 2
    return sender("shard", [(2 * p + c, 2 * ((p + k) % line) + c) for p in range(line) for c in range(2)])


def stack_kernel(*refs):
    for k, ref in enumerate(refs[:-1]):
        refs[-1][k] = ref[...]


def shifts(line, steps):
    return [list(range(1, line))] if steps == 1 else [list(range(1, line, 2)), list(range(2, line, 2))]


def direct_gather(x, steps=1):
    line = lax.axis_size("shard") // 2
    came = {}
    for step in shifts(line, steps):
        came |= dict(zip(step, (yield [(line_shift(k), x) for k in step])))
    rows, width = x.shape
    (mine,) = token_call(
        stack_kernel, rows, [x] + [came[line - q] for q in range(1, line)],
        [jax.ShapeDtypeStruct((line, rows, width), x.dtype)],
    )
    return mine.reshape(line * rows, width)


def direct_scatter(rows, steps=1):
    line = lax.axis_size("shard") // 2
    parts = list(rows.reshape(line, rows.shape[0] // line, -1))
    came = [parts[0]]
    for step in shifts(line, steps):
        came += yield [(line_shift(k), parts[k]) for k in step]
    return came


def rep_sender(bit):
    return sender("rep", [(i, i ^ (1 << bit)) for i in range(lax.axis_size("rep"))])


def rep_orders(units):
    bits = list(range(lax.axis_size("rep").bit_length() - 1))
    return [bits] * (units // 2) + [bits[::-1]] * (units - units // 2)


def paired(sends):
    middle = len(sends) // 2
    return [v for pair in zip(sends[:middle], sends[middle:]) for v in pair]


def rep_scatter(units, merge=False):
    orders = rep_orders(len(units))
    units = [dict(enumerate(u)) for u in units]
    for i in range(len(orders[0])):
        bits = [1 << o[i] for o in orders]
        keys = [[m for m in unit if m & bit] for unit, bit in zip(units, bits)]
        came = yield from exchange_blocks(units, keys, [o[i] for o in orders], merge)
        units = [
            {m ^ bit: unit[m ^ bit] + v for m, v in zip(key, new)}
            for unit, bit, key, new in zip(units, bits, keys, came)
        ]
    return [u[0] for u in units]


def rep_gather(units, merge=False):
    orders = [o[::-1] for o in rep_orders(len(units))]
    units = [{0: u} for u in units]
    for i in range(len(orders[0])):
        keys = [list(unit) for unit in units]
        came = yield from exchange_blocks(units, keys, [o[i] for o in orders], merge)
        for unit, o, key, new in zip(units, orders, keys, came):
            unit |= {m ^ (1 << o[i]): v for m, v in zip(key, new)}
    return [[u[m] for m in range(len(u))] for u in units]


def rep_flip(m):
    return sender("rep", [(i, i ^ m) for i in range(lax.axis_size("rep"))])


def rep_scatter_direct(blocks):
    came = yield [(rep_flip(m), blocks[m]) for m in range(1, len(blocks))]
    return sum(v.astype(F32) for v in [blocks[0], *came]).astype(blocks[0].dtype)


def rep_gather_direct(block):
    came = yield [(rep_flip(m), block) for m in range(1, lax.axis_size("rep"))]
    return [block, *came]


def exchange_blocks(units, keys, bits, merge):
    if merge:
        came = yield [
            (rep_sender(bit), jnp.concatenate([unit[m] for m in key]) if len(key) > 1 else unit[key[0]])
            for unit, key, bit in paired(list(zip(units, keys, bits)))
        ]
        order = paired(list(range(len(units))))
        return [cut_units(came[order.index(u)], len(keys[u])) for u in range(len(units))]
    flat = paired([(u, m) for u, key in enumerate(keys) for m in key])
    came = yield [(rep_sender(bits[u]), units[u][m]) for u, m in flat]
    came = dict(zip(flat, came))
    return [[came[u, m] for m in key] for u, key in enumerate(keys)]


def shard_exchange(x, counts=()):
    shards = lax.axis_size("shard")
    me = lax.axis_index("shard")
    take = lambda k: lax.dynamic_index_in_dim(x, me ^ k, 0, keepdims=False)
    out, counts = [take(0)], list(counts)
    while len(out) < shards:
        step = range(len(out), min(shards, len(out) + (counts.pop(0) if counts else shards)))
        out += yield [(sender("shard", [(i, i ^ k) for i in range(shards)]), take(k)) for k in step]
    return out


def chip_exchange(x, counts=(), out=None):
    shards = lax.axis_size("shard")
    me = lax.axis_index("shard")
    pick = lambda k: lax.dynamic_index_in_dim(x, me ^ k, 0, keepdims=False)
    (came,) = yield [
        (sender("shard", [(i, i ^ 1) for i in range(shards)]), jnp.stack([pick(k) for k in range(1, shards, 2)]))
    ]
    held = [jnp.stack([pick(2 * q), came[q]]) for q in range(shards // 2)]
    out, counts = [] if out is None else out, list(counts)
    out += [held[0][0], held[0][1]]
    while len(out) < shards:
        q = len(out) // 2
        step = range(q, min(shards // 2, q + (counts.pop(0) if counts else shards)))
        came = yield [(sender("shard", [(i, i ^ (2 * q)) for i in range(shards)]), held[q]) for q in step]
        out += [v[f] for v in came for f in range(2)]
    return out


def stack_units(blocks, count):
    size = len(blocks) // count
    return [jnp.stack(blocks[i * size : (i + 1) * size]) for i in range(count)]


def to_tokens(x):
    shards = lax.axis_size("shard")
    line = shards // 2
    (came,) = yield [(sender("shard", [(i, i ^ 1) for i in range(shards)]), x[1])]
    held = jnp.stack([x[0], came], axis=1)
    came = yield [
        (sender("shard", [(2 * p + c, 2 * ((p + k) % line) + c) for p in range(line) for c in range(2)]), held[k])
        for k in range(1, line)
    ]
    came = [held[0], *came]
    return [jnp.concatenate([came[(line - q) % line][f] for q in range(line)], axis=1) for f in range(2)]


def cut_units(x, count):
    size = x.shape[0] // count
    return [x[i * size : (i + 1) * size] for i in range(count)]


def recut_piece(weights):
    shards, reps = lax.axis_size("shard"), lax.axis_size("rep")
    part = weights[0].shape[0] // reps
    start = lax.axis_index("rep") * part
    pieces = [
        lax.dynamic_slice_in_dim(w, start, part, 0).reshape(part, shards, -1).transpose(1, 0, 2) for w in weights
    ]
    return jnp.concatenate(pieces, axis=2)


def halves(x):
    return cut_units(x, 2)


def unit_specs(units):
    size = units[0][0].shape[0]
    return [
        pl.BlockSpec((1,) + v.shape[1:], lambda k, me, g=g: (jnp.clip(k - g * size, 0, size - 1), 0, 0))
        for g, u in enumerate(units) for v in u
    ]


def columns_kernel(units, reps, parts, me_ref, *refs):
    outs = refs[-parts:]
    size = pl.num_programs(0) // units
    part = refs[0].shape[1]
    for g in range(units):
        @pl.when(pl.program_id(0) // size == g)
        def _(chosen=refs[g * reps : (g + 1) * reps]):
            for m in range(reps):
                row = pl.multiple_of((me_ref[0] ^ m) * part, part)
                for i, out_ref in enumerate(outs):
                    width = out_ref.shape[1]
                    out_ref[pl.ds(row, part), :] = chosen[m][0, :, i * width : (i + 1) * width].astype(out_ref.dtype)


def join(units, parts, spec, shapes, filled=(), mib=32):
    reps = lax.axis_size("rep")
    operands = [v for u in units for v in u]
    return pl.pallas_call(
        functools.partial(columns_kernel, len(units), reps, parts),
        grid_spec=pltpu.PrefetchScalarGridSpec(
            num_scalar_prefetch=1,
            grid=(len(units) * units[0][0].shape[0],),
            in_specs=unit_specs(units) + [pl.BlockSpec(memory_space=pl.ANY)] * len(filled),
            out_specs=[spec] * parts,
        ),
        out_shape=shapes,
        input_output_aliases={1 + len(operands) + i: i for i in range(len(filled))},
        compiler_params=params(mib),
        cost_estimate=NO_COST,
    )(jnp.stack([lax.axis_index("rep"), lax.axis_index("shard")]).astype(jnp.int32), *operands, *filled)


def recut_join(units, first=0, filled=()):
    shards, reps = lax.axis_size("shard"), lax.axis_size("rep")
    _, part, columns = units[0][0].shape
    rows = part * reps
    return join(
        units, 1, pl.BlockSpec((rows, columns), lambda k, me: ((k + first) ^ me[1], 0)),
        [jax.ShapeDtypeStruct((shards * rows, columns), BF16)], filled,
    )[0]


def rows_in_order(units):
    blocks, part, columns = units[0][0].shape
    rows = part * lax.axis_size("rep")
    return join(
        units, 1, pl.BlockSpec((rows, columns), lambda k, me: (k, 0)),
        [jax.ShapeDtypeStruct((len(units) * blocks * rows, columns), BF16)],
    )[0]


def columns_join(units, parts):
    shards, reps = lax.axis_size("shard"), lax.axis_size("rep")
    _, part, columns = units[0][0].shape
    rows, width = part * reps, columns // parts
    return join(
        units, parts, pl.BlockSpec((rows, width), lambda k, me: (0, k ^ me[1])),
        [jax.ShapeDtypeStruct((rows, shards * width), F32)] * parts, mib=56 if parts == 2 else 32,
    )


def rows_kernel(units, reps, me_ref, *refs):
    out_ref = refs[-1]
    part = refs[0].shape[0]
    for u in range(units):
        for m in range(reps):
            row = pl.multiple_of((me_ref[0] ^ m) * (units * part) + u * part, part)
            out_ref[pl.ds(row, part), :] = refs[u * reps + m][...].astype(F32)


def rows_join(units):
    reps = lax.axis_size("rep")
    operands = [v for u in units for v in u]
    part, columns = operands[0].shape
    block = 512 if columns % 512 == 0 else columns
    return pl.pallas_call(
        functools.partial(rows_kernel, len(units), reps),
        grid_spec=pltpu.PrefetchScalarGridSpec(
            num_scalar_prefetch=1,
            grid=(columns // block,),
            in_specs=[pl.BlockSpec((part, block), lambda j, me: (0, j))] * len(operands),
            out_specs=pl.BlockSpec((part * len(operands), block), lambda j, me: (0, j)),
        ),
        out_shape=jax.ShapeDtypeStruct((part * len(operands), columns), F32),
        compiler_params=params(32),
        cost_estimate=NO_COST,
    )(lax.axis_index("rep").astype(jnp.int32)[None], *operands)


def mixing_kernel(me_ref, *refs):
    out_ref = refs[-1]
    out_ref[...] = jnp.zeros_like(out_ref)
    width = refs[0].shape[2]
    for k, ref in enumerate(refs[:-1]):
        start = pl.multiple_of((me_ref[0] ^ k) * width, width)
        out_ref[:, : ref.shape[1], pl.ds(start, width)] = ref[...]


def mixing_gather(weight):
    shards = lax.axis_size("shard")
    piece = jnp.pad(jnp.swapaxes(weight, 1, 2), ((0, 0), (0, 2), (0, 0)))
    piece = jnp.concatenate([piece, piece], axis=1)
    (came,) = yield [(sender("shard", [(i, i ^ 1) for i in range(shards)]), piece)]
    held = jnp.stack([piece, came])
    came = yield [
        (sender("shard", [(i, i ^ (2 * q)) for i in range(shards)]), held) for q in range(1, shards // 2)
    ]
    came = [v[f] for v in [held, *came] for f in range(2)]
    return pl.pallas_call(
        mixing_kernel,
        grid_spec=pltpu.PrefetchScalarGridSpec(
            num_scalar_prefetch=1,
            grid=(1,),
            in_specs=[pl.BlockSpec(piece.shape, lambda i, me: (0, 0, 0))] * shards,
            out_specs=pl.BlockSpec((2, LANES, shards * piece.shape[2]), lambda i, me: (0, 0, 0)),
        ),
        out_shape=jax.ShapeDtypeStruct((2, LANES, shards * piece.shape[2]), BF16),
        compiler_params=params(32),
    )(lax.axis_index("shard").astype(jnp.int32)[None], *came)


def sum_small(blocks):
    shards, reps = lax.axis_size("shard"), lax.axis_size("rep")
    me = lax.axis_index("shard")
    blocks = blocks.reshape((shards // 2, 2) + blocks.shape[1:])
    pick = lambda f: lax.dynamic_index_in_dim(blocks, (me % 2) ^ f, 1, keepdims=False)
    (came,) = yield [(sender("shard", [(i, i ^ 1) for i in range(shards)]), pick(1))]
    pair = pick(0) + came
    take = lambda q: lax.dynamic_index_in_dim(pair, (me // 2) ^ q, 0, keepdims=False)
    total = take(0)
    came = yield [
        (sender("shard", [(i, i ^ (2 * q)) for i in range(shards)]), take(q)) for q in range(1, shards // 2)
    ]
    for v in came:
        total = total + v
    came = yield [(sender("rep", [(i, i ^ k) for i in range(reps)]), total) for k in range(1, reps)]
    stacked = jnp.stack([total, *came])
    me = lax.axis_index("rep")
    return sum(lax.dynamic_index_in_dim(stacked, me ^ k, 0, keepdims=False) for k in range(reps))


def lane(shape):
    return lax.broadcasted_iota(jnp.int32, shape, len(shape) - 1)


def column(values, index):
    return values[:, index : index + 1]


def split(values):
    high = values.astype(BF16)
    return high, (values - high.astype(F32)).astype(BF16)


def moments(values):
    mean = jnp.mean(values, axis=-1, keepdims=True)
    centred = values - mean
    spread = jnp.mean(centred * centred, axis=-1, keepdims=True)
    return mean, centred, lax.rsqrt(spread + EPSILON)


def mix_forward(streams, weight, static):
    count = len(streams)
    rows = streams[0].shape[0]
    stats = [moments(y) for y in streams]
    parts = [split(centred) for _, centred, _ in stats]
    raw = dot(jnp.concatenate([p[0] for p in parts] + [p[1] for p in parts], axis=0), weight, NT)
    at = lane((rows, LANES))
    pres, coefficients = [], []
    for i in range(count):
        pre = (raw[i * rows : (i + 1) * rows] + raw[(count + i) * rows : (count + i + 1) * rows]) * stats[i][2]
        pres.append(pre)
        coefficients.append(static[i : i + 1] + jnp.tanh(pre))
    entering = sum(column(c, 0) * y for c, y in zip(coefficients, streams))
    mean, centred, scale = moments(entering)
    packed = []
    for i in range(count):
        value = jnp.where(at < 6, pres[i], 0.0)
        value = jnp.where(at == 6, stats[i][0], jnp.where(at == 7, stats[i][2], value))
        packed.append(jnp.where(at == 8, mean, jnp.where(at == 9, scale, value)))
    return centred * scale, coefficients, packed


def mix_carry(streams, coefficients, j):
    return sum(column(c, 1 + j) * y for c, y in zip(coefficients, streams))


def mix_backward(streams, packed, static, grad_entering, grad_carried, grad_beta, weight_rows, weight_mean):
    count = len(streams)
    rows, width = streams[0].shape
    at = lane((rows, LANES))
    tanhs = [jnp.where(at < 6, jnp.tanh(p), 0.0) for p in packed]
    coefficients = [static[i : i + 1] + tanhs[i] for i in range(count)]
    mean, scale = column(packed[0], 8), column(packed[0], 9)
    entering = (sum(column(c, 0) * y for c, y in zip(coefficients, streams)) - mean) * scale
    inner = jnp.mean(grad_entering * entering, axis=-1, keepdims=True)
    outer = jnp.mean(grad_entering, axis=-1, keepdims=True)
    grad_sum = scale * (grad_entering - outer - entering * inner)
    grads, both, normed, scalars = [], [], [], []
    for i in range(count):
        y = streams[i]
        value = jnp.where(at == 0, jnp.sum(grad_sum * y, axis=-1, keepdims=True), 0.0)
        for j in range(count):
            value = jnp.where(at == 1 + j, jnp.sum(grad_carried[j] * y, axis=-1, keepdims=True), value)
        value = jnp.where(at == 1 + count, grad_beta[i], value)
        grad_pre = value * (1.0 - tanhs[i] * tanhs[i])
        high = grad_pre.astype(BF16).astype(F32)
        low = grad_pre - high
        both.append((high + pltpu.roll(low, 8, 1)).astype(BF16))
        grads.append(value)
        normed.append((y - column(packed[i], 6)) * column(packed[i], 7))
        scalars.append((
            jnp.sum(grad_pre * weight_mean, axis=-1, keepdims=True),
            jnp.sum(jnp.where(at < 6, grad_pre * packed[i], 0.0), axis=-1, keepdims=True) / width,
        ))
    both = jnp.concatenate(both, axis=0)
    grad_normed = dot(both, weight_rows)
    mixing_sum = dot(both, jnp.concatenate([n.astype(BF16) for n in normed], axis=0), TN)
    out = []
    for i in range(count):
        value = column(coefficients[i], 0) * grad_sum
        for j in range(count):
            value = value + column(coefficients[i], 1 + j) * grad_carried[j]
        a, b = scalars[i]
        out.append(
            value + column(packed[i], 7) * (grad_normed[i * rows : (i + 1) * rows] - a - normed[i] * b)
        )
    return out, mixing_sum, grads


def load_streams(ref):
    return [ref[i].astype(F32) for i in range(ref.shape[0])]


def coefficients_of(packed, static):
    return [static[i : i + 1] + jnp.tanh(packed[i]) for i in range(len(packed))]


def first_kernel(x_ref, weight_ref, static_ref, entering_ref, packed_ref, turned_ref):
    streams = [x_ref[:, i, :] for i in range(x_ref.shape[1])]
    for i, stream in enumerate(streams):
        turned_ref[i] = stream
    entering, _, packed = mix_forward([v.astype(F32) for v in streams], weight_ref[...], static_ref[...])
    entering_ref[...] = entering.astype(BF16)
    for i, value in enumerate(packed):
        packed_ref[i] = value


def middle_kernel(
    x_ref, packed_ref, static_ref, branch_ref, w_ref, weight_ref, static_next_ref,
    m_ref, entering_ref, down_ref, packed_next_ref,
):
    streams = load_streams(x_ref)
    count = len(streams)
    coefficients = coefficients_of([packed_ref[i] for i in range(count)], static_ref[...])
    branch = branch_ref[...]
    middle = []
    for j in range(count):
        middle.append(mix_carry(streams, coefficients, j) + column(coefficients[j], 5) * branch)
        m_ref[j] = middle[j]
    entering, following, packed = mix_forward(middle, weight_ref[...], static_next_ref[...])
    entering_ref[...] = entering.astype(BF16)
    for i, value in enumerate(packed):
        packed_next_ref[i] = value
    down_ref[...] = sum(column(following[j], 5) * w_ref[j].astype(F32) for j in range(count)).astype(BF16)


def total(refs):
    return sum(ref[...].astype(F32) for ref in refs)


def out_kernel(m_ref, packed_ref, static_ref, *refs):
    out_ref = refs[-1]
    streams = load_streams(m_ref)
    count = len(streams)
    coefficients = coefficients_of([packed_ref[i] for i in range(count)], static_ref[...])
    z = total(refs[:-1])
    for j in range(count):
        out_ref[:, j, :] = (mix_carry(streams, coefficients, j) + column(coefficients[j], 5) * z).astype(BF16)


def accumulate(step, mixing_ref, static_ref, mixing_sum, grads):
    @pl.when(step == 0)
    def _():
        mixing_ref[...] = jnp.zeros_like(mixing_ref)
        static_ref[...] = jnp.zeros_like(static_ref)

    mixing_ref[...] += mixing_sum
    at = lax.broadcasted_iota(jnp.int32, static_ref.shape, 0)
    sums = jnp.zeros(static_ref.shape, F32)
    for i, grad in enumerate(grads):
        sums = jnp.where(at == i, jnp.sum(grad, axis=0, keepdims=True), sums)
    static_ref[...] += sums


def middle_back_kernel(
    terms, m_ref, packed_ref, static_ref, packed_first_ref, static_first_ref, w_ref, branch_ref,
    weight_rows_ref, weight_mean_ref, *refs,
):
    grad_m_ref, grad_branch_ref, grad_beta_ref, mixing_ref, static_sum_ref = refs[2 * terms :]
    streams = load_streams(m_ref)
    count = len(streams)
    cotangent = load_streams(w_ref)
    z = total(refs[:terms])
    grad_entering = total(refs[terms : 2 * terms])
    grad_beta = [jnp.sum(w * z, axis=-1, keepdims=True) for w in cotangent]
    grads, mixing_sum, grad_pres = mix_backward(
        streams, [packed_ref[i] for i in range(count)], static_ref[...], grad_entering, cotangent, grad_beta,
        weight_rows_ref[...], weight_mean_ref[...],
    )
    accumulate(pl.program_id(0), mixing_ref, static_sum_ref, mixing_sum, grad_pres)
    first = coefficients_of([packed_first_ref[i] for i in range(count)], static_first_ref[...])
    branch = branch_ref[...]
    at = lane(grad_beta_ref.shape)
    beta = jnp.zeros(grad_beta_ref.shape, F32)
    for j in range(count):
        grad_m_ref[j] = grads[j]
        beta = jnp.where(at == j, jnp.sum(grads[j] * branch, axis=-1, keepdims=True), beta)
    grad_beta_ref[...] = beta
    grad_branch_ref[...] = sum(column(first[j], 5) * grads[j] for j in range(count)).astype(BF16)


def first_back_kernel(
    x_ref, packed_ref, static_ref, grad_m_ref, grad_beta_ref, weight_rows_ref, weight_mean_ref, *refs
):
    grad_ref, mixing_ref, static_sum_ref = refs[-3:]
    streams = load_streams(x_ref)
    count = len(streams)
    grad_entering = total(refs[:-3])
    beta = grad_beta_ref[...]
    grads, mixing_sum, grad_pres = mix_backward(
        streams, [packed_ref[i] for i in range(count)], static_ref[...], grad_entering,
        [grad_m_ref[i] for i in range(count)], [column(beta, i) for i in range(count)],
        weight_rows_ref[...], weight_mean_ref[...],
    )
    accumulate(pl.program_id(0), mixing_ref, static_sum_ref, mixing_sum, grad_pres)
    for i in range(count):
        grad_ref[:, i, :] = grads[i]


def token_call(kernel, tokens, operands, outputs, flops=0, mib=40):
    block = 32 if tokens % 32 == 0 else tokens

    def spec(shape):
        if tokens not in shape[:-1]:
            return pl.BlockSpec(shape, lambda i, n=len(shape): (0,) * n)
        axis = shape.index(tokens)
        cut = tuple(block if d == axis else s for d, s in enumerate(shape))
        return pl.BlockSpec(cut, lambda i, axis=axis, n=len(shape): tuple(i if d == axis else 0 for d in range(n)))

    size = sum(math.prod(o.shape) * o.dtype.itemsize for o in list(operands) + list(outputs))
    return pl.pallas_call(
        kernel,
        grid=(tokens // block,),
        in_specs=[spec(o.shape) for o in operands],
        out_specs=[spec(o.shape) for o in outputs],
        out_shape=list(outputs),
        compiler_params=params(mib),
        cost_estimate=NO_COST,
    )(*operands)


def rows_of(operand):
    return operand[0].shape[0] // 2 if isinstance(operand, tuple) else operand.shape[0]


def whole_of(operand):
    return operand[0] if isinstance(operand, tuple) else operand


def half_of(operand):
    return operand[1] if isinstance(operand, tuple) else 0


def tile_of(size):
    return next((t for t in (512, 384, 256, 128) if size % t == 0), size)


def product_kernel(dims, added, a_ref, b_ref, *refs):
    out = dot(a_ref[...], b_ref[...], dims)
    if added:
        out = out + refs[0][...].astype(F32)
    refs[-1][...] = out.astype(refs[-1].dtype)


def product(a, b, dims=NN, add=None, into=None, filled=()):
    rows, depth = rows_of(a), whole_of(a).shape[1]
    half, columns = half_of(a), b.shape[0] if dims == NT else b.shape[1]
    tile = tile_of(columns)
    operands = [whole_of(a), b] + ([] if add is None else [add]) + list(filled)
    specs = [
        pl.BlockSpec((rows, depth), lambda j: (half, 0)),
        pl.BlockSpec((tile, depth), lambda j: (j, 0)) if dims == NT else pl.BlockSpec((depth, tile), lambda j: (0, j)),
    ]
    if add is not None:
        specs.append(pl.BlockSpec((rows, tile), lambda j: (0, j)))
    specs += [pl.BlockSpec(memory_space=pl.ANY)] * len(filled)
    at = into or 0
    return pl.pallas_call(
        functools.partial(product_kernel, dims, add is not None),
        grid=(columns // tile,),
        in_specs=specs,
        out_specs=pl.BlockSpec((rows, tile), lambda j: (at, j)),
        out_shape=jax.ShapeDtypeStruct((rows if into is None else 2 * rows, columns), BF16),
        input_output_aliases={len(operands) - 1: 0} if filled else {},
        compiler_params=params(40),
        cost_estimate=NO_COST,
    )(*operands)


def columns_product_kernel(units, reps, me_ref, x0, x1, y0, y1, *refs):
    outs, sums = refs[:-1], refs[-1]
    sums[...] = dot(x0[...], y0[...], TN) + dot(x1[...], y1[...], TN)
    step = pl.program_id(0)
    size = pl.num_programs(0) // units
    part = sums.shape[0] // reps
    for u in range(units):
        @pl.when(step // size == u)
        def _(u=u):
            for m in range(reps):
                row = pl.multiple_of((me_ref[0] ^ m) * part, part)
                outs[u * reps + m][0] = sums[pl.ds(row, part), :].astype(BF16)


def columns_product(xs, ys, units):
    shards, reps = lax.axis_size("shard"), lax.axis_size("rep")
    tokens, columns = rows_of(ys[0]), whole_of(ys[0]).shape[1]
    rows = whole_of(xs[0]).shape[1] // shards
    size, part = shards // units, rows // reps
    x_specs = [pl.BlockSpec((tokens, rows), lambda s, me, h=half_of(x): (h, s)) for x in xs]
    y_specs = [pl.BlockSpec((tokens, columns), lambda s, me, h=half_of(y): (h, 0)) for y in ys]
    out = pl.pallas_call(
        functools.partial(columns_product_kernel, units, reps),
        grid_spec=pltpu.PrefetchScalarGridSpec(
            num_scalar_prefetch=1,
            grid=(shards,),
            in_specs=x_specs + y_specs,
            out_specs=[
                pl.BlockSpec((1, part, columns), lambda s, me, u=u: (jnp.clip(s - u * size, 0, size - 1), 0, 0))
                for u in range(units) for _ in range(reps)
            ],
            scratch_shapes=[pltpu.VMEM((rows, columns), F32)],
        ),
        out_shape=[jax.ShapeDtypeStruct((size, part, columns), BF16)] * (units * reps),
        compiler_params=params(48),
        cost_estimate=NO_COST,
    )(lax.axis_index("rep").astype(jnp.int32)[None], *[whole_of(v) for v in [*xs, *ys]])
    return [out[u * reps : (u + 1) * reps] for u in range(units)]


def rows_product_kernel(units, reps, me_ref, x0, x1, y0, y1, *refs):
    outs, sums = refs[:-1], refs[-1]
    sums[...] = dot(x0[...], y0[...], TN) + dot(x1[...], y1[...], TN)
    part = outs[0].shape[0]
    for u in range(units):
        for m in range(reps):
            row = pl.multiple_of((me_ref[0] ^ m) * (units * part) + u * part, part)
            outs[u * reps + m][...] = sums[pl.ds(row, part), :].astype(BF16)


def rows_product(xs, ys, units):
    reps = lax.axis_size("rep")
    tokens, columns = rows_of(ys[0]), whole_of(ys[0]).shape[1]
    rows = whole_of(xs[0]).shape[1]
    part, tile = rows // (units * reps), tile_of(columns)
    x_specs = [pl.BlockSpec((tokens, rows), lambda j, me, h=half_of(x): (h, 0)) for x in xs]
    y_specs = [pl.BlockSpec((tokens, tile), lambda j, me, h=half_of(y): (h, j)) for y in ys]
    out = pl.pallas_call(
        functools.partial(rows_product_kernel, units, reps),
        grid_spec=pltpu.PrefetchScalarGridSpec(
            num_scalar_prefetch=1,
            grid=(columns // tile,),
            in_specs=x_specs + y_specs,
            out_specs=[pl.BlockSpec((part, tile), lambda j, me: (0, j))] * (units * reps),
            scratch_shapes=[pltpu.VMEM((rows, tile), F32)],
        ),
        out_shape=[jax.ShapeDtypeStruct((part, columns), BF16)] * (units * reps),
        compiler_params=params(48),
        cost_estimate=NO_COST,
    )(lax.axis_index("rep").astype(jnp.int32)[None], *[whole_of(v) for v in [*xs, *ys]])
    return [out[u * reps : (u + 1) * reps] for u in range(units)]


def ffn_tile(hidden):
    return 256 if hidden % 256 == 0 else hidden


def chunks(rows):
    step = 320 if rows % 320 == 0 else rows
    return [slice(i, i + step) for i in range(0, rows, step)]


def ffn_kernel(x_ref, gate_ref, up_ref, *refs):
    active_ref, by_gate_ref, by_up_ref = refs[-3:]
    for cut in chunks(x_ref.shape[0]):
        gate = dot(x_ref[cut, :], gate_ref[...])
        up = dot(x_ref[cut, :], up_ref[...])
        sigmoid = 1.0 / (1.0 + jnp.exp2(gate * -LOG2E))
        swish = gate * sigmoid
        active_ref[cut, :] = (swish * up).astype(BF16)
        by_gate_ref[cut, :] = (up * sigmoid * (1.0 + gate - swish)).astype(BF16)
        by_up_ref[cut, :] = swish.astype(BF16)


def ffn_forward(x, weight, half, filled=()):
    rows, width = x.shape
    hidden = weight.shape[1] // 2
    tile = ffn_tile(hidden)
    tiles = hidden // tile
    return pl.pallas_call(
        ffn_kernel,
        grid=(tiles,),
        in_specs=[
            pl.BlockSpec((rows, width), lambda j: (0, 0)),
            pl.BlockSpec((width, tile), lambda j: (0, j)),
            pl.BlockSpec((width, tile), lambda j: (0, j + tiles)),
        ] + [pl.BlockSpec(memory_space=pl.ANY)] * len(filled),
        out_specs=[pl.BlockSpec((rows, tile), lambda j: (half, j))] * 3,
        out_shape=[jax.ShapeDtypeStruct((2 * rows, hidden), BF16)] * 3,
        input_output_aliases={3 + i: i for i in range(len(filled))},
        compiler_params=params(40),
        cost_estimate=NO_COST,
    )(x, weight, weight, *filled)


def ffn_back_kernel(tiles, x_ref, down_ref, by_gate_ref, by_up_ref, *refs):
    out_ref = refs[-1]
    step = pl.program_id(0)
    tile = down_ref.shape[0]
    for cut in chunks(x_ref.shape[0]):
        grad = dot(x_ref[cut, :], down_ref[...], NT)
        first = pl.multiple_of(step * tile, tile)
        second = pl.multiple_of((step + tiles) * tile, tile)
        out_ref[cut, pl.ds(first, tile)] = (grad * by_gate_ref[cut, :].astype(F32)).astype(BF16)
        out_ref[cut, pl.ds(second, tile)] = (grad * by_up_ref[cut, :].astype(F32)).astype(BF16)


def ffn_backward(x, down, by_gate, by_up, half, filled=()):
    rows, width = x.shape
    hidden = down.shape[0]
    tile = ffn_tile(hidden)
    tiles = hidden // tile
    return pl.pallas_call(
        functools.partial(ffn_back_kernel, tiles),
        grid=(tiles,),
        in_specs=[
            pl.BlockSpec((rows, width), lambda j: (0, 0)),
            pl.BlockSpec((tile, width), lambda j: (j, 0)),
            pl.BlockSpec((rows, tile), lambda j: (half, j)),
            pl.BlockSpec((rows, tile), lambda j: (half, j)),
        ] + [pl.BlockSpec(memory_space=pl.ANY)] * len(filled),
        out_specs=pl.BlockSpec((rows, 2 * hidden), lambda j: (half, 0)),
        out_shape=jax.ShapeDtypeStruct((2 * rows, 2 * hidden), BF16),
        input_output_aliases={4 + i: i for i in range(len(filled))},
        compiler_params=params(40),
        cost_estimate=NO_COST,
    )(x, down, by_gate, by_up, *filled)


def turn(values):
    return pltpu.roll(values, values.shape[-1] // 2, 1)


def allowed(place_ref, query_place, query_start):
    keys = place_ref[...]
    return (keys <= query_place) & (keys >= query_start)


def attend_kernel(
    heads, width, q_ref, k_ref, v_ref, cos_q, sin_q, cos_k, sin_k, key_place, query_place, query_start,
    out_ref, rot_q_ref, rot_k_ref, log_ref, value_t,
):
    scale = width ** (-0.5)

    @pl.when(pl.program_id(0) == 0)
    def _():
        for h in range(heads):
            cut = slice(h * width, (h + 1) * width)
            key = k_ref[:, cut].astype(F32)
            rot_k_ref[:, cut] = (key * cos_k[...] + turn(key) * sin_k[...]).astype(BF16)
            value_t[cut, :] = v_ref[:, cut].T

    mask = allowed(key_place, query_place[...], query_start[...])
    for h in range(heads):
        cut = slice(h * width, (h + 1) * width)
        query = q_ref[:, cut].astype(F32)
        query = (query * cos_q[...] + turn(query) * sin_q[...]).astype(BF16)
        rot_q_ref[:, cut] = query
        scores = jnp.where(mask, dot(rot_k_ref[:, cut], query, NT), NEGATIVE)
        top = jnp.max(scores, axis=0, keepdims=True)
        weights = jnp.exp2((scores - top) * (scale * LOG2E))
        total = jnp.sum(weights, axis=0, keepdims=True)
        weights = (weights * (1.0 / total)).astype(BF16)
        out_ref[:, cut] = dot(value_t[cut, :], weights).T.astype(BF16)
        log_ref[h : h + 1] = top * (scale * LOG2E) + jnp.log2(total)


def attend_back_kernel(
    heads, width, q_ref, k_ref, v_ref, grad_ref, log_ref, cos_q, sin_q, cos_k, sin_k, key_place, query_place,
    query_start, out_ref, key_t, sum_k, sum_v,
):
    scale = width ** (-0.5)
    step = pl.program_id(0)
    block = q_ref.shape[0]
    here = pl.ds(pl.multiple_of(step * block, block), block)

    @pl.when(step == 0)
    def _():
        for h in range(heads):
            cut = slice(h * width, (h + 1) * width)
            key_t[cut, :] = k_ref[:, cut].T
        sum_k[...] = jnp.zeros_like(sum_k)
        sum_v[...] = jnp.zeros_like(sum_v)

    mask = allowed(key_place, query_place[...], query_start[...])
    for h in range(heads):
        cut = slice(h * width, (h + 1) * width)
        query = q_ref[:, cut]
        grad = grad_ref[:, cut]
        scores = dot(k_ref[:, cut], query, NT) * (scale * LOG2E) - log_ref[h : h + 1]
        weights = jnp.exp2(jnp.where(mask, scores, NEGATIVE))
        grad_weights = dot(v_ref[:, cut], grad, NT)
        centre = jnp.sum(weights * grad_weights, axis=0, keepdims=True)
        grad_scores = (weights * (grad_weights - centre)).astype(BF16)
        grad_query = (dot(key_t[cut, :], grad_scores) * scale).T
        out_ref[here, cut] = (grad_query * cos_q[...] - turn(grad_query) * sin_q[...]).astype(BF16)
        sum_k[:, cut] += dot(grad_scores, query)
        sum_v[:, cut] += dot(weights.astype(BF16), grad)

    @pl.when(step == pl.num_programs(0) - 1)
    def _():
        for h in range(heads):
            cut = slice(h * width, (h + 1) * width)
            key = sum_k[:, cut] * scale
            second = slice((heads + h) * width, (heads + h + 1) * width)
            third = slice((2 * heads + h) * width, (2 * heads + h + 1) * width)
            out_ref[:, second] = (key * cos_k[...] - turn(key) * sin_k[...]).astype(BF16)
            out_ref[:, third] = sum_v[:, cut].astype(BF16)


def attention(qkv, cosine, sine, place, start, heads):
    tokens, width = qkv.shape[0], qkv.shape[1] // 3
    head_width = width // heads
    block = 256 if tokens % 256 == 0 else tokens
    row = lambda i: (i, 0)
    whole = lambda i: (0, 0)
    along = lambda i: (0, i)
    key_place = jnp.broadcast_to(place[:, None], (tokens, block))
    blocks = tokens // block
    return pl.pallas_call(
        functools.partial(attend_kernel, heads, head_width),
        grid=(blocks,),
        in_specs=[
            pl.BlockSpec((block, width), row),
            pl.BlockSpec((tokens, width), lambda i: (0, 1)),
            pl.BlockSpec((tokens, width), lambda i: (0, 2)),
            pl.BlockSpec((block, head_width), row),
            pl.BlockSpec((block, head_width), row),
            pl.BlockSpec((tokens, head_width), whole),
            pl.BlockSpec((tokens, head_width), whole),
            pl.BlockSpec((tokens, block), whole),
            pl.BlockSpec((1, block), along),
            pl.BlockSpec((1, block), along),
        ],
        out_specs=[
            pl.BlockSpec((block, width), row),
            pl.BlockSpec((block, width), row),
            pl.BlockSpec((tokens, width), whole),
            pl.BlockSpec((heads, block), along),
        ],
        out_shape=[
            jax.ShapeDtypeStruct((tokens, width), BF16),
            jax.ShapeDtypeStruct((tokens, width), BF16),
            jax.ShapeDtypeStruct((tokens, width), BF16),
            jax.ShapeDtypeStruct((heads, tokens), F32),
        ],
        scratch_shapes=[pltpu.VMEM((width, tokens), BF16)],
        compiler_params=params(48),
        cost_estimate=NO_COST,
    )(qkv, qkv, qkv, cosine, sine, cosine, sine, key_place, place[None], start[None])


def attention_back(qkv, rot_q, rot_k, grad, logs, cosine, sine, place, start, heads):
    tokens, width = rot_q.shape
    head_width = width // heads
    block = 256 if tokens % 256 == 0 else tokens
    row = lambda i: (i, 0)
    whole = lambda i: (0, 0)
    along = lambda i: (0, i)
    key_place = jnp.broadcast_to(place[:, None], (tokens, block))
    return pl.pallas_call(
        functools.partial(attend_back_kernel, heads, head_width),
        grid=(tokens // block,),
        in_specs=[
            pl.BlockSpec((block, width), row),
            pl.BlockSpec((tokens, width), whole),
            pl.BlockSpec((tokens, width), lambda i: (0, 2)),
            pl.BlockSpec((block, width), row),
            pl.BlockSpec((heads, block), along),
            pl.BlockSpec((block, head_width), row),
            pl.BlockSpec((block, head_width), row),
            pl.BlockSpec((tokens, head_width), whole),
            pl.BlockSpec((tokens, head_width), whole),
            pl.BlockSpec((tokens, block), whole),
            pl.BlockSpec((1, block), along),
            pl.BlockSpec((1, block), along),
        ],
        out_specs=pl.BlockSpec((tokens, 3 * width), whole),
        out_shape=jax.ShapeDtypeStruct((tokens, 3 * width), BF16),
        scratch_shapes=[
            pltpu.VMEM((width, tokens), BF16),
            pltpu.VMEM((tokens, width), F32),
            pltpu.VMEM((tokens, width), F32),
        ],
        compiler_params=params(56),
        cost_estimate=NO_COST,
    )(rot_q, rot_k, qkv, grad, logs, cosine, sine, cosine, sine, key_place, place[None], start[None])


def sequence_places(ordering, lengths):
    ending = jnp.cumsum(lengths)
    segment = jnp.sum((ordering[:, None] >= ending[None, :]).astype(jnp.int32), axis=1)
    opening = ending - lengths
    chosen = segment[:, None] == jnp.arange(lengths.shape[0], dtype=jnp.int32)[None, :]
    return jnp.sum(jnp.where(chosen, opening[None, :], 0), axis=1)


def rope_tables(position, head_width):
    middle = head_width // 2
    frequency = jnp.exp(
        jnp.arange(middle, dtype=F32) * (-2.0 * math.log(10000.0) / head_width)
    )
    angles = position.astype(F32)[:, None] * frequency[None, :]
    sine = jnp.sin(angles)
    cosine = jnp.cos(angles)
    return jnp.concatenate([cosine, cosine], axis=1), jnp.concatenate([-sine, sine], axis=1)


def per_device(
    streams, cotangent, lengths, packed_at, query_weight, key_weight, value_weight, output_weight,
    gate_weight, up_weight, down_weight, mixing_weight, mixing_static,
):
    shards = lax.axis_size("shard")
    line = shards // 2
    me = lax.axis_index("shard")
    spot, core = me // 2, me % 2
    tokens, count, width = streams.shape
    head_width = width // HEADS
    heads = HEADS // shards
    local = heads * head_width
    shape = jax.ShapeDtypeStruct

    rounds = Rounds()
    run, also, then, tie, hold, finish = (
        rounds.run, rounds.also, rounds.then, rounds.tie, rounds.hold, rounds.finish
    )
    me_rep = lax.axis_index("rep")

    gather_mixing = Task(mixing_gather(mixing_weight))
    recut_qkv = Task(chip_exchange(recut_piece([query_weight, key_weight, value_weight])))
    run(gather_mixing, recut_qkv)
    run(gather_mixing, recut_qkv)
    finish(gather_mixing)
    mixing_rows = gather_mixing.value
    mixing_mean = jnp.sum(mixing_rows.astype(F32), axis=2)[:, None, :] / width
    static = jnp.pad(mixing_static, ((0, 0), (0, 0), (0, LANES - 6)))
    entering, packed, x = token_call(
        first_kernel, tokens, [streams, mixing_rows[0], static[0]],
        [
            shape((tokens, width), BF16), shape((count, tokens, LANES), F32),
            shape((count, tokens, width), BF16),
        ],
    )
    part = output_weight.shape[0] // lax.axis_size("rep")
    output_part = lax.dynamic_slice_in_dim(output_weight, me_rep * part, part, 0)
    gather_in = Task(line_gather(jnp.concatenate([entering, output_part], axis=0)))
    finish(recut_qkv)
    gather_qkv = Task(rep_gather(stack_units(recut_qkv.value, 2), True))
    run(gather_in, gather_qkv)
    gate_up_piece = recut_piece([tie(gate_weight), up_weight])
    run(gather_in, gather_qkv)
    hold(gate_up_piece)

    places = tie(packed_at)[0].reshape(line, 2, tokens)
    turned = jnp.roll(places, -spot, axis=0)
    place = jnp.concatenate(
        [
            lax.dynamic_index_in_dim(turned, core, 1, keepdims=False).reshape(-1),
            lax.dynamic_index_in_dim(turned, 1 - core, 1, keepdims=False).reshape(-1),
        ]
    )
    start = sequence_places(place, lengths[0])
    cosine, sine = rope_tables(place - start, head_width)
    w = tie(cotangent).transpose(1, 0, 2)
    run(gather_in)
    hold(cosine, sine, w)
    finish(gather_in, gather_qkv)
    gathered = gather_in.value.reshape(line, tokens + part, width)
    mine_in = gathered[:, :tokens].reshape(line * tokens, width)
    swap = Task(other_core(mine_in))
    gather_output = Task(rep_gather(cut_units(gathered[:, tokens:], 2), True))
    recut_gate_up = Task(shard_exchange(gate_up_piece, (shards // 4, 3 * shards // 8, shards // 8)))
    run(swap, recut_gate_up, gather_output)
    attention_weight = recut_join(gather_qkv.value)
    hold(attention_weight)
    mine_qkv = product(mine_in, attention_weight, into=0)
    other_in = swap.value
    run(recut_gate_up, gather_output)
    qkv = product(other_in, attention_weight, into=1, filled=(mine_qkv,))
    attended, rot_q, rot_k, logs = attention(qkv, cosine, sine, place, start, heads)
    finish(gather_output)
    hold(attended)
    gate_up_low = [lax.dynamic_index_in_dim(gate_up_piece, me, 0, keepdims=False)]
    gate_up_low += recut_gate_up.arrived[: shards // 2 - 1]
    gather_low = Task(rep_gather(stack_units(gate_up_low, 2), True))
    tokens_out = Task(to_tokens(attended.reshape(2, line, tokens, local)))
    run(tokens_out, recut_gate_up, gather_low)
    output_mine = rows_in_order(gather_output.value)
    swap = Task(other_core(output_mine))
    run(tokens_out, swap, recut_gate_up)
    branch = dot(tokens_out.value[0], output_mine) + dot(tokens_out.value[1], swap.value)

    middle, entering_next, down_in, packed_next = token_call(
        middle_kernel, tokens,
        [x, packed, static[0], branch, w, mixing_rows[1], static[1]],
        [
            shape((count, tokens, width), F32), shape((tokens, width), BF16),
            shape((tokens, width), BF16), shape((count, tokens, LANES), F32),
        ],
    )
    finish(recut_gate_up)
    gather_high = Task(rep_gather(stack_units(recut_gate_up.value[shards // 2 :], 2), True))
    gather_ffn, gather_down = Task(direct_gather(entering_next, 2)), Task(direct_gather(down_in, 2))
    run(gather_ffn, gather_low)
    finish(gather_low)
    gate_up = recut_join(gather_low.value)
    run(gather_ffn, gather_high)
    finish(gather_ffn)
    mine_ffn = gather_ffn.value
    swap = Task(other_core(mine_ffn))
    run(gather_down, swap, gather_high)
    finish(gather_high)
    gate_up = recut_join(gather_high.value, shards // 2, (gate_up,))
    hidden = gate_up.shape[1] // 2
    filled = ffn_forward(mine_ffn, gate_up, 0)
    other_ffn = swap.value
    run(gather_down)
    active, by_gate, by_up = ffn_forward(other_ffn, gate_up, 1, filled)
    theirs = product((active, 1), down_weight)
    finish(gather_down)
    mine_down = gather_down.value
    swap_z, swap = Task(other_core(theirs)), Task(other_core(mine_down))
    run(swap_z, swap)
    filled = ffn_backward(mine_down, down_weight, by_gate, by_up, 0)
    other_down = swap.value
    scatter_z = Task(direct_scatter(product((active, 0), down_weight, add=swap_z.value), 2))
    run(scatter_z)
    grad_both = ffn_backward(other_down, down_weight, by_gate, by_up, 1, (filled,))
    theirs = product((grad_both, 1), gate_up, NT)
    hold(theirs)
    swap = Task(other_core(theirs))
    run(scatter_z, swap)
    gate_up_blocks = columns_product([mine_ffn, other_ffn], [(grad_both, 0), (grad_both, 1)], 2)
    hold(*gate_up_blocks[0])
    finish(scatter_z)
    scatter_f = Task(direct_scatter(product((grad_both, 0), gate_up, NT, add=swap.value), 2))
    scatter_gate_up = Task(rep_scatter(gate_up_blocks))
    run(scatter_f, (scatter_gate_up, 1))
    down_blocks = rows_product([(active, 0), (active, 1)], [mine_down, other_down], 2)
    hold(*down_blocks[0])
    run(scatter_f, scatter_gate_up)
    finish(scatter_f)

    grad_middle, grad_branch, grad_beta, mixing_sum_next, static_sum_next = token_call(
        functools.partial(middle_back_kernel, line), tokens,
        [
            middle, packed_next, static[1], packed, static[0], w, branch, mixing_rows[1], mixing_mean[1],
            *scatter_z.value, *scatter_f.value,
        ],
        [
            shape((count, tokens, width), F32), shape((tokens, width), BF16), shape((tokens, LANES), F32),
            shape((LANES, width), F32), shape((8, LANES), F32),
        ],
    )
    gather_branch = Task(direct_gather(grad_branch, 2))
    run(gather_branch, scatter_gate_up)
    finish(scatter_gate_up)
    low = []
    recut_grad = Task(chip_exchange(jnp.concatenate(scatter_gate_up.value, axis=0), (line // 4, line // 4), low))
    (result,) = token_call(
        out_kernel, tokens, [tie(middle), packed_next, static[1], *scatter_z.value],
        [shape((tokens, count, width), BF16)],
    )
    scatter_down = Task(rep_scatter(down_blocks, True))
    run(gather_branch, scatter_down)
    hold(result)
    finish(gather_branch)
    mine_branch = gather_branch.value
    swap = Task(other_core(mine_branch))
    run(swap, scatter_down, recut_grad)
    finish(scatter_down)
    gather_down_rows = Task(rep_gather(scatter_down.value, True))
    grad_mine = product(mine_branch, output_weight, NT, into=0)
    other_branch = swap.value
    run(recut_grad, gather_down_rows)
    grad_attended = product(other_branch, output_weight, NT, into=1, filled=(grad_mine,))
    grad_qkv = attention_back(qkv, rot_q, rot_k, grad_attended, logs, cosine, sine, place, start, heads)
    theirs = product((grad_qkv, 1), attention_weight, NT)
    run(recut_grad, gather_down_rows)
    gather_low = Task(rep_gather(stack_units(low[: shards // 2], 2), True))
    hold(theirs)
    run(recut_grad, gather_low)
    qkv_blocks = columns_product([mine_in, other_in], [(grad_qkv, 0), (grad_qkv, 1)], 2)
    output_blocks = rows_product([(attended, 0), (attended, 1)], [mine_branch, other_branch], 2)
    hold(*qkv_blocks[0], *output_blocks[0])
    finish(recut_grad, gather_down_rows)
    gather_high = Task(rep_gather(stack_units(low[shards // 2 :], 2), True))
    swap = Task(other_core(theirs))
    scatter_output = Task(rep_scatter(output_blocks, True))
    run(swap, scatter_output)
    down_rows = rows_join(gather_down_rows.value)
    hold(down_rows)
    scatter_a = Task(direct_scatter(product((grad_qkv, 0), attention_weight, NT, add=swap.value), 2))
    scatter_qkv = Task(rep_scatter(qkv_blocks, True))
    run(scatter_a, scatter_qkv)
    run(scatter_a, scatter_qkv, gather_low)
    finish(scatter_qkv, scatter_a, gather_low)
    recut_qkv_grad = Task(chip_exchange(jnp.concatenate(scatter_qkv.value, axis=0)))
    grad_streams, mixing_sum, static_sum = token_call(
        first_back_kernel, tokens,
        [x, packed, static[0], grad_middle, grad_beta, mixing_rows[0], mixing_mean[0], *scatter_a.value],
        [shape((tokens, count, width), F32), shape((LANES, width), F32), shape((8, LANES), F32)],
    )
    run(recut_qkv_grad, gather_high, scatter_output)
    hold(grad_streams)
    run(recut_qkv_grad, gather_high)
    finish(recut_qkv_grad, gather_high, scatter_output)
    gather_qkv_grad = Task(rep_gather(stack_units(recut_qkv_grad.value, 2), True))
    gather_output = Task(rep_gather(scatter_output.value, True))
    mixing_sums = jnp.stack([mixing_sum, mixing_sum_next])
    mixing_sums = (mixing_sums[:, :6] + mixing_sums[:, 8:14]).reshape(12, shards, -1)
    small = jnp.concatenate(
        [
            jnp.pad(mixing_sums.transpose(1, 0, 2), ((0, 0), (0, 4), (0, 0))),
            jnp.broadcast_to(jnp.concatenate([static_sum, static_sum_next])[None], (shards, 16, LANES)),
        ],
        axis=2,
    )
    sum_last = Task(sum_small(small))
    run(sum_last, gather_qkv_grad, gather_output)
    gate_rows, up_rows = columns_join([[tie(v) for v in u] for u in gather_low.value + gather_high.value], 2)
    run(sum_last, gather_qkv_grad)
    hold(gate_rows)
    run(sum_last, gather_output)
    finish(gather_qkv_grad, gather_output, sum_last)
    output_rows = rows_join(gather_output.value)
    small = sum_last.value
    rows = width // shards
    own_mixing = jnp.swapaxes(small[:12, :rows].reshape(2, 6, rows), 1, 2)
    static_sums = jnp.stack([small[0:count, rows : rows + 6], small[8 : 8 + count, rows : rows + 6]])
    query_rows, key_rows, value_rows = columns_join(gather_qkv_grad.value, 3)
    return (
        result, grad_streams, query_rows, key_rows, value_rows, output_rows,
        gate_rows, up_rows, down_rows, own_mixing, static_sums,
    )


def solution(mesh):
    tokens = P(("rep", "shard"), None, None)
    rows = P("shard", None)
    return jax.shard_map(
        per_device,
        mesh=mesh,
        in_specs=(tokens, tokens, P("rep", None), P("rep", None)) + (rows,) * 7 + (P(None, "shard", None), P()),
        out_specs=(tokens, tokens) + (rows,) * 7 + (P(None, "shard", None), P()),
        check_vma=False,
    )
```

```python
import functools
import math

import jax
import jax.numpy as jnp
from jax import lax
from jax.experimental import pallas as pl
from jax.experimental.pallas import tpu as pltpu
from jax.sharding import PartitionSpec as P

HEADS = 16
EPSILON = 1e-05
NEGATIVE = -1e30
LANES = 128
LOG2E = 1.4426950408889634
F32 = jnp.float32
BF16 = jnp.bfloat16
NO_COST = pl.CostEstimate(flops=0, bytes_accessed=0, transcendentals=0)
NN = (((1,), (0,)), ((), ()))
NT = (((1,), (1,)), ((), ()))
TN = (((0,), (0,)), ((), ()))


def dot(a, b, dims=NN):
    return lax.dot_general(a, b, dims, preferred_element_type=F32)


def params(mib):
    return pltpu.CompilerParams(vmem_limit_bytes=mib << 20)


def after(value, *events):
    return lax.optimization_barrier((value, *events))[0] if events else value


def assemble_kernel(line, x_ref, *refs):
    rights, lefts, out_ref = refs[: line - 1], refs[line - 1 : -1], refs[-1]
    out_ref[0] = x_ref[...]
    for k in range(1, line):
        out_ref[k] = lefts[k - 1][...] + rights[line - k - 1][...]


class Task:
    def __init__(self, steps):
        self.steps, self.value, self.over, self.arrived = steps, None, False, []
        self.advance(None)

    def advance(self, arrived):
        self.arrived += arrived or []
        try:
            self.sends = list(self.steps.send(arrived))
            self.left = list(range(len(self.sends)))
            self.got = [None] * len(self.sends)
        except StopIteration as stop:
            self.value, self.over, self.left = stop.value, True, []


class Rounds:
    def __init__(self):
        self.base, self.fence, self.last = (), (), ()

    def hold(self, *values):
        self.fence += values

    def tie(self, value):
        return after(value, *self.fence)

    def run(self, *jobs):
        self.base, self.fence = self.fence, ()
        self.last = self.base
        self.send(jobs, self.base)

    def also(self, *jobs):
        self.last = self.send(jobs, self.base)

    def then(self, *jobs):
        self.last = self.send(jobs, self.last)

    def send(self, jobs, events):
        sends = []
        for job in jobs:
            task, pairs = job if isinstance(job, tuple) else (job, len(job.left))
            sends += [(task, i) for i in task.left[: 2 * pairs]]
        out = tuple(t.sends[i][0](after(t.sends[i][1], *events)) for t, i in sends)
        self.fence += out
        for (t, i), v in zip(sends, out):
            t.got[i] = v
            t.left.remove(i)
        for t in {id(t): t for t, _ in sends}.values():
            if not t.left:
                t.advance(t.got)
        return out

    def finish(self, *tasks):
        while any(not t.over for t in tasks):
            self.run(*tasks)


def sender(axis, pairs):
    return lambda x: lax.ppermute(x, axis, pairs)


def assemble_kernel(line, x_ref, *refs):
    rights, lefts, out_ref = refs[: line - 1], refs[line - 1 : -1], refs[-1]
    out_ref[0] = x_ref[...]
    for k in range(1, line):
        out_ref[k] = lefts[k - 1][...] + rights[line - k - 1][...]


def line_gather(x):
    line = lax.axis_size("shard") // 2
    right = left = x
    rights, lefts = [], []
    for step in range(line - 1):
        right, left = yield [
            (sender("shard", [(2 * p + c, 2 * p + 2 + c) for p in range(step, line - 1) for c in range(2)]), right),
            (sender("shard", [(2 * p + c, 2 * p - 2 + c) for p in range(1, line - step) for c in range(2)]), left),
        ]
        rights.append(right)
        lefts.append(left)
    rows, width = x.shape
    (mine,) = token_call(
        functools.partial(assemble_kernel, line), rows, [x, *rights, *lefts],
        [jax.ShapeDtypeStruct((line, rows, width), x.dtype)], block=rows // 2 if rows % 32 == 0 else rows,
    )
    return mine.reshape(line * rows, width)


def other_core(x):
    size = lax.axis_size("shard")
    (other,) = yield [(sender("shard", [(i, i ^ 1) for i in range(size)]), x)]
    return other


def line_shift(k):
    line = lax.axis_size("shard") // 2
    return sender("shard", [(2 * p + c, 2 * ((p + k) % line) + c) for p in range(line) for c in range(2)])


def shifts(line, steps):
    return [list(range(1, line))] if steps == 1 else [list(range(1, line, 2)), list(range(2, line, 2))]


def direct_gather(x, steps=1):
    line = lax.axis_size("shard") // 2
    came = {}
    for step in shifts(line, steps):
        came |= dict(zip(step, (yield [(line_shift(k), x) for k in step])))
    return jnp.concatenate([x] + [came[line - q] for q in range(1, line)], axis=0)


def direct_scatter(rows, steps=1):
    line = lax.axis_size("shard") // 2
    parts = list(rows.reshape(line, rows.shape[0] // line, -1))
    came = [parts[0]]
    for step in shifts(line, steps):
        came += yield [(line_shift(k), parts[k]) for k in step]
    return came


def rep_sender(bit):
    return sender("rep", [(i, i ^ (1 << bit)) for i in range(lax.axis_size("rep"))])


def rep_orders(units):
    bits = list(range(lax.axis_size("rep").bit_length() - 1))
    return [bits] * (units // 2) + [bits[::-1]] * (units - units // 2)


def paired(sends):
    middle = len(sends) // 2
    return [v for pair in zip(sends[:middle], sends[middle:]) for v in pair]


def rep_scatter(units, merge=False):
    orders = rep_orders(len(units))
    units = [dict(enumerate(u)) for u in units]
    for i in range(len(orders[0])):
        bits = [1 << o[i] for o in orders]
        keys = [[m for m in unit if m & bit] for unit, bit in zip(units, bits)]
        came = yield from exchange_blocks(units, keys, [o[i] for o in orders], merge)
        units = [
            {m ^ bit: unit[m ^ bit] + v for m, v in zip(key, new)}
            for unit, bit, key, new in zip(units, bits, keys, came)
        ]
    return [u[0] for u in units]


def rep_gather(units, merge=False):
    orders = [o[::-1] for o in rep_orders(len(units))]
    units = [{0: u} for u in units]
    for i in range(len(orders[0])):
        keys = [list(unit) for unit in units]
        came = yield from exchange_blocks(units, keys, [o[i] for o in orders], merge)
        for unit, o, key, new in zip(units, orders, keys, came):
            unit |= {m ^ (1 << o[i]): v for m, v in zip(key, new)}
    return [[u[m] for m in range(len(u))] for u in units]


def rep_flip(m):
    return sender("rep", [(i, i ^ m) for i in range(lax.axis_size("rep"))])


def rep_scatter_direct(blocks):
    came = yield [(rep_flip(m), blocks[m]) for m in range(1, len(blocks))]
    return sum(v.astype(F32) for v in [blocks[0], *came]).astype(blocks[0].dtype)


def rep_gather_direct(block):
    came = yield [(rep_flip(m), block) for m in range(1, lax.axis_size("rep"))]
    return [block, *came]


def exchange_blocks(units, keys, bits, merge):
    if merge:
        came = yield [
            (rep_sender(bit), jnp.concatenate([unit[m] for m in key]) if len(key) > 1 else unit[key[0]])
            for unit, key, bit in paired(list(zip(units, keys, bits)))
        ]
        order = paired(list(range(len(units))))
        return [cut_units(came[order.index(u)], len(keys[u])) for u in range(len(units))]
    flat = paired([(u, m) for u, key in enumerate(keys) for m in key])
    came = yield [(rep_sender(bits[u]), units[u][m]) for u, m in flat]
    came = dict(zip(flat, came))
    return [[came[u, m] for m in key] for u, key in enumerate(keys)]


def chip_exchange(x, counts=(), out=None):
    shards = lax.axis_size("shard")
    me = lax.axis_index("shard")
    pick = lambda k: lax.dynamic_index_in_dim(x, me ^ k, 0, keepdims=False)
    (came,) = yield [
        (sender("shard", [(i, i ^ 1) for i in range(shards)]), jnp.stack([pick(k) for k in range(1, shards, 2)]))
    ]
    held = [jnp.stack([pick(2 * q), came[q]]) for q in range(shards // 2)]
    out, counts = [] if out is None else out, list(counts)
    out += [held[0][0], held[0][1]]
    while len(out) < shards:
        q = len(out) // 2
        step = range(q, min(shards // 2, q + (counts.pop(0) if counts else shards)))
        came = yield [(sender("shard", [(i, i ^ (2 * q)) for i in range(shards)]), held[q]) for q in step]
        out += [v[f] for v in came for f in range(2)]
    return out


def stack_units(blocks, count):
    size = len(blocks) // count
    return [jnp.stack(blocks[i * size : (i + 1) * size]) for i in range(count)]


def to_tokens(x):
    shards = lax.axis_size("shard")
    line = shards // 2
    (came,) = yield [(sender("shard", [(i, i ^ 1) for i in range(shards)]), x[1])]
    held = jnp.stack([x[0], came], axis=1)
    came = yield [
        (sender("shard", [(2 * p + c, 2 * ((p + k) % line) + c) for p in range(line) for c in range(2)]), held[k])
        for k in range(1, line)
    ]
    came = [held[0], *came]
    return [jnp.concatenate([came[(line - q) % line][f] for q in range(line)], axis=1) for f in range(2)]


def cut_units(x, count):
    size = x.shape[0] // count
    return [x[i * size : (i + 1) * size] for i in range(count)]


def recut_piece(weights):
    shards, reps = lax.axis_size("shard"), lax.axis_size("rep")
    part = weights[0].shape[0] // reps
    start = lax.axis_index("rep") * part
    pieces = [
        lax.dynamic_slice_in_dim(w, start, part, 0).reshape(part, shards, -1).transpose(1, 0, 2) for w in weights
    ]
    return jnp.concatenate(pieces, axis=2)


def halves(x):
    return cut_units(x, 2)


def unit_specs(units):
    size = units[0][0].shape[0]
    return [
        pl.BlockSpec((1,) + v.shape[1:], lambda k, me, g=g: (jnp.clip(k - g * size, 0, size - 1), 0, 0))
        for g, u in enumerate(units) for v in u
    ]


def columns_kernel(units, reps, parts, me_ref, *refs):
    outs = refs[-parts:]
    size = pl.num_programs(0) // units
    part = refs[0].shape[1]
    for g in range(units):
        @pl.when(pl.program_id(0) // size == g)
        def _(chosen=refs[g * reps : (g + 1) * reps]):
            for m in range(reps):
                row = pl.multiple_of((me_ref[0] ^ m) * part, part)
                for i, out_ref in enumerate(outs):
                    width = out_ref.shape[1]
                    out_ref[pl.ds(row, part), :] = chosen[m][0, :, i * width : (i + 1) * width].astype(out_ref.dtype)


def join(units, parts, spec, shapes, filled=(), mib=32):
    reps = lax.axis_size("rep")
    operands = [v for u in units for v in u]
    return pl.pallas_call(
        functools.partial(columns_kernel, len(units), reps, parts),
        grid_spec=pltpu.PrefetchScalarGridSpec(
            num_scalar_prefetch=1,
            grid=(len(units) * units[0][0].shape[0],),
            in_specs=unit_specs(units) + [pl.BlockSpec(memory_space=pl.ANY)] * len(filled),
            out_specs=[spec] * parts,
        ),
        out_shape=shapes,
        input_output_aliases={1 + len(operands) + i: i for i in range(len(filled))},
        compiler_params=params(mib),
        cost_estimate=NO_COST,
    )(jnp.stack([lax.axis_index("rep"), lax.axis_index("shard")]).astype(jnp.int32), *operands, *filled)


def recut_join(units, first=0, filled=()):
    shards, reps = lax.axis_size("shard"), lax.axis_size("rep")
    _, part, columns = units[0][0].shape
    rows = part * reps
    return join(
        units, 1, pl.BlockSpec((rows, columns), lambda k, me: ((k + first) ^ me[1], 0)),
        [jax.ShapeDtypeStruct((shards * rows, columns), BF16)], filled,
    )[0]


def rows_in_order(units):
    blocks, part, columns = units[0][0].shape
    rows = part * lax.axis_size("rep")
    return join(
        units, 1, pl.BlockSpec((rows, columns), lambda k, me: (k, 0)),
        [jax.ShapeDtypeStruct((len(units) * blocks * rows, columns), BF16)],
    )[0]


def columns_join(units, parts):
    shards, reps = lax.axis_size("shard"), lax.axis_size("rep")
    _, part, columns = units[0][0].shape
    rows, width = part * reps, columns // parts
    return join(
        units, parts, pl.BlockSpec((rows, width), lambda k, me: (0, k ^ me[1])),
        [jax.ShapeDtypeStruct((rows, shards * width), F32)] * parts, mib=56 if parts == 2 else 32,
    )


def rows_kernel(units, reps, me_ref, *refs):
    out_ref = refs[-1]
    part = refs[0].shape[0]
    for u in range(units):
        for m in range(reps):
            row = pl.multiple_of((me_ref[0] ^ m) * (units * part) + u * part, part)
            out_ref[pl.ds(row, part), :] = refs[u * reps + m][...].astype(F32)


def rows_join(units):
    reps = lax.axis_size("rep")
    operands = [v for u in units for v in u]
    part, columns = operands[0].shape
    block = 512 if columns % 512 == 0 else columns
    return pl.pallas_call(
        functools.partial(rows_kernel, len(units), reps),
        grid_spec=pltpu.PrefetchScalarGridSpec(
            num_scalar_prefetch=1,
            grid=(columns // block,),
            in_specs=[pl.BlockSpec((part, block), lambda j, me: (0, j))] * len(operands),
            out_specs=pl.BlockSpec((part * len(operands), block), lambda j, me: (0, j)),
        ),
        out_shape=jax.ShapeDtypeStruct((part * len(operands), columns), F32),
        compiler_params=params(32),
        cost_estimate=NO_COST,
    )(lax.axis_index("rep").astype(jnp.int32)[None], *operands)


def mixing_kernel(me_ref, *refs):
    out_ref = refs[-1]
    out_ref[...] = jnp.zeros_like(out_ref)
    width = refs[0].shape[2]
    for k, ref in enumerate(refs[:-1]):
        start = pl.multiple_of((me_ref[0] ^ k) * width, width)
        out_ref[:, : ref.shape[1], pl.ds(start, width)] = ref[...]


def mixing_gather(weight):
    shards = lax.axis_size("shard")
    piece = jnp.pad(jnp.swapaxes(weight, 1, 2), ((0, 0), (0, 2), (0, 0)))
    piece = jnp.concatenate([piece, piece], axis=1)
    (came,) = yield [(sender("shard", [(i, i ^ 1) for i in range(shards)]), piece)]
    held = jnp.stack([piece, came])
    came = yield [
        (sender("shard", [(i, i ^ (2 * q)) for i in range(shards)]), held) for q in range(1, shards // 2)
    ]
    came = [v[f] for v in [held, *came] for f in range(2)]
    return pl.pallas_call(
        mixing_kernel,
        grid_spec=pltpu.PrefetchScalarGridSpec(
            num_scalar_prefetch=1,
            grid=(1,),
            in_specs=[pl.BlockSpec(piece.shape, lambda i, me: (0, 0, 0))] * shards,
            out_specs=pl.BlockSpec((2, LANES, shards * piece.shape[2]), lambda i, me: (0, 0, 0)),
        ),
        out_shape=jax.ShapeDtypeStruct((2, LANES, shards * piece.shape[2]), BF16),
        compiler_params=params(32),
    )(lax.axis_index("shard").astype(jnp.int32)[None], *came)


def sum_small(blocks):
    shards, reps = lax.axis_size("shard"), lax.axis_size("rep")
    me = lax.axis_index("shard")
    blocks = blocks.reshape((shards // 2, 2) + blocks.shape[1:])
    pick = lambda f: lax.dynamic_index_in_dim(blocks, (me % 2) ^ f, 1, keepdims=False)
    (came,) = yield [(sender("shard", [(i, i ^ 1) for i in range(shards)]), pick(1))]
    pair = pick(0) + came
    take = lambda q: lax.dynamic_index_in_dim(pair, (me // 2) ^ q, 0, keepdims=False)
    total = take(0)
    came = yield [
        (sender("shard", [(i, i ^ (2 * q)) for i in range(shards)]), take(q)) for q in range(1, shards // 2)
    ]
    for v in came:
        total = total + v
    came = yield [(sender("rep", [(i, i ^ k) for i in range(reps)]), total) for k in range(1, reps)]
    terms = [total, *came]
    while len(terms) > 1:
        terms = [a + b for a, b in zip(terms[::2], terms[1::2])]
    return terms[0]


def lane(shape):
    return lax.broadcasted_iota(jnp.int32, shape, len(shape) - 1)


def column(values, index):
    return values[:, index : index + 1]


def split(values):
    high = values.astype(BF16)
    return high, (values - high.astype(F32)).astype(BF16)


def moments(values):
    mean = jnp.mean(values, axis=-1, keepdims=True)
    centred = values - mean
    spread = jnp.mean(centred * centred, axis=-1, keepdims=True)
    return mean, centred, lax.rsqrt(spread + EPSILON)


def mix_forward(streams, weight, static):
    count = len(streams)
    rows = streams[0].shape[0]
    stats = [moments(y) for y in streams]
    parts = [split(centred) for _, centred, _ in stats]
    raw = dot(jnp.concatenate([p[0] for p in parts] + [p[1] for p in parts], axis=0), weight, NT)
    at = lane((rows, LANES))
    pres, coefficients = [], []
    for i in range(count):
        pre = (raw[i * rows : (i + 1) * rows] + raw[(count + i) * rows : (count + i + 1) * rows]) * stats[i][2]
        pres.append(pre)
        coefficients.append(static[i : i + 1] + jnp.tanh(pre))
    entering = sum(column(c, 0) * y for c, y in zip(coefficients, streams))
    mean, centred, scale = moments(entering)
    packed = []
    for i in range(count):
        value = jnp.where(at < 6, pres[i], 0.0)
        value = jnp.where(at == 6, stats[i][0], jnp.where(at == 7, stats[i][2], value))
        packed.append(jnp.where(at == 8, mean, jnp.where(at == 9, scale, value)))
    return centred * scale, coefficients, packed


def mix_carry(streams, coefficients, j):
    return sum(column(c, 1 + j) * y for c, y in zip(coefficients, streams))


def mix_backward(streams, packed, static, grad_entering, grad_carried, grad_beta, weight_rows, weight_mean):
    count = len(streams)
    rows, width = streams[0].shape
    at = lane((rows, LANES))
    tanhs = [jnp.where(at < 6, jnp.tanh(p), 0.0) for p in packed]
    coefficients = [static[i : i + 1] + tanhs[i] for i in range(count)]
    mean, scale = column(packed[0], 8), column(packed[0], 9)
    entering = (sum(column(c, 0) * y for c, y in zip(coefficients, streams)) - mean) * scale
    inner = jnp.mean(grad_entering * entering, axis=-1, keepdims=True)
    outer = jnp.mean(grad_entering, axis=-1, keepdims=True)
    grad_sum = scale * (grad_entering - outer - entering * inner)
    grads, both, normed, scalars = [], [], [], []
    for i in range(count):
        y = streams[i]
        value = jnp.where(at == 0, jnp.sum(grad_sum * y, axis=-1, keepdims=True), 0.0)
        for j in range(count):
            value = jnp.where(at == 1 + j, jnp.sum(grad_carried[j] * y, axis=-1, keepdims=True), value)
        value = jnp.where(at == 1 + count, grad_beta[i], value)
        grad_pre = value * (1.0 - tanhs[i] * tanhs[i])
        high = grad_pre.astype(BF16).astype(F32)
        low = grad_pre - high
        both.append((high + pltpu.roll(low, 8, 1)).astype(BF16))
        grads.append(value)
        normed.append((y - column(packed[i], 6)) * column(packed[i], 7))
        scalars.append((
            jnp.sum(grad_pre * weight_mean, axis=-1, keepdims=True),
            jnp.sum(jnp.where(at < 6, grad_pre * packed[i], 0.0), axis=-1, keepdims=True) / width,
        ))
    both = jnp.concatenate(both, axis=0)
    grad_normed = dot(both, weight_rows)
    mixing_sum = dot(both, jnp.concatenate([n.astype(BF16) for n in normed], axis=0), TN)
    out = []
    for i in range(count):
        value = column(coefficients[i], 0) * grad_sum
        for j in range(count):
            value = value + column(coefficients[i], 1 + j) * grad_carried[j]
        a, b = scalars[i]
        out.append(
            value + column(packed[i], 7) * (grad_normed[i * rows : (i + 1) * rows] - a - normed[i] * b)
        )
    return out, mixing_sum, grads


def load_streams(ref):
    return [ref[i].astype(F32) for i in range(ref.shape[0])]


def coefficients_of(packed, static):
    return [static[i : i + 1] + jnp.tanh(packed[i]) for i in range(len(packed))]


def first_kernel(x_ref, weight_ref, static_ref, entering_ref, packed_ref, turned_ref):
    streams = [x_ref[:, i, :] for i in range(x_ref.shape[1])]
    for i, stream in enumerate(streams):
        turned_ref[i] = stream
    entering, _, packed = mix_forward([v.astype(F32) for v in streams], weight_ref[...], static_ref[...])
    entering_ref[...] = entering.astype(BF16)
    for i, value in enumerate(packed):
        packed_ref[i] = value


def middle_kernel(
    x_ref, packed_ref, static_ref, branch_ref, w_ref, weight_ref, static_next_ref,
    m_ref, entering_ref, down_ref, packed_next_ref,
):
    streams = load_streams(x_ref)
    count = len(streams)
    coefficients = coefficients_of([packed_ref[i] for i in range(count)], static_ref[...])
    branch = branch_ref[...]
    middle = []
    for j in range(count):
        middle.append(mix_carry(streams, coefficients, j) + column(coefficients[j], 5) * branch)
        m_ref[j] = middle[j]
    entering, following, packed = mix_forward(middle, weight_ref[...], static_next_ref[...])
    entering_ref[...] = entering.astype(BF16)
    for i, value in enumerate(packed):
        packed_next_ref[i] = value
    down_ref[...] = sum(column(following[j], 5) * w_ref[j].astype(F32) for j in range(count)).astype(BF16)


def total(refs):
    return sum(ref[...].astype(F32) for ref in refs)


def out_kernel(m_ref, packed_ref, static_ref, *refs):
    out_ref = refs[-1]
    streams = load_streams(m_ref)
    count = len(streams)
    coefficients = coefficients_of([packed_ref[i] for i in range(count)], static_ref[...])
    z = total(refs[:-1])
    for j in range(count):
        out_ref[:, j, :] = (mix_carry(streams, coefficients, j) + column(coefficients[j], 5) * z).astype(BF16)


def accumulate(step, mixing_ref, static_ref, mixing_sum, grads):
    @pl.when(step == 0)
    def _():
        mixing_ref[...] = jnp.zeros_like(mixing_ref)
        static_ref[...] = jnp.zeros_like(static_ref)

    mixing_ref[...] += mixing_sum
    at = lax.broadcasted_iota(jnp.int32, static_ref.shape, 0)
    sums = jnp.zeros(static_ref.shape, F32)
    for i, grad in enumerate(grads):
        sums = jnp.where(at == i, jnp.sum(grad, axis=0, keepdims=True), sums)
    static_ref[...] += sums


def middle_back_kernel(
    terms, m_ref, packed_ref, static_ref, packed_first_ref, static_first_ref, w_ref, branch_ref,
    weight_rows_ref, weight_mean_ref, *refs,
):
    grad_m_ref, grad_branch_ref, grad_beta_ref, mixing_ref, static_sum_ref = refs[2 * terms :]
    streams = load_streams(m_ref)
    count = len(streams)
    cotangent = load_streams(w_ref)
    z = total(refs[:terms])
    grad_entering = total(refs[terms : 2 * terms])
    grad_beta = [jnp.sum(w * z, axis=-1, keepdims=True) for w in cotangent]
    grads, mixing_sum, grad_pres = mix_backward(
        streams, [packed_ref[i] for i in range(count)], static_ref[...], grad_entering, cotangent, grad_beta,
        weight_rows_ref[...], weight_mean_ref[...],
    )
    accumulate(pl.program_id(0), mixing_ref, static_sum_ref, mixing_sum, grad_pres)
    first = coefficients_of([packed_first_ref[i] for i in range(count)], static_first_ref[...])
    branch = branch_ref[...]
    at = lane(grad_beta_ref.shape)
    beta = jnp.zeros(grad_beta_ref.shape, F32)
    for j in range(count):
        grad_m_ref[j] = grads[j]
        beta = jnp.where(at == j, jnp.sum(grads[j] * branch, axis=-1, keepdims=True), beta)
    grad_beta_ref[...] = beta
    grad_branch_ref[...] = sum(column(first[j], 5) * grads[j] for j in range(count)).astype(BF16)


def first_back_kernel(
    x_ref, packed_ref, static_ref, grad_m_ref, grad_beta_ref, weight_rows_ref, weight_mean_ref, *refs
):
    grad_ref, mixing_ref, static_sum_ref = refs[-3:]
    streams = load_streams(x_ref)
    count = len(streams)
    grad_entering = total(refs[:-3])
    beta = grad_beta_ref[...]
    grads, mixing_sum, grad_pres = mix_backward(
        streams, [packed_ref[i] for i in range(count)], static_ref[...], grad_entering,
        [grad_m_ref[i] for i in range(count)], [column(beta, i) for i in range(count)],
        weight_rows_ref[...], weight_mean_ref[...],
    )
    accumulate(pl.program_id(0), mixing_ref, static_sum_ref, mixing_sum, grad_pres)
    for i in range(count):
        grad_ref[:, i, :] = grads[i]


def token_call(kernel, tokens, operands, outputs, block=None, mib=40):
    block = block or (32 if tokens % 32 == 0 else tokens)

    def spec(shape):
        if tokens not in shape[:-1]:
            return pl.BlockSpec(shape, lambda i, n=len(shape): (0,) * n)
        axis = shape.index(tokens)
        cut = tuple(block if d == axis else s for d, s in enumerate(shape))
        return pl.BlockSpec(cut, lambda i, axis=axis, n=len(shape): tuple(i if d == axis else 0 for d in range(n)))

    size = sum(math.prod(o.shape) * o.dtype.itemsize for o in list(operands) + list(outputs))
    return pl.pallas_call(
        kernel,
        grid=(tokens // block,),
        in_specs=[spec(o.shape) for o in operands],
        out_specs=[spec(o.shape) for o in outputs],
        out_shape=list(outputs),
        compiler_params=params(mib),
        cost_estimate=NO_COST,
    )(*operands)


def rows_of(operand):
    return operand[0].shape[0] // 2 if isinstance(operand, tuple) else operand.shape[0]


def whole_of(operand):
    return operand[0] if isinstance(operand, tuple) else operand


def half_of(operand):
    return operand[1] if isinstance(operand, tuple) else 0


def tile_of(size):
    return next((t for t in (512, 384, 256, 128) if size % t == 0), size)


def product_kernel(dims, added, a_ref, b_ref, *refs):
    out = dot(a_ref[...], b_ref[...], dims)
    if added:
        out = out + refs[0][...].astype(F32)
    refs[-1][...] = out.astype(refs[-1].dtype)


def product(a, b, dims=NN, add=None, into=None, filled=()):
    rows, depth = rows_of(a), whole_of(a).shape[1]
    half, columns = half_of(a), b.shape[0] if dims == NT else b.shape[1]
    tile = tile_of(columns)
    operands = [whole_of(a), b] + ([] if add is None else [add]) + list(filled)
    specs = [
        pl.BlockSpec((rows, depth), lambda j: (half, 0)),
        pl.BlockSpec((tile, depth), lambda j: (j, 0)) if dims == NT else pl.BlockSpec((depth, tile), lambda j: (0, j)),
    ]
    if add is not None:
        specs.append(pl.BlockSpec((rows, tile), lambda j: (0, j)))
    specs += [pl.BlockSpec(memory_space=pl.ANY)] * len(filled)
    at = into or 0
    return pl.pallas_call(
        functools.partial(product_kernel, dims, add is not None),
        grid=(columns // tile,),
        in_specs=specs,
        out_specs=pl.BlockSpec((rows, tile), lambda j: (at, j)),
        out_shape=jax.ShapeDtypeStruct((rows if into is None else 2 * rows, columns), BF16),
        input_output_aliases={len(operands) - 1: 0} if filled else {},
        compiler_params=params(40),
        cost_estimate=NO_COST,
    )(*operands)


def columns_product_kernel(units, reps, me_ref, x0, x1, y0, y1, *refs):
    outs, sums = refs[:-1], refs[-1]
    sums[...] = dot(x0[...], y0[...], TN) + dot(x1[...], y1[...], TN)
    step = pl.program_id(0)
    size = pl.num_programs(0) // units
    part = sums.shape[0] // reps
    for u in range(units):
        @pl.when(step // size == u)
        def _(u=u):
            for m in range(reps):
                row = pl.multiple_of((me_ref[0] ^ m) * part, part)
                outs[u * reps + m][0] = sums[pl.ds(row, part), :].astype(BF16)


def columns_product(xs, ys, units):
    shards, reps = lax.axis_size("shard"), lax.axis_size("rep")
    tokens, columns = rows_of(ys[0]), whole_of(ys[0]).shape[1]
    rows = whole_of(xs[0]).shape[1] // shards
    size, part = shards // units, rows // reps
    x_specs = [pl.BlockSpec((tokens, rows), lambda s, me, h=half_of(x): (h, s)) for x in xs]
    y_specs = [pl.BlockSpec((tokens, columns), lambda s, me, h=half_of(y): (h, 0)) for y in ys]
    out = pl.pallas_call(
        functools.partial(columns_product_kernel, units, reps),
        grid_spec=pltpu.PrefetchScalarGridSpec(
            num_scalar_prefetch=1,
            grid=(shards,),
            in_specs=x_specs + y_specs,
            out_specs=[
                pl.BlockSpec((1, part, columns), lambda s, me, u=u: (jnp.clip(s - u * size, 0, size - 1), 0, 0))
                for u in range(units) for _ in range(reps)
            ],
            scratch_shapes=[pltpu.VMEM((rows, columns), F32)],
        ),
        out_shape=[jax.ShapeDtypeStruct((size, part, columns), BF16)] * (units * reps),
        compiler_params=params(48),
        cost_estimate=NO_COST,
    )(lax.axis_index("rep").astype(jnp.int32)[None], *[whole_of(v) for v in [*xs, *ys]])
    return [out[u * reps : (u + 1) * reps] for u in range(units)]


def rows_product_kernel(units, reps, me_ref, x0, x1, y0, y1, *refs):
    outs, sums = refs[:-1], refs[-1]
    sums[...] = dot(x0[...], y0[...], TN) + dot(x1[...], y1[...], TN)
    part = outs[0].shape[0]
    for u in range(units):
        for m in range(reps):
            row = pl.multiple_of((me_ref[0] ^ m) * (units * part) + u * part, part)
            outs[u * reps + m][...] = sums[pl.ds(row, part), :].astype(BF16)


def rows_product(xs, ys, units):
    reps = lax.axis_size("rep")
    tokens, columns = rows_of(ys[0]), whole_of(ys[0]).shape[1]
    rows = whole_of(xs[0]).shape[1]
    part, tile = rows // (units * reps), tile_of(columns)
    x_specs = [pl.BlockSpec((tokens, rows), lambda j, me, h=half_of(x): (h, 0)) for x in xs]
    y_specs = [pl.BlockSpec((tokens, tile), lambda j, me, h=half_of(y): (h, j)) for y in ys]
    out = pl.pallas_call(
        functools.partial(rows_product_kernel, units, reps),
        grid_spec=pltpu.PrefetchScalarGridSpec(
            num_scalar_prefetch=1,
            grid=(columns // tile,),
            in_specs=x_specs + y_specs,
            out_specs=[pl.BlockSpec((part, tile), lambda j, me: (0, j))] * (units * reps),
            scratch_shapes=[pltpu.VMEM((rows, tile), F32)],
        ),
        out_shape=[jax.ShapeDtypeStruct((part, columns), BF16)] * (units * reps),
        compiler_params=params(48),
        cost_estimate=NO_COST,
    )(lax.axis_index("rep").astype(jnp.int32)[None], *[whole_of(v) for v in [*xs, *ys]])
    return [out[u * reps : (u + 1) * reps] for u in range(units)]


def ffn_tile(hidden):
    return 256 if hidden % 256 == 0 else hidden


def chunks(rows):
    step = 320 if rows % 320 == 0 else rows
    return [slice(i, i + step) for i in range(0, rows, step)]


def ffn_kernel(x_ref, gate_ref, up_ref, *refs):
    active_ref, by_gate_ref, by_up_ref = refs[-3:]
    for cut in chunks(x_ref.shape[0]):
        gate = dot(x_ref[cut, :], gate_ref[...])
        up = dot(x_ref[cut, :], up_ref[...])
        sigmoid = 1.0 / (1.0 + jnp.exp2(gate * -LOG2E))
        swish = gate * sigmoid
        active_ref[cut, :] = (swish * up).astype(BF16)
        by_gate_ref[cut, :] = (up * sigmoid * (1.0 + gate - swish)).astype(BF16)
        by_up_ref[cut, :] = swish.astype(BF16)


def ffn_forward(x, weight, half, filled=()):
    rows, width = x.shape
    hidden = weight.shape[1] // 2
    tile = ffn_tile(hidden)
    tiles = hidden // tile
    return pl.pallas_call(
        ffn_kernel,
        grid=(tiles,),
        in_specs=[
            pl.BlockSpec((rows, width), lambda j: (0, 0)),
            pl.BlockSpec((width, tile), lambda j: (0, j)),
            pl.BlockSpec((width, tile), lambda j: (0, j + tiles)),
        ] + [pl.BlockSpec(memory_space=pl.ANY)] * len(filled),
        out_specs=[pl.BlockSpec((rows, tile), lambda j: (half, j))] * 3,
        out_shape=[jax.ShapeDtypeStruct((2 * rows, hidden), BF16)] * 3,
        input_output_aliases={3 + i: i for i in range(len(filled))},
        compiler_params=params(40),
        cost_estimate=NO_COST,
    )(x, weight, weight, *filled)


def ffn_back_kernel(tiles, x_ref, down_ref, by_gate_ref, by_up_ref, *refs):
    out_ref = refs[-1]
    step = pl.program_id(0)
    tile = down_ref.shape[0]
    for cut in chunks(x_ref.shape[0]):
        grad = dot(x_ref[cut, :], down_ref[...], NT)
        first = pl.multiple_of(step * tile, tile)
        second = pl.multiple_of((step + tiles) * tile, tile)
        out_ref[cut, pl.ds(first, tile)] = (grad * by_gate_ref[cut, :].astype(F32)).astype(BF16)
        out_ref[cut, pl.ds(second, tile)] = (grad * by_up_ref[cut, :].astype(F32)).astype(BF16)


def ffn_backward(x, down, by_gate, by_up, half, filled=()):
    rows, width = x.shape
    hidden = down.shape[0]
    tile = ffn_tile(hidden)
    tiles = hidden // tile
    return pl.pallas_call(
        functools.partial(ffn_back_kernel, tiles),
        grid=(tiles,),
        in_specs=[
            pl.BlockSpec((rows, width), lambda j: (0, 0)),
            pl.BlockSpec((tile, width), lambda j: (j, 0)),
            pl.BlockSpec((rows, tile), lambda j: (half, j)),
            pl.BlockSpec((rows, tile), lambda j: (half, j)),
        ] + [pl.BlockSpec(memory_space=pl.ANY)] * len(filled),
        out_specs=pl.BlockSpec((rows, 2 * hidden), lambda j: (half, 0)),
        out_shape=jax.ShapeDtypeStruct((2 * rows, 2 * hidden), BF16),
        input_output_aliases={4 + i: i for i in range(len(filled))},
        compiler_params=params(40),
        cost_estimate=NO_COST,
    )(x, down, by_gate, by_up, *filled)


def turn(values):
    return pltpu.roll(values, values.shape[-1] // 2, 1)


def allowed(place_ref, query_place, query_start):
    keys = place_ref[...]
    return (keys <= query_place) & (keys >= query_start)


def attend_kernel(
    heads, width, q_ref, k_ref, v_ref, cos_q, sin_q, cos_k, sin_k, key_place, query_place, query_start,
    out_ref, rot_q_ref, rot_k_ref, log_ref, value_t,
):
    scale = width ** (-0.5)

    @pl.when(pl.program_id(0) == 0)
    def _():
        for h in range(heads):
            cut = slice(h * width, (h + 1) * width)
            key = k_ref[:, cut].astype(F32)
            rot_k_ref[:, cut] = (key * cos_k[...] + turn(key) * sin_k[...]).astype(BF16)
            value_t[cut, :] = v_ref[:, cut].T

    mask = allowed(key_place, query_place[...], query_start[...])
    for h in range(heads):
        cut = slice(h * width, (h + 1) * width)
        query = q_ref[:, cut].astype(F32)
        query = (query * cos_q[...] + turn(query) * sin_q[...]).astype(BF16)
        rot_q_ref[:, cut] = query
        scores = jnp.where(mask, dot(rot_k_ref[:, cut], query, NT), NEGATIVE)
        top = jnp.max(scores, axis=0, keepdims=True)
        weights = jnp.exp2((scores - top) * (scale * LOG2E))
        total = jnp.sum(weights, axis=0, keepdims=True)
        weights = (weights * (1.0 / total)).astype(BF16)
        out_ref[:, cut] = dot(value_t[cut, :], weights).T.astype(BF16)
        log_ref[h : h + 1] = top * (scale * LOG2E) + jnp.log2(total)


def attend_back_kernel(
    heads, width, q_ref, k_ref, v_ref, grad_ref, log_ref, cos_q, sin_q, cos_k, sin_k, key_place, query_place,
    query_start, out_ref, key_t, sum_k, sum_v,
):
    scale = width ** (-0.5)
    step = pl.program_id(0)
    block = q_ref.shape[0]
    here = pl.ds(pl.multiple_of(step * block, block), block)

    @pl.when(step == 0)
    def _():
        for h in range(heads):
            cut = slice(h * width, (h + 1) * width)
            key_t[cut, :] = k_ref[:, cut].T
        sum_k[...] = jnp.zeros_like(sum_k)
        sum_v[...] = jnp.zeros_like(sum_v)

    mask = allowed(key_place, query_place[...], query_start[...])
    for h in range(heads):
        cut = slice(h * width, (h + 1) * width)
        query = q_ref[:, cut]
        grad = grad_ref[:, cut]
        scores = dot(k_ref[:, cut], query, NT) * (scale * LOG2E) - log_ref[h : h + 1]
        weights = jnp.exp2(jnp.where(mask, scores, NEGATIVE))
        grad_weights = dot(v_ref[:, cut], grad, NT)
        centre = jnp.sum(weights * grad_weights, axis=0, keepdims=True)
        grad_scores = (weights * (grad_weights - centre)).astype(BF16)
        grad_query = (dot(key_t[cut, :], grad_scores) * scale).T
        out_ref[here, cut] = (grad_query * cos_q[...] - turn(grad_query) * sin_q[...]).astype(BF16)
        sum_k[:, cut] += dot(grad_scores, query)
        sum_v[:, cut] += dot(weights.astype(BF16), grad)

    @pl.when(step == pl.num_programs(0) - 1)
    def _():
        for h in range(heads):
            cut = slice(h * width, (h + 1) * width)
            key = sum_k[:, cut] * scale
            second = slice((heads + h) * width, (heads + h + 1) * width)
            third = slice((2 * heads + h) * width, (2 * heads + h + 1) * width)
            out_ref[:, second] = (key * cos_k[...] - turn(key) * sin_k[...]).astype(BF16)
            out_ref[:, third] = sum_v[:, cut].astype(BF16)


def attention(qkv, cosine, sine, place, start, heads):
    tokens, width = qkv.shape[0], qkv.shape[1] // 3
    head_width = width // heads
    block = 256 if tokens % 256 == 0 else tokens
    row = lambda i: (i, 0)
    whole = lambda i: (0, 0)
    along = lambda i: (0, i)
    key_place = jnp.broadcast_to(place[:, None], (tokens, block))
    blocks = tokens // block
    return pl.pallas_call(
        functools.partial(attend_kernel, heads, head_width),
        grid=(blocks,),
        in_specs=[
            pl.BlockSpec((block, width), row),
            pl.BlockSpec((tokens, width), lambda i: (0, 1)),
            pl.BlockSpec((tokens, width), lambda i: (0, 2)),
            pl.BlockSpec((block, head_width), row),
            pl.BlockSpec((block, head_width), row),
            pl.BlockSpec((tokens, head_width), whole),
            pl.BlockSpec((tokens, head_width), whole),
            pl.BlockSpec((tokens, block), whole),
            pl.BlockSpec((1, block), along),
            pl.BlockSpec((1, block), along),
        ],
        out_specs=[
            pl.BlockSpec((block, width), row),
            pl.BlockSpec((block, width), row),
            pl.BlockSpec((tokens, width), whole),
            pl.BlockSpec((heads, block), along),
        ],
        out_shape=[
            jax.ShapeDtypeStruct((tokens, width), BF16),
            jax.ShapeDtypeStruct((tokens, width), BF16),
            jax.ShapeDtypeStruct((tokens, width), BF16),
            jax.ShapeDtypeStruct((heads, tokens), F32),
        ],
        scratch_shapes=[pltpu.VMEM((width, tokens), BF16)],
        compiler_params=params(48),
        cost_estimate=NO_COST,
    )(qkv, qkv, qkv, cosine, sine, cosine, sine, key_place, place[None], start[None])


def attention_back(qkv, rot_q, rot_k, grad, logs, cosine, sine, place, start, heads):
    tokens, width = rot_q.shape
    head_width = width // heads
    block = 256 if tokens % 256 == 0 else tokens
    row = lambda i: (i, 0)
    whole = lambda i: (0, 0)
    along = lambda i: (0, i)
    key_place = jnp.broadcast_to(place[:, None], (tokens, block))
    return pl.pallas_call(
        functools.partial(attend_back_kernel, heads, head_width),
        grid=(tokens // block,),
        in_specs=[
            pl.BlockSpec((block, width), row),
            pl.BlockSpec((tokens, width), whole),
            pl.BlockSpec((tokens, width), lambda i: (0, 2)),
            pl.BlockSpec((block, width), row),
            pl.BlockSpec((heads, block), along),
            pl.BlockSpec((block, head_width), row),
            pl.BlockSpec((block, head_width), row),
            pl.BlockSpec((tokens, head_width), whole),
            pl.BlockSpec((tokens, head_width), whole),
            pl.BlockSpec((tokens, block), whole),
            pl.BlockSpec((1, block), along),
            pl.BlockSpec((1, block), along),
        ],
        out_specs=pl.BlockSpec((tokens, 3 * width), whole),
        out_shape=jax.ShapeDtypeStruct((tokens, 3 * width), BF16),
        scratch_shapes=[
            pltpu.VMEM((width, tokens), BF16),
            pltpu.VMEM((tokens, width), F32),
            pltpu.VMEM((tokens, width), F32),
        ],
        compiler_params=params(56),
        cost_estimate=NO_COST,
    )(rot_q, rot_k, qkv, grad, logs, cosine, sine, cosine, sine, key_place, place[None], start[None])


def sequence_places(ordering, lengths):
    ending = jnp.cumsum(lengths)
    segment = jnp.sum((ordering[:, None] >= ending[None, :]).astype(jnp.int32), axis=1)
    opening = ending - lengths
    chosen = segment[:, None] == jnp.arange(lengths.shape[0], dtype=jnp.int32)[None, :]
    return jnp.sum(jnp.where(chosen, opening[None, :], 0), axis=1)


def rope_tables(position, head_width):
    middle = head_width // 2
    frequency = jnp.exp(
        jnp.arange(middle, dtype=F32) * (-2.0 * math.log(10000.0) / head_width)
    )
    angles = position.astype(F32)[:, None] * frequency[None, :]
    sine = jnp.sin(angles)
    cosine = jnp.cos(angles)
    return jnp.concatenate([cosine, cosine], axis=1), jnp.concatenate([-sine, sine], axis=1)


def per_device(
    streams, cotangent, lengths, packed_at, query_weight, key_weight, value_weight, output_weight,
    gate_weight, up_weight, down_weight, mixing_weight, mixing_static,
):
    shards = lax.axis_size("shard")
    line = shards // 2
    me = lax.axis_index("shard")
    spot, core = me // 2, me % 2
    tokens, count, width = streams.shape
    head_width = width // HEADS
    heads = HEADS // shards
    local = heads * head_width
    shape = jax.ShapeDtypeStruct

    rounds = Rounds()
    run, also, then, tie, hold, finish = (
        rounds.run, rounds.also, rounds.then, rounds.tie, rounds.hold, rounds.finish
    )
    me_rep = lax.axis_index("rep")

    gather_mixing = Task(mixing_gather(mixing_weight))
    recut_qkv = Task(chip_exchange(recut_piece([query_weight, key_weight, value_weight])))
    run(gather_mixing, recut_qkv)
    run(gather_mixing, recut_qkv)
    finish(gather_mixing)
    mixing_rows = gather_mixing.value
    mixing_mean = jnp.sum(mixing_rows.astype(F32), axis=2)[:, None, :] / width
    static = jnp.pad(mixing_static, ((0, 0), (0, 0), (0, LANES - 6)))
    entering, packed, x = token_call(
        first_kernel, tokens, [streams, mixing_rows[0], static[0]],
        [
            shape((tokens, width), BF16), shape((count, tokens, LANES), F32),
            shape((count, tokens, width), BF16),
        ],
    )
    part = output_weight.shape[0] // lax.axis_size("rep")
    output_part = lax.dynamic_slice_in_dim(output_weight, me_rep * part, part, 0)
    gather_in = Task(line_gather(jnp.concatenate([entering, output_part], axis=0)))
    finish(recut_qkv)
    gather_qkv = Task(rep_gather(stack_units(recut_qkv.value, 2), True))
    run(gather_in, gather_qkv)
    gate_up_piece = recut_piece([tie(gate_weight), up_weight])
    run(gather_in, gather_qkv)
    hold(gate_up_piece)

    places = tie(packed_at)[0].reshape(line, 2, tokens)
    turned = jnp.roll(places, -spot, axis=0)
    place = jnp.concatenate(
        [
            lax.dynamic_index_in_dim(turned, core, 1, keepdims=False).reshape(-1),
            lax.dynamic_index_in_dim(turned, 1 - core, 1, keepdims=False).reshape(-1),
        ]
    )
    start = sequence_places(place, lengths[0])
    cosine, sine = rope_tables(place - start, head_width)
    w = tie(cotangent).transpose(1, 0, 2)
    gate_up_blocks = []
    recut_gate_up = Task(chip_exchange(gate_up_piece, (line // 4, line // 4), gate_up_blocks))
    run(gather_in, recut_gate_up)
    hold(cosine, sine, w)
    finish(gather_in, gather_qkv)
    gathered = gather_in.value.reshape(line, tokens + part, width)
    mine_in = gathered[:, :tokens].reshape(line * tokens, width)
    swap = Task(other_core(mine_in))
    gather_output = Task(rep_gather(cut_units(gathered[:, tokens:], 2), True))
    run(swap, recut_gate_up, gather_output)
    attention_weight = recut_join(gather_qkv.value)
    hold(attention_weight)
    mine_qkv = product(mine_in, attention_weight, into=0)
    other_in = swap.value
    run(recut_gate_up, gather_output)
    qkv = product(other_in, attention_weight, into=1, filled=(mine_qkv,))
    attended, rot_q, rot_k, logs = attention(qkv, cosine, sine, place, start, heads)
    finish(gather_output)
    hold(attended)
    gather_low = Task(rep_gather(stack_units(gate_up_blocks[: shards // 2], 2), True))
    tokens_out = Task(to_tokens(attended.reshape(2, line, tokens, local)))
    run(tokens_out, recut_gate_up, gather_low)
    finish(recut_gate_up)
    output_mine = rows_in_order(gather_output.value)
    swap = Task(other_core(output_mine))
    run(tokens_out, swap)
    branch = dot(tokens_out.value[0], output_mine) + dot(tokens_out.value[1], swap.value)

    middle, entering_next, down_in, packed_next = token_call(
        middle_kernel, tokens,
        [x, packed, static[0], branch, w, mixing_rows[1], static[1]],
        [
            shape((count, tokens, width), F32), shape((tokens, width), BF16),
            shape((tokens, width), BF16), shape((count, tokens, LANES), F32),
        ],
    )
    finish(recut_gate_up)
    gather_high = Task(rep_gather(stack_units(gate_up_blocks[shards // 2 :], 2), True))
    gather_ffn, gather_down = Task(direct_gather(entering_next, 2)), Task(direct_gather(down_in, 2))
    run(gather_ffn, gather_low)
    finish(gather_low)
    gate_up = recut_join(gather_low.value)
    run(gather_ffn, gather_high)
    finish(gather_ffn)
    mine_ffn = gather_ffn.value
    swap = Task(other_core(mine_ffn))
    run(gather_down, swap, gather_high)
    finish(gather_high)
    gate_up = recut_join(gather_high.value, shards // 2, (gate_up,))
    hidden = gate_up.shape[1] // 2
    filled = ffn_forward(mine_ffn, gate_up, 0)
    other_ffn = swap.value
    run(gather_down)
    active, by_gate, by_up = ffn_forward(other_ffn, gate_up, 1, filled)
    theirs = product((active, 1), down_weight)
    finish(gather_down)
    mine_down = gather_down.value
    swap_z, swap = Task(other_core(theirs)), Task(other_core(mine_down))
    run(swap_z, swap)
    filled = ffn_backward(mine_down, down_weight, by_gate, by_up, 0)
    other_down = swap.value
    scatter_z = Task(direct_scatter(product((active, 0), down_weight, add=swap_z.value), 2))
    run(scatter_z)
    grad_both = ffn_backward(other_down, down_weight, by_gate, by_up, 1, (filled,))
    theirs = product((grad_both, 1), gate_up, NT)
    hold(theirs)
    swap = Task(other_core(theirs))
    run(scatter_z, swap)
    f_mine = product((grad_both, 0), gate_up, NT, add=swap.value)
    ready = after(grad_both, f_mine)
    gate_up_blocks = columns_product([mine_ffn, other_ffn], [(ready, 0), (ready, 1)], 2)
    finish(scatter_z)
    scatter_f = Task(direct_scatter(f_mine, 2))
    scatter_gate_up = Task(rep_scatter(gate_up_blocks))
    run(scatter_f, (scatter_gate_up, 1))
    down_blocks = rows_product([(active, 0), (active, 1)], [mine_down, other_down], 2)
    hold(*down_blocks[0])
    run(scatter_f, scatter_gate_up)
    finish(scatter_f)

    grad_middle, grad_branch, grad_beta, mixing_sum_next, static_sum_next = token_call(
        functools.partial(middle_back_kernel, line), tokens,
        [
            middle, packed_next, static[1], packed, static[0], w, branch, mixing_rows[1], mixing_mean[1],
            *scatter_z.value, *scatter_f.value,
        ],
        [
            shape((count, tokens, width), F32), shape((tokens, width), BF16), shape((tokens, LANES), F32),
            shape((LANES, width), F32), shape((8, LANES), F32),
        ],
    )
    gather_branch = Task(direct_gather(grad_branch, 2))
    run(gather_branch, scatter_gate_up)
    finish(scatter_gate_up)
    low = []
    recut_grad = Task(chip_exchange(jnp.concatenate(scatter_gate_up.value, axis=0), (line // 4, line // 4), low))
    (result,) = token_call(
        out_kernel, tokens, [tie(middle), packed_next, static[1], *scatter_z.value],
        [shape((tokens, count, width), BF16)],
    )
    scatter_down = Task(rep_scatter(down_blocks, True))
    run(gather_branch, scatter_down)
    hold(result)
    finish(gather_branch)
    mine_branch = gather_branch.value
    swap = Task(other_core(mine_branch))
    run(swap, recut_grad)
    grad_mine = product(mine_branch, output_weight, NT, into=0)
    other_branch = swap.value
    run(recut_grad, scatter_down)
    finish(scatter_down)
    gather_down_rows = Task(rep_gather(scatter_down.value, True))
    output_blocks = rows_product([(attended, 0), (attended, 1)], [mine_branch, other_branch], 2)
    hold(*output_blocks[0])
    grad_attended = product(other_branch, output_weight, NT, into=1, filled=(grad_mine,))
    grad_qkv = attention_back(qkv, rot_q, rot_k, grad_attended, logs, cosine, sine, place, start, heads)
    theirs = product((grad_qkv, 1), attention_weight, NT)
    gather_low = Task(rep_gather(stack_units(low[: shards // 2], 2), True))
    run(recut_grad, gather_down_rows, gather_low)
    hold(theirs)
    scatter_output = Task(rep_scatter(output_blocks, True))
    run(recut_grad, gather_down_rows)
    finish(recut_grad, gather_down_rows)
    qkv_blocks = columns_product([mine_in, other_in], [(grad_qkv, 0), (grad_qkv, 1)], 2)
    hold(*qkv_blocks[0])
    gather_high = Task(rep_gather(stack_units(low[shards // 2 :], 2), True))
    swap = Task(other_core(theirs))
    run(swap, scatter_output)
    scatter_a = Task(direct_scatter(product((grad_qkv, 0), attention_weight, NT, add=swap.value), 2))
    scatter_qkv = Task(rep_scatter(qkv_blocks, True))
    run(scatter_a, scatter_qkv)
    run(scatter_a, scatter_qkv, gather_low)
    finish(scatter_qkv, scatter_a, gather_low)
    recut_qkv_grad = Task(chip_exchange(jnp.concatenate(scatter_qkv.value, axis=0)))
    run(recut_qkv_grad, gather_high, scatter_output)
    finish(scatter_output)
    gather_output = Task(rep_gather(scatter_output.value, True))
    grad_streams, mixing_sum, static_sum = token_call(
        first_back_kernel, tokens,
        [x, packed, static[0], tie(grad_middle), grad_beta, mixing_rows[0], mixing_mean[0], *scatter_a.value],
        [shape((tokens, count, width), F32), shape((LANES, width), F32), shape((8, LANES), F32)],
    )
    run(recut_qkv_grad, gather_high)
    hold(grad_streams)
    finish(recut_qkv_grad, gather_high)
    gather_qkv_grad = Task(rep_gather(stack_units(recut_qkv_grad.value, 2), True))
    mixing_sums = jnp.stack([mixing_sum, mixing_sum_next])
    mixing_sums = (mixing_sums[:, :6] + mixing_sums[:, 8:14]).reshape(12, shards, -1)
    small = jnp.concatenate(
        [
            jnp.pad(mixing_sums.transpose(1, 0, 2), ((0, 0), (0, 4), (0, 0))),
            jnp.broadcast_to(jnp.concatenate([static_sum, static_sum_next])[None], (shards, 16, LANES)),
        ],
        axis=2,
    )
    sum_last = Task(sum_small(small))
    run(sum_last, gather_qkv_grad, gather_output)
    gate_rows, up_rows = columns_join([[tie(v) for v in u] for u in gather_low.value + gather_high.value], 2)
    down_rows = rows_join([[tie(v) for v in u] for u in gather_down_rows.value])
    run(sum_last, gather_qkv_grad)
    hold(gate_rows, down_rows)
    run(sum_last, gather_output)
    finish(gather_qkv_grad, sum_last, gather_output)
    output_rows = rows_join(gather_output.value)
    small = sum_last.value
    rows = width // shards
    own_mixing = jnp.swapaxes(small[:12, :rows].reshape(2, 6, rows), 1, 2)
    static_sums = jnp.stack([small[0:count, rows : rows + 6], small[8 : 8 + count, rows : rows + 6]])
    query_rows, key_rows, value_rows = columns_join(gather_qkv_grad.value, 3)
    return (
        result, grad_streams, query_rows, key_rows, value_rows, output_rows,
        gate_rows, up_rows, down_rows, own_mixing, static_sums,
    )


def solution(mesh):
    tokens = P(("rep", "shard"), None, None)
    rows = P("shard", None)
    return jax.shard_map(
        per_device,
        mesh=mesh,
        in_specs=(tokens, tokens, P("rep", None), P("rep", None)) + (rows,) * 7 + (P(None, "shard", None), P()),
        out_specs=(tokens, tokens) + (rows,) * 7 + (P(None, "shard", None), P()),
        check_vma=False,
    )
```

```python
import functools
import math

import jax
import jax.numpy as jnp
from jax import lax
from jax.experimental import pallas as pl
from jax.experimental.pallas import tpu as pltpu
from jax.sharding import PartitionSpec as P

HEADS = 16
EPSILON = 1e-05
NEGATIVE = -1e30
LANES = 128
LOG2E = 1.4426950408889634
F32 = jnp.float32
BF16 = jnp.bfloat16
NO_COST = pl.CostEstimate(flops=0, bytes_accessed=0, transcendentals=0)
NN = (((1,), (0,)), ((), ()))
NT = (((1,), (1,)), ((), ()))
TN = (((0,), (0,)), ((), ()))


def dot(a, b, dims=NN):
    return lax.dot_general(a, b, dims, preferred_element_type=F32)


def params(mib):
    return pltpu.CompilerParams(vmem_limit_bytes=mib << 20)


def after(value, *events):
    return lax.optimization_barrier((value, *events))[0] if events else value


def assemble_kernel(line, x_ref, *refs):
    rights, lefts, out_ref = refs[: line - 1], refs[line - 1 : -1], refs[-1]
    out_ref[0] = x_ref[...]
    for k in range(1, line):
        out_ref[k] = lefts[k - 1][...] + rights[line - k - 1][...]


class Task:
    def __init__(self, steps):
        self.steps, self.value, self.over, self.arrived = steps, None, False, []
        self.advance(None)

    def advance(self, arrived):
        self.arrived += arrived or []
        try:
            self.sends = list(self.steps.send(arrived))
            self.left = list(range(len(self.sends)))
            self.got = [None] * len(self.sends)
        except StopIteration as stop:
            self.value, self.over, self.left = stop.value, True, []


class Rounds:
    def __init__(self):
        self.base, self.fence, self.last = (), (), ()

    def hold(self, *values):
        self.fence += values

    def tie(self, value):
        return after(value, *self.fence)

    def run(self, *jobs):
        self.base, self.fence = self.fence, ()
        self.last = self.base
        self.send(jobs, self.base)

    def also(self, *jobs):
        self.last = self.send(jobs, self.base)

    def then(self, *jobs):
        self.last = self.send(jobs, self.last)

    def send(self, jobs, events):
        sends = []
        for job in jobs:
            task, pairs = job if isinstance(job, tuple) else (job, len(job.left))
            sends += [(task, i) for i in task.left[: 2 * pairs]]
        out = tuple(t.sends[i][0](after(t.sends[i][1], *events)) for t, i in sends)
        self.fence += out
        for (t, i), v in zip(sends, out):
            t.got[i] = v
            t.left.remove(i)
        for t in {id(t): t for t, _ in sends}.values():
            if not t.left:
                t.advance(t.got)
        return out

    def finish(self, *tasks):
        while any(not t.over for t in tasks):
            self.run(*tasks)


def sender(axis, pairs):
    return lambda x: lax.ppermute(x, axis, pairs)


def assemble_kernel(line, x_ref, *refs):
    rights, lefts, out_ref = refs[: line - 1], refs[line - 1 : -1], refs[-1]
    out_ref[0] = x_ref[...]
    for k in range(1, line):
        out_ref[k] = lefts[k - 1][...] + rights[line - k - 1][...]


def line_gather(x):
    line = lax.axis_size("shard") // 2
    right = left = x
    rights, lefts = [], []
    for step in range(line - 1):
        right, left = yield [
            (sender("shard", [(2 * p + c, 2 * p + 2 + c) for p in range(step, line - 1) for c in range(2)]), right),
            (sender("shard", [(2 * p + c, 2 * p - 2 + c) for p in range(1, line - step) for c in range(2)]), left),
        ]
        rights.append(right)
        lefts.append(left)
    rows, width = x.shape
    (mine,) = token_call(
        functools.partial(assemble_kernel, line), rows, [x, *rights, *lefts],
        [jax.ShapeDtypeStruct((line, rows, width), x.dtype)], block=rows // 2 if rows % 32 == 0 else rows,
    )
    return mine.reshape(line * rows, width)


def other_core(x):
    size = lax.axis_size("shard")
    (other,) = yield [(sender("shard", [(i, i ^ 1) for i in range(size)]), x)]
    return other


def line_shift(k):
    line = lax.axis_size("shard") // 2
    return sender("shard", [(2 * p + c, 2 * ((p + k) % line) + c) for p in range(line) for c in range(2)])


def shifts(line, steps):
    return [list(range(1, line))] if steps == 1 else [list(range(1, line, 2)), list(range(2, line, 2))]


def direct_gather(x, steps=1):
    line = lax.axis_size("shard") // 2
    came = {}
    for step in shifts(line, steps):
        came |= dict(zip(step, (yield [(line_shift(k), x) for k in step])))
    return jnp.concatenate([x] + [came[line - q] for q in range(1, line)], axis=0)


def direct_scatter(rows, steps=1):
    line = lax.axis_size("shard") // 2
    parts = list(rows.reshape(line, rows.shape[0] // line, -1))
    came = [parts[0]]
    for step in shifts(line, steps):
        came += yield [(line_shift(k), parts[k]) for k in step]
    return came


def rep_sender(bit):
    return sender("rep", [(i, i ^ (1 << bit)) for i in range(lax.axis_size("rep"))])


def rep_orders(units):
    bits = list(range(lax.axis_size("rep").bit_length() - 1))
    return [bits] * (units // 2) + [bits[::-1]] * (units - units // 2)


def paired(sends):
    middle = len(sends) // 2
    return [v for pair in zip(sends[:middle], sends[middle:]) for v in pair]


def rep_scatter(units, merge=False):
    orders = rep_orders(len(units))
    units = [dict(enumerate(u)) for u in units]
    for i in range(len(orders[0])):
        bits = [1 << o[i] for o in orders]
        keys = [[m for m in unit if m & bit] for unit, bit in zip(units, bits)]
        came = yield from exchange_blocks(units, keys, [o[i] for o in orders], merge)
        units = [
            {m ^ bit: unit[m ^ bit] + v for m, v in zip(key, new)}
            for unit, bit, key, new in zip(units, bits, keys, came)
        ]
    return [u[0] for u in units]


def rep_gather(units, merge=False):
    orders = [o[::-1] for o in rep_orders(len(units))]
    units = [{0: u} for u in units]
    for i in range(len(orders[0])):
        keys = [list(unit) for unit in units]
        came = yield from exchange_blocks(units, keys, [o[i] for o in orders], merge)
        for unit, o, key, new in zip(units, orders, keys, came):
            unit |= {m ^ (1 << o[i]): v for m, v in zip(key, new)}
    return [[u[m] for m in range(len(u))] for u in units]


def rep_flip(m):
    return sender("rep", [(i, i ^ m) for i in range(lax.axis_size("rep"))])


def rep_scatter_direct(blocks):
    came = yield [(rep_flip(m), blocks[m]) for m in range(1, len(blocks))]
    return sum(v.astype(F32) for v in [blocks[0], *came]).astype(blocks[0].dtype)


def rep_gather_direct(block):
    came = yield [(rep_flip(m), block) for m in range(1, lax.axis_size("rep"))]
    return [block, *came]


def exchange_blocks(units, keys, bits, merge):
    if merge:
        came = yield [
            (rep_sender(bit), jnp.concatenate([unit[m] for m in key]) if len(key) > 1 else unit[key[0]])
            for unit, key, bit in paired(list(zip(units, keys, bits)))
        ]
        order = paired(list(range(len(units))))
        return [cut_units(came[order.index(u)], len(keys[u])) for u in range(len(units))]
    flat = paired([(u, m) for u, key in enumerate(keys) for m in key])
    came = yield [(rep_sender(bits[u]), units[u][m]) for u, m in flat]
    came = dict(zip(flat, came))
    return [[came[u, m] for m in key] for u, key in enumerate(keys)]


def chip_exchange(x, counts=(), out=None, split=None):
    shards = lax.axis_size("shard")
    me = lax.axis_index("shard")
    pick = lambda k: lax.dynamic_index_in_dim(x, me ^ k, 0, keepdims=False)
    (came,) = yield [
        (sender("shard", [(i, i ^ 1) for i in range(shards)]), jnp.stack([pick(k) for k in range(1, shards, 2)]))
    ]
    out, counts = [] if out is None else out, list(counts)
    blocks = {0: pick(0), 1: came[0]}
    left = []
    for q in range(1, shards // 2):
        if split is None or q < split:
            left.append(((2 * q, 2 * q + 1), jnp.stack([pick(2 * q), came[q]])))
        else:
            left += [((2 * q + 1,), came[q]), ((2 * q,), pick(2 * q))]
    while left:
        amount = counts.pop(0) if counts else len(left)
        step, left = left[:amount], left[amount:]
        arrived = yield [
            (sender("shard", [(i, i ^ (keys[0] & ~1)) for i in range(shards)]), v) for keys, v in step
        ]
        for (keys, _), v in zip(step, arrived):
            blocks |= {k: v[f] for f, k in enumerate(keys)} if len(keys) > 1 else {keys[0]: v}
        out[:] = [blocks[k] for k in range(shards) if all(i in blocks for i in range(k + 1))]
    return out


def stack_units(blocks, count):
    size = len(blocks) // count
    return [jnp.stack(blocks[i * size : (i + 1) * size]) for i in range(count)]


def to_tokens(x):
    shards = lax.axis_size("shard")
    line = shards // 2
    (came,) = yield [(sender("shard", [(i, i ^ 1) for i in range(shards)]), x[1])]
    held = jnp.stack([x[0], came], axis=1)
    came = yield [
        (sender("shard", [(2 * p + c, 2 * ((p + k) % line) + c) for p in range(line) for c in range(2)]), held[k])
        for k in range(1, line)
    ]
    came = [held[0], *came]
    return [jnp.concatenate([came[(line - q) % line][f] for q in range(line)], axis=1) for f in range(2)]


def cut_units(x, count):
    size = x.shape[0] // count
    return [x[i * size : (i + 1) * size] for i in range(count)]


def recut_piece(weights):
    shards, reps = lax.axis_size("shard"), lax.axis_size("rep")
    part = weights[0].shape[0] // reps
    start = lax.axis_index("rep") * part
    pieces = [
        lax.dynamic_slice_in_dim(w, start, part, 0).reshape(part, shards, -1).transpose(1, 0, 2) for w in weights
    ]
    return jnp.concatenate(pieces, axis=2)


def halves(x):
    return cut_units(x, 2)


def unit_specs(units):
    size = units[0][0].shape[0]
    return [
        pl.BlockSpec((1,) + v.shape[1:], lambda k, me, g=g: (jnp.clip(k - g * size, 0, size - 1), 0, 0))
        for g, u in enumerate(units) for v in u
    ]


def columns_kernel(units, reps, parts, me_ref, *refs):
    outs = refs[-parts:]
    size = pl.num_programs(0) // units
    part = refs[0].shape[1]
    for g in range(units):
        @pl.when(pl.program_id(0) // size == g)
        def _(chosen=refs[g * reps : (g + 1) * reps]):
            for m in range(reps):
                row = pl.multiple_of((me_ref[0] ^ m) * part, part)
                for i, out_ref in enumerate(outs):
                    width = out_ref.shape[1]
                    out_ref[pl.ds(row, part), :] = chosen[m][0, :, i * width : (i + 1) * width].astype(out_ref.dtype)


def join(units, parts, spec, shapes, filled=(), mib=32):
    reps = lax.axis_size("rep")
    operands = [v for u in units for v in u]
    return pl.pallas_call(
        functools.partial(columns_kernel, len(units), reps, parts),
        grid_spec=pltpu.PrefetchScalarGridSpec(
            num_scalar_prefetch=1,
            grid=(len(units) * units[0][0].shape[0],),
            in_specs=unit_specs(units) + [pl.BlockSpec(memory_space=pl.ANY)] * len(filled),
            out_specs=[spec] * parts,
        ),
        out_shape=shapes,
        input_output_aliases={1 + len(operands) + i: i for i in range(len(filled))},
        compiler_params=params(mib),
        cost_estimate=NO_COST,
    )(jnp.stack([lax.axis_index("rep"), lax.axis_index("shard")]).astype(jnp.int32), *operands, *filled)


def recut_join(units, first=0, filled=()):
    shards, reps = lax.axis_size("shard"), lax.axis_size("rep")
    _, part, columns = units[0][0].shape
    rows = part * reps
    return join(
        units, 1, pl.BlockSpec((rows, columns), lambda k, me: ((k + first) ^ me[1], 0)),
        [jax.ShapeDtypeStruct((shards * rows, columns), BF16)], filled,
    )[0]


def rows_in_order(units):
    blocks, part, columns = units[0][0].shape
    rows = part * lax.axis_size("rep")
    return join(
        units, 1, pl.BlockSpec((rows, columns), lambda k, me: (k, 0)),
        [jax.ShapeDtypeStruct((len(units) * blocks * rows, columns), BF16)],
    )[0]


def columns_join(units, parts):
    shards, reps = lax.axis_size("shard"), lax.axis_size("rep")
    _, part, columns = units[0][0].shape
    rows, width = part * reps, columns // parts
    return join(
        units, parts, pl.BlockSpec((rows, width), lambda k, me: (0, k ^ me[1])),
        [jax.ShapeDtypeStruct((rows, shards * width), F32)] * parts, mib=56 if parts == 2 else 32,
    )


def rows_kernel(units, reps, me_ref, *refs):
    out_ref = refs[-1]
    part = refs[0].shape[0]
    for u in range(units):
        for m in range(reps):
            row = pl.multiple_of((me_ref[0] ^ m) * (units * part) + u * part, part)
            out_ref[pl.ds(row, part), :] = refs[u * reps + m][...].astype(F32)


def rows_join(units):
    reps = lax.axis_size("rep")
    operands = [v for u in units for v in u]
    part, columns = operands[0].shape
    block = 512 if columns % 512 == 0 else columns
    return pl.pallas_call(
        functools.partial(rows_kernel, len(units), reps),
        grid_spec=pltpu.PrefetchScalarGridSpec(
            num_scalar_prefetch=1,
            grid=(columns // block,),
            in_specs=[pl.BlockSpec((part, block), lambda j, me: (0, j))] * len(operands),
            out_specs=pl.BlockSpec((part * len(operands), block), lambda j, me: (0, j)),
        ),
        out_shape=jax.ShapeDtypeStruct((part * len(operands), columns), F32),
        compiler_params=params(32),
        cost_estimate=NO_COST,
    )(lax.axis_index("rep").astype(jnp.int32)[None], *operands)


def mixing_kernel(me_ref, *refs):
    out_ref = refs[-1]
    out_ref[...] = jnp.zeros_like(out_ref)
    width = refs[0].shape[2]
    for k, ref in enumerate(refs[:-1]):
        start = pl.multiple_of((me_ref[0] ^ k) * width, width)
        out_ref[:, : ref.shape[1], pl.ds(start, width)] = ref[...]


def mixing_gather(weight):
    shards = lax.axis_size("shard")
    piece = jnp.pad(jnp.swapaxes(weight, 1, 2), ((0, 0), (0, 2), (0, 0)))
    piece = jnp.concatenate([piece, piece], axis=1)
    (came,) = yield [(sender("shard", [(i, i ^ 1) for i in range(shards)]), piece)]
    held = jnp.stack([piece, came])
    came = yield [
        (sender("shard", [(i, i ^ (2 * q)) for i in range(shards)]), held) for q in range(1, shards // 2)
    ]
    came = [v[f] for v in [held, *came] for f in range(2)]
    return pl.pallas_call(
        mixing_kernel,
        grid_spec=pltpu.PrefetchScalarGridSpec(
            num_scalar_prefetch=1,
            grid=(1,),
            in_specs=[pl.BlockSpec(piece.shape, lambda i, me: (0, 0, 0))] * shards,
            out_specs=pl.BlockSpec((2, LANES, shards * piece.shape[2]), lambda i, me: (0, 0, 0)),
        ),
        out_shape=jax.ShapeDtypeStruct((2, LANES, shards * piece.shape[2]), BF16),
        compiler_params=params(32),
    )(lax.axis_index("shard").astype(jnp.int32)[None], *came)


def sum_small(blocks):
    shards, reps = lax.axis_size("shard"), lax.axis_size("rep")
    me = lax.axis_index("shard")
    blocks = blocks.reshape((shards // 2, 2) + blocks.shape[1:])
    pick = lambda f: lax.dynamic_index_in_dim(blocks, (me % 2) ^ f, 1, keepdims=False)
    (came,) = yield [(sender("shard", [(i, i ^ 1) for i in range(shards)]), pick(1))]
    pair = pick(0) + came
    take = lambda q: lax.dynamic_index_in_dim(pair, (me // 2) ^ q, 0, keepdims=False)
    total = take(0)
    came = yield [
        (sender("shard", [(i, i ^ (2 * q)) for i in range(shards)]), take(q)) for q in range(1, shards // 2)
    ]
    for v in came:
        total = total + v
    came = yield [(sender("rep", [(i, i ^ k) for i in range(reps)]), total) for k in range(1, reps)]
    terms = [total, *came]
    while len(terms) > 1:
        terms = [a + b for a, b in zip(terms[::2], terms[1::2])]
    return terms[0]


def lane(shape):
    return lax.broadcasted_iota(jnp.int32, shape, len(shape) - 1)


def column(values, index):
    return values[:, index : index + 1]


def split(values):
    high = values.astype(BF16)
    return high, (values - high.astype(F32)).astype(BF16)


def moments(values):
    mean = jnp.mean(values, axis=-1, keepdims=True)
    centred = values - mean
    spread = jnp.mean(centred * centred, axis=-1, keepdims=True)
    return mean, centred, lax.rsqrt(spread + EPSILON)


def mix_forward(streams, weight, static):
    count = len(streams)
    rows = streams[0].shape[0]
    stats = [moments(y) for y in streams]
    parts = [split(centred) for _, centred, _ in stats]
    raw = dot(jnp.concatenate([p[0] for p in parts] + [p[1] for p in parts], axis=0), weight, NT)
    at = lane((rows, LANES))
    pres, coefficients = [], []
    for i in range(count):
        pre = (raw[i * rows : (i + 1) * rows] + raw[(count + i) * rows : (count + i + 1) * rows]) * stats[i][2]
        pres.append(pre)
        coefficients.append(static[i : i + 1] + jnp.tanh(pre))
    entering = sum(column(c, 0) * y for c, y in zip(coefficients, streams))
    mean, centred, scale = moments(entering)
    packed = []
    for i in range(count):
        value = jnp.where(at < 6, pres[i], 0.0)
        value = jnp.where(at == 6, stats[i][0], jnp.where(at == 7, stats[i][2], value))
        packed.append(jnp.where(at == 8, mean, jnp.where(at == 9, scale, value)))
    return centred * scale, coefficients, packed


def mix_carry(streams, coefficients, j):
    return sum(column(c, 1 + j) * y for c, y in zip(coefficients, streams))


def mix_backward(streams, packed, static, grad_entering, grad_carried, grad_beta, weight_rows, weight_mean):
    count = len(streams)
    rows, width = streams[0].shape
    at = lane((rows, LANES))
    tanhs = [jnp.where(at < 6, jnp.tanh(p), 0.0) for p in packed]
    coefficients = [static[i : i + 1] + tanhs[i] for i in range(count)]
    mean, scale = column(packed[0], 8), column(packed[0], 9)
    entering = (sum(column(c, 0) * y for c, y in zip(coefficients, streams)) - mean) * scale
    inner = jnp.mean(grad_entering * entering, axis=-1, keepdims=True)
    outer = jnp.mean(grad_entering, axis=-1, keepdims=True)
    grad_sum = scale * (grad_entering - outer - entering * inner)
    grads, both, normed, scalars = [], [], [], []
    for i in range(count):
        y = streams[i]
        value = jnp.where(at == 0, jnp.sum(grad_sum * y, axis=-1, keepdims=True), 0.0)
        for j in range(count):
            value = jnp.where(at == 1 + j, jnp.sum(grad_carried[j] * y, axis=-1, keepdims=True), value)
        value = jnp.where(at == 1 + count, grad_beta[i], value)
        grad_pre = value * (1.0 - tanhs[i] * tanhs[i])
        high = grad_pre.astype(BF16).astype(F32)
        low = grad_pre - high
        both.append((high + pltpu.roll(low, 8, 1)).astype(BF16))
        grads.append(value)
        normed.append((y - column(packed[i], 6)) * column(packed[i], 7))
        scalars.append((
            jnp.sum(grad_pre * weight_mean, axis=-1, keepdims=True),
            jnp.sum(jnp.where(at < 6, grad_pre * packed[i], 0.0), axis=-1, keepdims=True) / width,
        ))
    both = jnp.concatenate(both, axis=0)
    grad_normed = dot(both, weight_rows)
    mixing_sum = dot(both, jnp.concatenate([n.astype(BF16) for n in normed], axis=0), TN)
    out = []
    for i in range(count):
        value = column(coefficients[i], 0) * grad_sum
        for j in range(count):
            value = value + column(coefficients[i], 1 + j) * grad_carried[j]
        a, b = scalars[i]
        out.append(
            value + column(packed[i], 7) * (grad_normed[i * rows : (i + 1) * rows] - a - normed[i] * b)
        )
    return out, mixing_sum, grads


def load_streams(ref):
    return [ref[i].astype(F32) for i in range(ref.shape[0])]


def coefficients_of(packed, static):
    return [static[i : i + 1] + jnp.tanh(packed[i]) for i in range(len(packed))]


def first_kernel(x_ref, weight_ref, static_ref, entering_ref, packed_ref, turned_ref):
    streams = [x_ref[:, i, :] for i in range(x_ref.shape[1])]
    for i, stream in enumerate(streams):
        turned_ref[i] = stream
    entering, _, packed = mix_forward([v.astype(F32) for v in streams], weight_ref[...], static_ref[...])
    entering_ref[...] = entering.astype(BF16)
    for i, value in enumerate(packed):
        packed_ref[i] = value


def middle_kernel(
    x_ref, packed_ref, static_ref, branch_ref, w_ref, weight_ref, static_next_ref,
    m_ref, entering_ref, down_ref, packed_next_ref,
):
    streams = load_streams(x_ref)
    count = len(streams)
    coefficients = coefficients_of([packed_ref[i] for i in range(count)], static_ref[...])
    branch = branch_ref[...]
    middle = []
    for j in range(count):
        middle.append(mix_carry(streams, coefficients, j) + column(coefficients[j], 5) * branch)
        m_ref[j] = middle[j]
    entering, following, packed = mix_forward(middle, weight_ref[...], static_next_ref[...])
    entering_ref[...] = entering.astype(BF16)
    for i, value in enumerate(packed):
        packed_next_ref[i] = value
    down_ref[...] = sum(column(following[j], 5) * w_ref[j].astype(F32) for j in range(count)).astype(BF16)


def total(refs):
    return sum(ref[...].astype(F32) for ref in refs)


def out_kernel(m_ref, packed_ref, static_ref, *refs):
    out_ref = refs[-1]
    streams = load_streams(m_ref)
    count = len(streams)
    coefficients = coefficients_of([packed_ref[i] for i in range(count)], static_ref[...])
    z = total(refs[:-1])
    for j in range(count):
        out_ref[:, j, :] = (mix_carry(streams, coefficients, j) + column(coefficients[j], 5) * z).astype(BF16)


def accumulate(step, mixing_ref, static_ref, mixing_sum, grads):
    @pl.when(step == 0)
    def _():
        mixing_ref[...] = jnp.zeros_like(mixing_ref)
        static_ref[...] = jnp.zeros_like(static_ref)

    mixing_ref[...] += mixing_sum
    at = lax.broadcasted_iota(jnp.int32, static_ref.shape, 0)
    sums = jnp.zeros(static_ref.shape, F32)
    for i, grad in enumerate(grads):
        sums = jnp.where(at == i, jnp.sum(grad, axis=0, keepdims=True), sums)
    static_ref[...] += sums


def middle_back_kernel(
    terms, m_ref, packed_ref, static_ref, packed_first_ref, static_first_ref, w_ref, branch_ref,
    weight_rows_ref, weight_mean_ref, *refs,
):
    grad_m_ref, grad_branch_ref, grad_beta_ref, mixing_ref, static_sum_ref = refs[2 * terms :]
    streams = load_streams(m_ref)
    count = len(streams)
    cotangent = load_streams(w_ref)
    z = total(refs[:terms])
    grad_entering = total(refs[terms : 2 * terms])
    grad_beta = [jnp.sum(w * z, axis=-1, keepdims=True) for w in cotangent]
    grads, mixing_sum, grad_pres = mix_backward(
        streams, [packed_ref[i] for i in range(count)], static_ref[...], grad_entering, cotangent, grad_beta,
        weight_rows_ref[...], weight_mean_ref[...],
    )
    accumulate(pl.program_id(0), mixing_ref, static_sum_ref, mixing_sum, grad_pres)
    first = coefficients_of([packed_first_ref[i] for i in range(count)], static_first_ref[...])
    branch = branch_ref[...]
    at = lane(grad_beta_ref.shape)
    beta = jnp.zeros(grad_beta_ref.shape, F32)
    for j in range(count):
        grad_m_ref[j] = grads[j]
        beta = jnp.where(at == j, jnp.sum(grads[j] * branch, axis=-1, keepdims=True), beta)
    grad_beta_ref[...] = beta
    grad_branch_ref[...] = sum(column(first[j], 5) * grads[j] for j in range(count)).astype(BF16)


def first_back_kernel(
    x_ref, packed_ref, static_ref, grad_m_ref, grad_beta_ref, weight_rows_ref, weight_mean_ref, *refs
):
    grad_ref, mixing_ref, static_sum_ref = refs[-3:]
    streams = load_streams(x_ref)
    count = len(streams)
    grad_entering = total(refs[:-3])
    beta = grad_beta_ref[...]
    grads, mixing_sum, grad_pres = mix_backward(
        streams, [packed_ref[i] for i in range(count)], static_ref[...], grad_entering,
        [grad_m_ref[i] for i in range(count)], [column(beta, i) for i in range(count)],
        weight_rows_ref[...], weight_mean_ref[...],
    )
    accumulate(pl.program_id(0), mixing_ref, static_sum_ref, mixing_sum, grad_pres)
    for i in range(count):
        grad_ref[:, i, :] = grads[i]


def token_call(kernel, tokens, operands, outputs, block=None, mib=40):
    block = block or (32 if tokens % 32 == 0 else tokens)

    def spec(shape):
        if tokens not in shape[:-1]:
            return pl.BlockSpec(shape, lambda i, n=len(shape): (0,) * n)
        axis = shape.index(tokens)
        cut = tuple(block if d == axis else s for d, s in enumerate(shape))
        return pl.BlockSpec(cut, lambda i, axis=axis, n=len(shape): tuple(i if d == axis else 0 for d in range(n)))

    size = sum(math.prod(o.shape) * o.dtype.itemsize for o in list(operands) + list(outputs))
    return pl.pallas_call(
        kernel,
        grid=(tokens // block,),
        in_specs=[spec(o.shape) for o in operands],
        out_specs=[spec(o.shape) for o in outputs],
        out_shape=list(outputs),
        compiler_params=params(mib),
        cost_estimate=NO_COST,
    )(*operands)


def rows_of(operand):
    return operand[0].shape[0] // 2 if isinstance(operand, tuple) else operand.shape[0]


def whole_of(operand):
    return operand[0] if isinstance(operand, tuple) else operand


def half_of(operand):
    return operand[1] if isinstance(operand, tuple) else 0


def tile_of(size):
    return next((t for t in (512, 384, 256, 128) if size % t == 0), size)


def product_kernel(dims, added, a_ref, b_ref, *refs):
    out = dot(a_ref[...], b_ref[...], dims)
    if added:
        out = out + refs[0][...].astype(F32)
    refs[-1][...] = out.astype(refs[-1].dtype)


def product(a, b, dims=NN, add=None, into=None, filled=()):
    rows, depth = rows_of(a), whole_of(a).shape[1]
    half, columns = half_of(a), b.shape[0] if dims == NT else b.shape[1]
    tile = tile_of(columns)
    operands = [whole_of(a), b] + ([] if add is None else [add]) + list(filled)
    specs = [
        pl.BlockSpec((rows, depth), lambda j: (half, 0)),
        pl.BlockSpec((tile, depth), lambda j: (j, 0)) if dims == NT else pl.BlockSpec((depth, tile), lambda j: (0, j)),
    ]
    if add is not None:
        specs.append(pl.BlockSpec((rows, tile), lambda j: (0, j)))
    specs += [pl.BlockSpec(memory_space=pl.ANY)] * len(filled)
    at = into or 0
    return pl.pallas_call(
        functools.partial(product_kernel, dims, add is not None),
        grid=(columns // tile,),
        in_specs=specs,
        out_specs=pl.BlockSpec((rows, tile), lambda j: (at, j)),
        out_shape=jax.ShapeDtypeStruct((rows if into is None else 2 * rows, columns), BF16),
        input_output_aliases={len(operands) - 1: 0} if filled else {},
        compiler_params=params(40),
        cost_estimate=NO_COST,
    )(*operands)


def columns_product_kernel(units, reps, me_ref, x0, x1, y0, y1, *refs):
    outs, sums = refs[:-1], refs[-1]
    sums[...] = dot(x0[...], y0[...], TN) + dot(x1[...], y1[...], TN)
    step = pl.program_id(0)
    size = pl.num_programs(0) // units
    part = sums.shape[0] // reps
    for u in range(units):
        @pl.when(step // size == u)
        def _(u=u):
            for m in range(reps):
                row = pl.multiple_of((me_ref[0] ^ m) * part, part)
                outs[u * reps + m][0] = sums[pl.ds(row, part), :].astype(BF16)


def columns_product(xs, ys, units):
    shards, reps = lax.axis_size("shard"), lax.axis_size("rep")
    tokens, columns = rows_of(ys[0]), whole_of(ys[0]).shape[1]
    rows = whole_of(xs[0]).shape[1] // shards
    size, part = shards // units, rows // reps
    x_specs = [pl.BlockSpec((tokens, rows), lambda s, me, h=half_of(x): (h, s)) for x in xs]
    y_specs = [pl.BlockSpec((tokens, columns), lambda s, me, h=half_of(y): (h, 0)) for y in ys]
    out = pl.pallas_call(
        functools.partial(columns_product_kernel, units, reps),
        grid_spec=pltpu.PrefetchScalarGridSpec(
            num_scalar_prefetch=1,
            grid=(shards,),
            in_specs=x_specs + y_specs,
            out_specs=[
                pl.BlockSpec((1, part, columns), lambda s, me, u=u: (jnp.clip(s - u * size, 0, size - 1), 0, 0))
                for u in range(units) for _ in range(reps)
            ],
            scratch_shapes=[pltpu.VMEM((rows, columns), F32)],
        ),
        out_shape=[jax.ShapeDtypeStruct((size, part, columns), BF16)] * (units * reps),
        compiler_params=params(48),
        cost_estimate=NO_COST,
    )(lax.axis_index("rep").astype(jnp.int32)[None], *[whole_of(v) for v in [*xs, *ys]])
    return [out[u * reps : (u + 1) * reps] for u in range(units)]


def rows_product_kernel(units, reps, me_ref, x0, x1, y0, y1, *refs):
    outs, sums = refs[:-1], refs[-1]
    sums[...] = dot(x0[...], y0[...], TN) + dot(x1[...], y1[...], TN)
    part = outs[0].shape[0]
    for u in range(units):
        for m in range(reps):
            row = pl.multiple_of((me_ref[0] ^ m) * (units * part) + u * part, part)
            outs[u * reps + m][...] = sums[pl.ds(row, part), :].astype(BF16)


def rows_product(xs, ys, units):
    reps = lax.axis_size("rep")
    tokens, columns = rows_of(ys[0]), whole_of(ys[0]).shape[1]
    rows = whole_of(xs[0]).shape[1]
    part, tile = rows // (units * reps), tile_of(columns)
    x_specs = [pl.BlockSpec((tokens, rows), lambda j, me, h=half_of(x): (h, 0)) for x in xs]
    y_specs = [pl.BlockSpec((tokens, tile), lambda j, me, h=half_of(y): (h, j)) for y in ys]
    out = pl.pallas_call(
        functools.partial(rows_product_kernel, units, reps),
        grid_spec=pltpu.PrefetchScalarGridSpec(
            num_scalar_prefetch=1,
            grid=(columns // tile,),
            in_specs=x_specs + y_specs,
            out_specs=[pl.BlockSpec((part, tile), lambda j, me: (0, j))] * (units * reps),
            scratch_shapes=[pltpu.VMEM((rows, tile), F32)],
        ),
        out_shape=[jax.ShapeDtypeStruct((part, columns), BF16)] * (units * reps),
        compiler_params=params(48),
        cost_estimate=NO_COST,
    )(lax.axis_index("rep").astype(jnp.int32)[None], *[whole_of(v) for v in [*xs, *ys]])
    return [out[u * reps : (u + 1) * reps] for u in range(units)]


def ffn_tile(hidden):
    return 256 if hidden % 256 == 0 else hidden


def chunks(rows):
    step = 320 if rows % 320 == 0 else rows
    return [slice(i, i + step) for i in range(0, rows, step)]


def ffn_kernel(x_ref, gate_ref, up_ref, *refs):
    active_ref, by_gate_ref, by_up_ref = refs[-3:]
    for cut in chunks(x_ref.shape[0]):
        gate = dot(x_ref[cut, :], gate_ref[...])
        up = dot(x_ref[cut, :], up_ref[...])
        sigmoid = 1.0 / (1.0 + jnp.exp2(gate * -LOG2E))
        swish = gate * sigmoid
        active_ref[cut, :] = (swish * up).astype(BF16)
        by_gate_ref[cut, :] = (up * sigmoid * (1.0 + gate - swish)).astype(BF16)
        by_up_ref[cut, :] = swish.astype(BF16)


def ffn_forward(x, weight, half, filled=()):
    rows, width = x.shape
    hidden = weight.shape[1] // 2
    tile = ffn_tile(hidden)
    tiles = hidden // tile
    return pl.pallas_call(
        ffn_kernel,
        grid=(tiles,),
        in_specs=[
            pl.BlockSpec((rows, width), lambda j: (0, 0)),
            pl.BlockSpec((width, tile), lambda j: (0, j)),
            pl.BlockSpec((width, tile), lambda j: (0, j + tiles)),
        ] + [pl.BlockSpec(memory_space=pl.ANY)] * len(filled),
        out_specs=[pl.BlockSpec((rows, tile), lambda j: (half, j))] * 3,
        out_shape=[jax.ShapeDtypeStruct((2 * rows, hidden), BF16)] * 3,
        input_output_aliases={3 + i: i for i in range(len(filled))},
        compiler_params=params(40),
        cost_estimate=NO_COST,
    )(x, weight, weight, *filled)


def ffn_back_kernel(tiles, x_ref, down_ref, by_gate_ref, by_up_ref, *refs):
    out_ref = refs[-1]
    step = pl.program_id(0)
    tile = down_ref.shape[0]
    for cut in chunks(x_ref.shape[0]):
        grad = dot(x_ref[cut, :], down_ref[...], NT)
        first = pl.multiple_of(step * tile, tile)
        second = pl.multiple_of((step + tiles) * tile, tile)
        out_ref[cut, pl.ds(first, tile)] = (grad * by_gate_ref[cut, :].astype(F32)).astype(BF16)
        out_ref[cut, pl.ds(second, tile)] = (grad * by_up_ref[cut, :].astype(F32)).astype(BF16)


def ffn_backward(x, down, by_gate, by_up, half, filled=()):
    rows, width = x.shape
    hidden = down.shape[0]
    tile = ffn_tile(hidden)
    tiles = hidden // tile
    return pl.pallas_call(
        functools.partial(ffn_back_kernel, tiles),
        grid=(tiles,),
        in_specs=[
            pl.BlockSpec((rows, width), lambda j: (0, 0)),
            pl.BlockSpec((tile, width), lambda j: (j, 0)),
            pl.BlockSpec((rows, tile), lambda j: (half, j)),
            pl.BlockSpec((rows, tile), lambda j: (half, j)),
        ] + [pl.BlockSpec(memory_space=pl.ANY)] * len(filled),
        out_specs=pl.BlockSpec((rows, 2 * hidden), lambda j: (half, 0)),
        out_shape=jax.ShapeDtypeStruct((2 * rows, 2 * hidden), BF16),
        input_output_aliases={4 + i: i for i in range(len(filled))},
        compiler_params=params(40),
        cost_estimate=NO_COST,
    )(x, down, by_gate, by_up, *filled)


def turn(values):
    return pltpu.roll(values, values.shape[-1] // 2, 1)


def allowed(places, query_place, query_start):
    return (places <= query_place) & (places >= query_start)


def key_chunks(tokens):
    step = 128 if tokens % 128 == 0 else tokens
    return [slice(i, i + step) for i in range(0, tokens, step)]


def attend_kernel(
    heads, width, q_ref, k_ref, v_ref, cos_q, sin_q, cos_k, sin_k, key_place, query_place, query_start,
    out_ref, rot_q_ref, rot_k_ref, log_ref, value_t, scores, weights,
):
    scale = width ** (-0.5)

    @pl.when(pl.program_id(0) == 0)
    def _():
        for h in range(heads):
            cut = slice(h * width, (h + 1) * width)
            key = k_ref[:, cut].astype(F32)
            rot_k_ref[:, cut] = (key * cos_k[...] + turn(key) * sin_k[...]).astype(BF16)
            value_t[cut, :] = v_ref[:, cut].T

    chunks_here = key_chunks(k_ref.shape[0])
    tops = []
    for h in range(heads):
        cut = slice(h * width, (h + 1) * width)
        query = q_ref[:, cut].astype(F32)
        query = (query * cos_q[...] + turn(query) * sin_q[...]).astype(BF16)
        rot_q_ref[:, cut] = query
        tops.append(jnp.full((8, query.shape[0]), NEGATIVE, F32))
        scores[h] = dot(rot_k_ref[:, cut], query, NT)
    for keys in chunks_here:
        mask = allowed(key_place[keys, :], query_place[...], query_start[...])
        for h in range(heads):
            part = jnp.where(mask, scores[h, keys, :], NEGATIVE)
            scores[h, keys, :] = part
            tops[h] = jnp.maximum(tops[h], jnp.max(part.reshape(-1, 8, part.shape[1]), axis=0))
    for h in range(heads):
        cut = slice(h * width, (h + 1) * width)
        top = jnp.max(tops[h], axis=0, keepdims=True) * (scale * LOG2E)
        total = jnp.zeros((8, top.shape[1]), F32)
        for keys in chunks_here:
            part = jnp.exp2(scores[h, keys, :] * (scale * LOG2E) - top)
            total = total + jnp.sum(part.reshape(-1, 8, part.shape[1]), axis=0)
            weights[keys, :] = part.astype(BF16)
        total = jnp.sum(total, axis=0, keepdims=True)
        out_ref[:, cut] = (dot(value_t[cut, :], weights[...]) * (1.0 / total)).T.astype(BF16)
        log_ref[h : h + 1] = top + jnp.log2(total)


def attend_back_kernel(
    heads, width, q_ref, k_ref, v_ref, out_rows_ref, grad_ref, log_ref, cos_q, sin_q, cos_k, sin_k, key_place,
    query_place, query_start, out_ref, key_t, sum_k, sum_v, scores, grads, low_weights, low_grads,
):
    scale = width ** (-0.5)
    step = pl.program_id(0)
    block = q_ref.shape[0]
    here = pl.ds(pl.multiple_of(step * block, block), block)

    @pl.when(step == 0)
    def _():
        for h in range(heads):
            cut = slice(h * width, (h + 1) * width)
            key_t[cut, :] = k_ref[:, cut].T
        sum_k[...] = jnp.zeros_like(sum_k)
        sum_v[...] = jnp.zeros_like(sum_v)

    for h in range(heads):
        cut = slice(h * width, (h + 1) * width)
        query, grad = q_ref[:, cut], grad_ref[:, cut]
        centre = jnp.sum((grad.astype(F32) * out_rows_ref[:, cut].astype(F32)).T, axis=0, keepdims=True)
        scores[...] = dot(k_ref[:, cut], query, NT)
        grads[...] = dot(v_ref[:, cut], grad, NT)
        for keys in key_chunks(k_ref.shape[0]):
            mask = allowed(key_place[keys, :], query_place[...], query_start[...])
            part = scores[keys, :] * (scale * LOG2E) - log_ref[h : h + 1]
            weights = jnp.exp2(jnp.where(mask, part, NEGATIVE))
            low_weights[keys, :] = weights.astype(BF16)
            low_grads[keys, :] = (weights * (grads[keys, :] - centre)).astype(BF16)
        sum_v[:, cut] += dot(low_weights[...], grad)
        sum_k[:, cut] += dot(low_grads[...], query)
        grad_query = (dot(key_t[cut, :], low_grads[...]) * scale).T
        out_ref[here, cut] = (grad_query * cos_q[...] - turn(grad_query) * sin_q[...]).astype(BF16)

    @pl.when(step == pl.num_programs(0) - 1)
    def _():
        for h in range(heads):
            cut = slice(h * width, (h + 1) * width)
            key = sum_k[:, cut] * scale
            second = slice((heads + h) * width, (heads + h + 1) * width)
            third = slice((2 * heads + h) * width, (2 * heads + h + 1) * width)
            out_ref[:, second] = (key * cos_k[...] - turn(key) * sin_k[...]).astype(BF16)
            out_ref[:, third] = sum_v[:, cut].astype(BF16)


def attention(qkv, cosine, sine, place, start, heads):
    tokens, width = qkv.shape[0], qkv.shape[1] // 3
    head_width = width // heads
    block = 256 if tokens % 256 == 0 else tokens
    row = lambda i: (i, 0)
    whole = lambda i: (0, 0)
    along = lambda i: (0, i)
    key_place = jnp.broadcast_to(place[:, None], (tokens, block))
    blocks = tokens // block
    return pl.pallas_call(
        functools.partial(attend_kernel, heads, head_width),
        grid=(blocks,),
        in_specs=[
            pl.BlockSpec((block, width), row),
            pl.BlockSpec((tokens, width), lambda i: (0, 1)),
            pl.BlockSpec((tokens, width), lambda i: (0, 2)),
            pl.BlockSpec((block, head_width), row),
            pl.BlockSpec((block, head_width), row),
            pl.BlockSpec((tokens, head_width), whole),
            pl.BlockSpec((tokens, head_width), whole),
            pl.BlockSpec((tokens, block), whole),
            pl.BlockSpec((1, block), along),
            pl.BlockSpec((1, block), along),
        ],
        out_specs=[
            pl.BlockSpec((block, width), row),
            pl.BlockSpec((block, width), row),
            pl.BlockSpec((tokens, width), whole),
            pl.BlockSpec((heads, block), along),
        ],
        out_shape=[
            jax.ShapeDtypeStruct((tokens, width), BF16),
            jax.ShapeDtypeStruct((tokens, width), BF16),
            jax.ShapeDtypeStruct((tokens, width), BF16),
            jax.ShapeDtypeStruct((heads, tokens), F32),
        ],
        scratch_shapes=[pltpu.VMEM((width, tokens), BF16), pltpu.VMEM((heads, tokens, block), F32),
            pltpu.VMEM((tokens, block), BF16),
        ],
        compiler_params=params(48),
        cost_estimate=NO_COST,
    )(qkv, qkv, qkv, cosine, sine, cosine, sine, key_place, place[None], start[None])


def attention_back(qkv, rot_q, rot_k, attended, grad, logs, cosine, sine, place, start, heads):
    tokens, width = rot_q.shape
    head_width = width // heads
    block = 256 if tokens % 256 == 0 else tokens
    row = lambda i: (i, 0)
    whole = lambda i: (0, 0)
    along = lambda i: (0, i)
    key_place = jnp.broadcast_to(place[:, None], (tokens, block))
    return pl.pallas_call(
        functools.partial(attend_back_kernel, heads, head_width),
        grid=(tokens // block,),
        in_specs=[
            pl.BlockSpec((block, width), row),
            pl.BlockSpec((tokens, width), whole),
            pl.BlockSpec((tokens, width), lambda i: (0, 2)),
            pl.BlockSpec((block, width), row),
            pl.BlockSpec((block, width), row),
            pl.BlockSpec((heads, block), along),
            pl.BlockSpec((block, head_width), row),
            pl.BlockSpec((block, head_width), row),
            pl.BlockSpec((tokens, head_width), whole),
            pl.BlockSpec((tokens, head_width), whole),
            pl.BlockSpec((tokens, block), whole),
            pl.BlockSpec((1, block), along),
            pl.BlockSpec((1, block), along),
        ],
        out_specs=pl.BlockSpec((tokens, 3 * width), whole),
        out_shape=jax.ShapeDtypeStruct((tokens, 3 * width), BF16),
        scratch_shapes=[
            pltpu.VMEM((width, tokens), BF16),
            pltpu.VMEM((tokens, width), F32),
            pltpu.VMEM((tokens, width), F32),
            pltpu.VMEM((tokens, block), F32),
            pltpu.VMEM((tokens, block), F32),
            pltpu.VMEM((tokens, block), BF16),
            pltpu.VMEM((tokens, block), BF16),
        ],
        compiler_params=params(56),
        cost_estimate=NO_COST,
    )(rot_q, rot_k, qkv, attended, grad, logs, cosine, sine, cosine, sine, key_place, place[None], start[None])


def sequence_places(ordering, lengths):
    ending = jnp.cumsum(lengths)
    segment = jnp.sum((ordering[:, None] >= ending[None, :]).astype(jnp.int32), axis=1)
    opening = ending - lengths
    chosen = segment[:, None] == jnp.arange(lengths.shape[0], dtype=jnp.int32)[None, :]
    return jnp.sum(jnp.where(chosen, opening[None, :], 0), axis=1)


def rope_tables(position, head_width):
    middle = head_width // 2
    frequency = jnp.exp(
        jnp.arange(middle, dtype=F32) * (-2.0 * math.log(10000.0) / head_width)
    )
    angles = position.astype(F32)[:, None] * frequency[None, :]
    sine = jnp.sin(angles)
    cosine = jnp.cos(angles)
    return jnp.concatenate([cosine, cosine], axis=1), jnp.concatenate([-sine, sine], axis=1)


def per_device(
    streams, cotangent, lengths, packed_at, query_weight, key_weight, value_weight, output_weight,
    gate_weight, up_weight, down_weight, mixing_weight, mixing_static,
):
    shards = lax.axis_size("shard")
    line = shards // 2
    me = lax.axis_index("shard")
    spot, core = me // 2, me % 2
    tokens, count, width = streams.shape
    head_width = width // HEADS
    heads = HEADS // shards
    local = heads * head_width
    shape = jax.ShapeDtypeStruct

    rounds = Rounds()
    run, also, then, tie, hold, finish = (
        rounds.run, rounds.also, rounds.then, rounds.tie, rounds.hold, rounds.finish
    )
    me_rep = lax.axis_index("rep")

    gather_mixing = Task(mixing_gather(mixing_weight))
    recut_qkv = Task(chip_exchange(recut_piece([query_weight, key_weight, value_weight])))
    run(gather_mixing, recut_qkv)
    run(gather_mixing, recut_qkv)
    finish(gather_mixing)
    mixing_rows = gather_mixing.value
    mixing_mean = jnp.sum(mixing_rows.astype(F32), axis=2)[:, None, :] / width
    static = jnp.pad(mixing_static, ((0, 0), (0, 0), (0, LANES - 6)))
    entering, packed, x = token_call(
        first_kernel, tokens, [streams, mixing_rows[0], static[0]],
        [
            shape((tokens, width), BF16), shape((count, tokens, LANES), F32),
            shape((count, tokens, width), BF16),
        ],
    )
    part = output_weight.shape[0] // lax.axis_size("rep")
    output_part = lax.dynamic_slice_in_dim(output_weight, me_rep * part, part, 0)
    gather_in = Task(line_gather(jnp.concatenate([entering, output_part], axis=0)))
    finish(recut_qkv)
    gather_qkv = Task(rep_gather(stack_units(recut_qkv.value, 2), True))
    run(gather_in, gather_qkv)
    gate_up_piece = recut_piece([tie(gate_weight), up_weight])
    run(gather_in, gather_qkv)
    hold(gate_up_piece)

    places = tie(packed_at)[0].reshape(line, 2, tokens)
    turned = jnp.roll(places, -spot, axis=0)
    place = jnp.concatenate(
        [
            lax.dynamic_index_in_dim(turned, core, 1, keepdims=False).reshape(-1),
            lax.dynamic_index_in_dim(turned, 1 - core, 1, keepdims=False).reshape(-1),
        ]
    )
    start = sequence_places(place, lengths[0])
    cosine, sine = rope_tables(place - start, head_width)
    w = tie(cotangent).transpose(1, 0, 2)
    gate_up_blocks = []
    recut_gate_up = Task(chip_exchange(gate_up_piece, (line // 4, line // 4, line // 4), gate_up_blocks, line - 1))
    run(gather_in, recut_gate_up)
    hold(cosine, sine, w)
    finish(gather_in, gather_qkv)
    gathered = gather_in.value.reshape(line, tokens + part, width)
    mine_in = gathered[:, :tokens].reshape(line * tokens, width)
    swap = Task(other_core(mine_in))
    gather_output = Task(rep_gather(cut_units(gathered[:, tokens:], 2), True))
    run(swap, recut_gate_up, gather_output)
    attention_weight = recut_join(gather_qkv.value)
    hold(attention_weight)
    mine_qkv = product(mine_in, attention_weight, into=0)
    other_in = swap.value
    run(recut_gate_up, gather_output)
    qkv = product(other_in, attention_weight, into=1, filled=(mine_qkv,))
    attended, rot_q, rot_k, logs = attention(qkv, cosine, sine, place, start, heads)
    finish(gather_output)
    hold(attended)
    gather_low = Task(rep_gather(stack_units(gate_up_blocks[: shards // 2], 2), True))
    tokens_out = Task(to_tokens(attended.reshape(2, line, tokens, local)))
    run(tokens_out, recut_gate_up, gather_low)
    output_mine = rows_in_order(gather_output.value)
    swap = Task(other_core(output_mine))
    run(tokens_out, swap)
    branch = dot(tokens_out.value[0], output_mine) + dot(tokens_out.value[1], swap.value)
    hold(branch)
    run(recut_gate_up)

    middle, entering_next, down_in, packed_next = token_call(
        middle_kernel, tokens,
        [x, packed, static[0], branch, w, mixing_rows[1], static[1]],
        [
            shape((count, tokens, width), F32), shape((tokens, width), BF16),
            shape((tokens, width), BF16), shape((count, tokens, LANES), F32),
        ],
    )
    finish(recut_gate_up)
    hold(entering_next)
    gather_high = Task(rep_gather(stack_units(gate_up_blocks[shards // 2 :], 2), True))
    gather_ffn, gather_down = Task(direct_gather(entering_next, 2)), Task(direct_gather(down_in, 2))
    run(gather_ffn, gather_low)
    finish(gather_low)
    gate_up = recut_join(gather_low.value)
    run(gather_ffn, gather_high)
    finish(gather_ffn)
    mine_ffn = gather_ffn.value
    swap = Task(other_core(mine_ffn))
    run(gather_down, swap, gather_high)
    finish(gather_high)
    gate_up = recut_join(gather_high.value, shards // 2, (gate_up,))
    hidden = gate_up.shape[1] // 2
    filled = ffn_forward(mine_ffn, gate_up, 0)
    other_ffn = swap.value
    run(gather_down)
    active, by_gate, by_up = ffn_forward(other_ffn, gate_up, 1, filled)
    theirs = product((active, 1), down_weight)
    finish(gather_down)
    mine_down = gather_down.value
    swap_z, swap = Task(other_core(theirs)), Task(other_core(mine_down))
    run(swap_z, swap)
    filled = ffn_backward(mine_down, down_weight, by_gate, by_up, 0)
    other_down = swap.value
    scatter_z = Task(direct_scatter(product((active, 0), down_weight, add=swap_z.value), 2))
    run(scatter_z)
    grad_both = ffn_backward(other_down, down_weight, by_gate, by_up, 1, (filled,))
    theirs = product((grad_both, 1), gate_up, NT)
    down_blocks = rows_product([(active, 0), (active, 1)], [mine_down, other_down], 2)
    hold(theirs, *down_blocks[0])
    swap = Task(other_core(theirs))
    scatter_down = Task(rep_scatter(down_blocks, True))
    run(scatter_z, swap, scatter_down)
    f_mine = product((grad_both, 0), gate_up, NT, add=swap.value)
    ready = after(grad_both, f_mine)
    gate_up_blocks = columns_product([mine_ffn, other_ffn], [(ready, 0), (ready, 1)], 2)
    finish(scatter_z)
    scatter_f = Task(direct_scatter(f_mine, 2))
    scatter_gate_up = Task(rep_scatter(gate_up_blocks))
    run(scatter_f, (scatter_gate_up, 1))
    run(scatter_f, scatter_gate_up)
    finish(scatter_f)

    grad_middle, grad_branch, grad_beta, mixing_sum_next, static_sum_next = token_call(
        functools.partial(middle_back_kernel, line), tokens,
        [
            middle, packed_next, static[1], packed, static[0], w, branch, mixing_rows[1], mixing_mean[1],
            *scatter_z.value, *scatter_f.value,
        ],
        [
            shape((count, tokens, width), F32), shape((tokens, width), BF16), shape((tokens, LANES), F32),
            shape((LANES, width), F32), shape((8, LANES), F32),
        ],
    )
    gather_branch = Task(direct_gather(grad_branch, 2))
    run(gather_branch, scatter_gate_up)
    finish(scatter_gate_up)
    low = []
    recut_grad = Task(chip_exchange(jnp.concatenate(scatter_gate_up.value, axis=0), (line // 4, line // 4), low))
    (result,) = token_call(
        out_kernel, tokens, [tie(middle), packed_next, static[1], *scatter_z.value],
        [shape((tokens, count, width), BF16)],
    )
    run(gather_branch, scatter_down)
    hold(result)
    finish(gather_branch)
    mine_branch = gather_branch.value
    swap = Task(other_core(mine_branch))
    run(swap, recut_grad)
    finish(scatter_down)
    gather_down_rows = Task(rep_gather(scatter_down.value, True))
    grad_mine = product(mine_branch, output_weight, NT, into=0)
    other_branch = swap.value
    run(recut_grad, gather_down_rows)
    output_blocks = rows_product([(attended, 0), (attended, 1)], [mine_branch, other_branch], 2)
    hold(*output_blocks[0])
    grad_attended = product(other_branch, output_weight, NT, into=1, filled=(grad_mine,))
    hold(grad_attended)
    grad_qkv = attention_back(qkv, rot_q, rot_k, attended, grad_attended, logs, cosine, sine, place, start, heads)
    theirs = product((grad_qkv, 1), attention_weight, NT)
    run(recut_grad, gather_down_rows)
    hold(theirs)
    gather_low = Task(rep_gather(stack_units(low[: shards // 2], 2), True))
    scatter_output = Task(rep_scatter(output_blocks, True))
    run(recut_grad, gather_low, scatter_output)
    finish(recut_grad, gather_down_rows)
    qkv_blocks = columns_product([mine_in, other_in], [(grad_qkv, 0), (grad_qkv, 1)], 2)
    hold(*qkv_blocks[0])
    gather_high = Task(rep_gather(stack_units(low[shards // 2 :], 2), True))
    swap = Task(other_core(theirs))
    run(swap)
    scatter_a = Task(direct_scatter(product((grad_qkv, 0), attention_weight, NT, add=swap.value), 2))
    scatter_qkv = Task(rep_scatter(qkv_blocks, True))
    run(scatter_a, scatter_qkv)
    run(scatter_a, scatter_qkv, gather_low)
    finish(scatter_qkv, scatter_a, gather_low)
    recut_qkv_grad = Task(chip_exchange(jnp.concatenate(scatter_qkv.value, axis=0)))
    run(recut_qkv_grad, gather_high, scatter_output)
    finish(scatter_output)
    gather_output = Task(rep_gather(scatter_output.value, True))
    grad_streams, mixing_sum, static_sum = token_call(
        first_back_kernel, tokens,
        [x, packed, static[0], tie(grad_middle), grad_beta, mixing_rows[0], mixing_mean[0], *scatter_a.value],
        [shape((tokens, count, width), F32), shape((LANES, width), F32), shape((8, LANES), F32)],
    )
    run(recut_qkv_grad, gather_high)
    hold(grad_streams)
    finish(recut_qkv_grad, gather_high)
    gather_qkv_grad = Task(rep_gather(stack_units(recut_qkv_grad.value, 2), True))
    mixing_sums = jnp.stack([mixing_sum, mixing_sum_next])
    mixing_sums = (mixing_sums[:, :6] + mixing_sums[:, 8:14]).reshape(12, shards, -1)
    small = jnp.concatenate(
        [
            jnp.pad(mixing_sums.transpose(1, 0, 2), ((0, 0), (0, 4), (0, 0))),
            jnp.broadcast_to(jnp.concatenate([static_sum, static_sum_next])[None], (shards, 16, LANES)),
        ],
        axis=2,
    )
    sum_last = Task(sum_small(small))
    run(sum_last, gather_qkv_grad, gather_output)
    gate_rows, up_rows = columns_join([[tie(v) for v in u] for u in gather_low.value + gather_high.value], 2)
    down_rows = rows_join([[tie(v) for v in u] for u in gather_down_rows.value])
    run(sum_last, gather_qkv_grad)
    hold(gate_rows, down_rows)
    run(sum_last, gather_output)
    finish(gather_qkv_grad, sum_last, gather_output)
    output_rows = rows_join(gather_output.value)
    small = sum_last.value
    rows = width // shards
    own_mixing = jnp.swapaxes(small[:12, :rows].reshape(2, 6, rows), 1, 2)
    static_sums = jnp.stack([small[0:count, rows : rows + 6], small[8 : 8 + count, rows : rows + 6]])
    query_rows, key_rows, value_rows = columns_join(gather_qkv_grad.value, 3)
    return (
        result, grad_streams, query_rows, key_rows, value_rows, output_rows,
        gate_rows, up_rows, down_rows, own_mixing, static_sums,
    )


def solution(mesh):
    tokens = P(("rep", "shard"), None, None)
    rows = P("shard", None)
    return jax.shard_map(
        per_device,
        mesh=mesh,
        in_specs=(tokens, tokens, P("rep", None), P("rep", None)) + (rows,) * 7 + (P(None, "shard", None), P()),
        out_specs=(tokens, tokens) + (rows,) * 7 + (P(None, "shard", None), P()),
        check_vma=False,
    )
```

```python
import functools
import math

import jax
import jax.numpy as jnp
from jax import lax
from jax.experimental import pallas as pl
from jax.experimental.pallas import tpu as pltpu
from jax.sharding import PartitionSpec as P

HEADS = 16
EPSILON = 1e-05
NEGATIVE = -1e30
LANES = 128
LOG2E = 1.4426950408889634
F32 = jnp.float32
BF16 = jnp.bfloat16
NO_COST = pl.CostEstimate(flops=0, bytes_accessed=0, transcendentals=0)
NN = (((1,), (0,)), ((), ()))
NT = (((1,), (1,)), ((), ()))
TN = (((0,), (0,)), ((), ()))


def dot(a, b, dims=NN):
    return lax.dot_general(a, b, dims, preferred_element_type=F32)


def params(mib):
    return pltpu.CompilerParams(vmem_limit_bytes=mib << 20)


def after(value, *events):
    return lax.optimization_barrier((value, *events))[0] if events else value


def assemble_kernel(line, x_ref, *refs):
    rights, lefts, out_ref = refs[: line - 1], refs[line - 1 : -1], refs[-1]
    out_ref[0] = x_ref[...]
    for k in range(1, line):
        out_ref[k] = lefts[k - 1][...] + rights[line - k - 1][...]


class Task:
    def __init__(self, steps):
        self.steps, self.value, self.over, self.arrived = steps, None, False, []
        self.advance(None)

    def advance(self, arrived):
        self.arrived += arrived or []
        try:
            self.sends = list(self.steps.send(arrived))
            self.left = list(range(len(self.sends)))
            self.got = [None] * len(self.sends)
        except StopIteration as stop:
            self.value, self.over, self.left = stop.value, True, []


class Rounds:
    def __init__(self):
        self.base, self.fence, self.last = (), (), ()

    def hold(self, *values):
        self.fence += values

    def tie(self, value):
        return after(value, *self.fence)

    def run(self, *jobs):
        self.base, self.fence = self.fence, ()
        self.last = self.base
        self.send(jobs, self.base)

    def also(self, *jobs):
        self.last = self.send(jobs, self.base)

    def then(self, *jobs):
        self.last = self.send(jobs, self.last)

    def send(self, jobs, events):
        sends = []
        for job in jobs:
            task, pairs = job if isinstance(job, tuple) else (job, len(job.left))
            sends += [(task, i) for i in task.left[: 2 * pairs]]
        out = tuple(t.sends[i][0](after(t.sends[i][1], *events)) for t, i in sends)
        self.fence += out
        for (t, i), v in zip(sends, out):
            t.got[i] = v
            t.left.remove(i)
        for t in {id(t): t for t, _ in sends}.values():
            if not t.left:
                t.advance(t.got)
        return out

    def finish(self, *tasks):
        while any(not t.over for t in tasks):
            self.run(*tasks)


def sender(axis, pairs):
    return lambda x: lax.ppermute(x, axis, pairs)


def assemble_kernel(line, x_ref, *refs):
    rights, lefts, out_ref = refs[: line - 1], refs[line - 1 : -1], refs[-1]
    out_ref[0] = x_ref[...]
    for k in range(1, line):
        out_ref[k] = lefts[k - 1][...] + rights[line - k - 1][...]


def line_gather(x):
    line = lax.axis_size("shard") // 2
    right = left = x
    rights, lefts = [], []
    for step in range(line - 1):
        right, left = yield [
            (sender("shard", [(2 * p + c, 2 * p + 2 + c) for p in range(step, line - 1) for c in range(2)]), right),
            (sender("shard", [(2 * p + c, 2 * p - 2 + c) for p in range(1, line - step) for c in range(2)]), left),
        ]
        rights.append(right)
        lefts.append(left)
    rows, width = x.shape
    (mine,) = token_call(
        functools.partial(assemble_kernel, line), rows, [x, *rights, *lefts],
        [jax.ShapeDtypeStruct((line, rows, width), x.dtype)], block=rows // 2 if rows % 32 == 0 else rows,
    )
    return mine.reshape(line * rows, width)


def other_core(x):
    size = lax.axis_size("shard")
    (other,) = yield [(sender("shard", [(i, i ^ 1) for i in range(size)]), x)]
    return other


def line_shift(k):
    line = lax.axis_size("shard") // 2
    return sender("shard", [(2 * p + c, 2 * ((p + k) % line) + c) for p in range(line) for c in range(2)])


def shifts(line, steps):
    return [list(range(1, line))] if steps == 1 else [list(range(1, line, 2)), list(range(2, line, 2))]


def direct_gather(x, steps=1):
    line = lax.axis_size("shard") // 2
    came = {}
    for step in shifts(line, steps):
        came |= dict(zip(step, (yield [(line_shift(k), x) for k in step])))
    return jnp.concatenate([x] + [came[line - q] for q in range(1, line)], axis=0)


def direct_scatter(rows, steps=1):
    line = lax.axis_size("shard") // 2
    parts = list(rows.reshape(line, rows.shape[0] // line, -1))
    came = [parts[0]]
    for step in shifts(line, steps):
        came += yield [(line_shift(k), parts[k]) for k in step]
    return came


def rep_sender(bit):
    return sender("rep", [(i, i ^ (1 << bit)) for i in range(lax.axis_size("rep"))])


def rep_orders(units):
    bits = list(range(lax.axis_size("rep").bit_length() - 1))
    return [bits] * (units // 2) + [bits[::-1]] * (units - units // 2)


def paired(sends):
    middle = len(sends) // 2
    return [v for pair in zip(sends[:middle], sends[middle:]) for v in pair]


def rep_scatter(units, merge=False):
    orders = rep_orders(len(units))
    units = [dict(enumerate(u)) for u in units]
    for i in range(len(orders[0])):
        bits = [1 << o[i] for o in orders]
        keys = [[m for m in unit if m & bit] for unit, bit in zip(units, bits)]
        came = yield from exchange_blocks(units, keys, [o[i] for o in orders], merge)
        units = [
            {m ^ bit: unit[m ^ bit] + v for m, v in zip(key, new)}
            for unit, bit, key, new in zip(units, bits, keys, came)
        ]
    return [u[0] for u in units]


def rep_gather(units, merge=False):
    orders = [o[::-1] for o in rep_orders(len(units))]
    units = [{0: u} for u in units]
    for i in range(len(orders[0])):
        keys = [list(unit) for unit in units]
        came = yield from exchange_blocks(units, keys, [o[i] for o in orders], merge)
        for unit, o, key, new in zip(units, orders, keys, came):
            unit |= {m ^ (1 << o[i]): v for m, v in zip(key, new)}
    return [[u[m] for m in range(len(u))] for u in units]


def rep_flip(m):
    return sender("rep", [(i, i ^ m) for i in range(lax.axis_size("rep"))])


def rep_scatter_direct(blocks):
    came = yield [(rep_flip(m), blocks[m]) for m in range(1, len(blocks))]
    return sum(v.astype(F32) for v in [blocks[0], *came]).astype(blocks[0].dtype)


def rep_gather_direct(block):
    came = yield [(rep_flip(m), block) for m in range(1, lax.axis_size("rep"))]
    return [block, *came]


def exchange_blocks(units, keys, bits, merge):
    if merge:
        came = yield [
            (rep_sender(bit), jnp.concatenate([unit[m] for m in key]) if len(key) > 1 else unit[key[0]])
            for unit, key, bit in paired(list(zip(units, keys, bits)))
        ]
        order = paired(list(range(len(units))))
        return [cut_units(came[order.index(u)], len(keys[u])) for u in range(len(units))]
    flat = paired([(u, m) for u, key in enumerate(keys) for m in key])
    came = yield [(rep_sender(bits[u]), units[u][m]) for u, m in flat]
    came = dict(zip(flat, came))
    return [[came[u, m] for m in key] for u, key in enumerate(keys)]


def chip_exchange(x, counts=(), out=None, split=None):
    shards = lax.axis_size("shard")
    me = lax.axis_index("shard")
    pick = lambda k: lax.dynamic_index_in_dim(x, me ^ k, 0, keepdims=False)
    (came,) = yield [
        (sender("shard", [(i, i ^ 1) for i in range(shards)]), jnp.stack([pick(k) for k in range(1, shards, 2)]))
    ]
    out, counts = [] if out is None else out, list(counts)
    blocks = {0: pick(0), 1: came[0]}
    left = []
    for q in range(1, shards // 2):
        if split is None or q < split:
            left.append(((2 * q, 2 * q + 1), jnp.stack([pick(2 * q), came[q]])))
        else:
            left += [((2 * q + 1,), came[q]), ((2 * q,), pick(2 * q))]
    while left:
        amount = counts.pop(0) if counts else len(left)
        step, left = left[:amount], left[amount:]
        arrived = yield [
            (sender("shard", [(i, i ^ (keys[0] & ~1)) for i in range(shards)]), v) for keys, v in step
        ]
        for (keys, _), v in zip(step, arrived):
            blocks |= {k: v[f] for f, k in enumerate(keys)} if len(keys) > 1 else {keys[0]: v}
        out[:] = [blocks[k] for k in range(shards) if all(i in blocks for i in range(k + 1))]
    return out


def stack_units(blocks, count):
    size = len(blocks) // count
    return [jnp.stack(blocks[i * size : (i + 1) * size]) for i in range(count)]


def to_tokens(x):
    shards = lax.axis_size("shard")
    line = shards // 2
    (came,) = yield [(sender("shard", [(i, i ^ 1) for i in range(shards)]), x[1])]
    held = jnp.stack([x[0], came], axis=1)
    came = yield [
        (sender("shard", [(2 * p + c, 2 * ((p + k) % line) + c) for p in range(line) for c in range(2)]), held[k])
        for k in range(1, line)
    ]
    came = [held[0], *came]
    return [jnp.concatenate([came[(line - q) % line][f] for q in range(line)], axis=1) for f in range(2)]


def cut_units(x, count):
    size = x.shape[0] // count
    return [x[i * size : (i + 1) * size] for i in range(count)]


def recut_piece(weights):
    shards, reps = lax.axis_size("shard"), lax.axis_size("rep")
    part = weights[0].shape[0] // reps
    start = lax.axis_index("rep") * part
    pieces = [
        lax.dynamic_slice_in_dim(w, start, part, 0).reshape(part, shards, -1).transpose(1, 0, 2) for w in weights
    ]
    return jnp.concatenate(pieces, axis=2)


def halves(x):
    return cut_units(x, 2)


def unit_specs(units):
    size = units[0][0].shape[0]
    return [
        pl.BlockSpec((1,) + v.shape[1:], lambda k, me, g=g: (jnp.clip(k - g * size, 0, size - 1), 0, 0))
        for g, u in enumerate(units) for v in u
    ]


def columns_kernel(units, reps, parts, me_ref, *refs):
    outs = refs[-parts:]
    size = pl.num_programs(0) // units
    part = refs[0].shape[1]
    for g in range(units):
        @pl.when(pl.program_id(0) // size == g)
        def _(chosen=refs[g * reps : (g + 1) * reps]):
            for m in range(reps):
                row = pl.multiple_of((me_ref[0] ^ m) * part, part)
                for i, out_ref in enumerate(outs):
                    width = out_ref.shape[1]
                    out_ref[pl.ds(row, part), :] = chosen[m][0, :, i * width : (i + 1) * width].astype(out_ref.dtype)


def join(units, parts, spec, shapes, filled=(), mib=32):
    reps = lax.axis_size("rep")
    operands = [v for u in units for v in u]
    return pl.pallas_call(
        functools.partial(columns_kernel, len(units), reps, parts),
        grid_spec=pltpu.PrefetchScalarGridSpec(
            num_scalar_prefetch=1,
            grid=(len(units) * units[0][0].shape[0],),
            in_specs=unit_specs(units) + [pl.BlockSpec(memory_space=pl.ANY)] * len(filled),
            out_specs=[spec] * parts,
        ),
        out_shape=shapes,
        input_output_aliases={1 + len(operands) + i: i for i in range(len(filled))},
        compiler_params=params(mib),
        cost_estimate=NO_COST,
    )(jnp.stack([lax.axis_index("rep"), lax.axis_index("shard")]).astype(jnp.int32), *operands, *filled)


def recut_join(units, first=0, filled=()):
    shards, reps = lax.axis_size("shard"), lax.axis_size("rep")
    _, part, columns = units[0][0].shape
    rows = part * reps
    return join(
        units, 1, pl.BlockSpec((rows, columns), lambda k, me: ((k + first) ^ me[1], 0)),
        [jax.ShapeDtypeStruct((shards * rows, columns), BF16)], filled,
    )[0]


def rows_in_order(units):
    blocks, part, columns = units[0][0].shape
    rows = part * lax.axis_size("rep")
    return join(
        units, 1, pl.BlockSpec((rows, columns), lambda k, me: (k, 0)),
        [jax.ShapeDtypeStruct((len(units) * blocks * rows, columns), BF16)],
    )[0]


def columns_join(units, parts):
    shards, reps = lax.axis_size("shard"), lax.axis_size("rep")
    _, part, columns = units[0][0].shape
    rows, width = part * reps, columns // parts
    return join(
        units, parts, pl.BlockSpec((rows, width), lambda k, me: (0, k ^ me[1])),
        [jax.ShapeDtypeStruct((rows, shards * width), F32)] * parts, mib=56 if parts == 2 else 32,
    )


def rows_kernel(units, reps, me_ref, *refs):
    out_ref = refs[-1]
    part = refs[0].shape[0]
    for u in range(units):
        for m in range(reps):
            row = pl.multiple_of((me_ref[0] ^ m) * (units * part) + u * part, part)
            out_ref[pl.ds(row, part), :] = refs[u * reps + m][...].astype(F32)


def rows_join(units):
    reps = lax.axis_size("rep")
    operands = [v for u in units for v in u]
    part, columns = operands[0].shape
    block = 512 if columns % 512 == 0 else columns
    return pl.pallas_call(
        functools.partial(rows_kernel, len(units), reps),
        grid_spec=pltpu.PrefetchScalarGridSpec(
            num_scalar_prefetch=1,
            grid=(columns // block,),
            in_specs=[pl.BlockSpec((part, block), lambda j, me: (0, j))] * len(operands),
            out_specs=pl.BlockSpec((part * len(operands), block), lambda j, me: (0, j)),
        ),
        out_shape=jax.ShapeDtypeStruct((part * len(operands), columns), F32),
        compiler_params=params(32),
        cost_estimate=NO_COST,
    )(lax.axis_index("rep").astype(jnp.int32)[None], *operands)


def mixing_kernel(me_ref, *refs):
    out_ref = refs[-1]
    out_ref[...] = jnp.zeros_like(out_ref)
    width = refs[0].shape[2]
    for k, ref in enumerate(refs[:-1]):
        start = pl.multiple_of((me_ref[0] ^ k) * width, width)
        out_ref[:, : ref.shape[1], pl.ds(start, width)] = ref[...]


def mixing_gather(weight):
    shards = lax.axis_size("shard")
    piece = jnp.pad(jnp.swapaxes(weight, 1, 2), ((0, 0), (0, 2), (0, 0)))
    piece = jnp.concatenate([piece, piece], axis=1)
    (came,) = yield [(sender("shard", [(i, i ^ 1) for i in range(shards)]), piece)]
    held = jnp.stack([piece, came])
    came = yield [
        (sender("shard", [(i, i ^ (2 * q)) for i in range(shards)]), held) for q in range(1, shards // 2)
    ]
    came = [v[f] for v in [held, *came] for f in range(2)]
    return pl.pallas_call(
        mixing_kernel,
        grid_spec=pltpu.PrefetchScalarGridSpec(
            num_scalar_prefetch=1,
            grid=(1,),
            in_specs=[pl.BlockSpec(piece.shape, lambda i, me: (0, 0, 0))] * shards,
            out_specs=pl.BlockSpec((2, LANES, shards * piece.shape[2]), lambda i, me: (0, 0, 0)),
        ),
        out_shape=jax.ShapeDtypeStruct((2, LANES, shards * piece.shape[2]), BF16),
        compiler_params=params(32),
    )(lax.axis_index("shard").astype(jnp.int32)[None], *came)


def sum_small(blocks):
    shards, reps = lax.axis_size("shard"), lax.axis_size("rep")
    me = lax.axis_index("shard")
    blocks = blocks.reshape((shards // 2, 2) + blocks.shape[1:])
    pick = lambda f: lax.dynamic_index_in_dim(blocks, (me % 2) ^ f, 1, keepdims=False)
    (came,) = yield [(sender("shard", [(i, i ^ 1) for i in range(shards)]), pick(1))]
    pair = pick(0) + came
    take = lambda q: lax.dynamic_index_in_dim(pair, (me // 2) ^ q, 0, keepdims=False)
    total = take(0)
    came = yield [
        (sender("shard", [(i, i ^ (2 * q)) for i in range(shards)]), take(q)) for q in range(1, shards // 2)
    ]
    for v in came:
        total = total + v
    came = yield [(sender("rep", [(i, i ^ k) for i in range(reps)]), total) for k in range(1, reps)]
    terms = [total, *came]
    while len(terms) > 1:
        terms = [a + b for a, b in zip(terms[::2], terms[1::2])]
    return terms[0]


def lane(shape):
    return lax.broadcasted_iota(jnp.int32, shape, len(shape) - 1)


def column(values, index):
    return values[:, index : index + 1]


def split(values):
    high = values.astype(BF16)
    return high, (values - high.astype(F32)).astype(BF16)


def moments(values):
    mean = jnp.mean(values, axis=-1, keepdims=True)
    centred = values - mean
    spread = jnp.mean(centred * centred, axis=-1, keepdims=True)
    return mean, centred, lax.rsqrt(spread + EPSILON)


def mix_forward(streams, weight, static):
    count = len(streams)
    rows = streams[0].shape[0]
    stats = [moments(y) for y in streams]
    parts = [split(centred) for _, centred, _ in stats]
    raw = dot(jnp.concatenate([p[0] for p in parts] + [p[1] for p in parts], axis=0), weight, NT)
    at = lane((rows, LANES))
    pres, coefficients = [], []
    for i in range(count):
        pre = (raw[i * rows : (i + 1) * rows] + raw[(count + i) * rows : (count + i + 1) * rows]) * stats[i][2]
        pres.append(pre)
        coefficients.append(static[i : i + 1] + jnp.tanh(pre))
    entering = sum(column(c, 0) * y for c, y in zip(coefficients, streams))
    mean, centred, scale = moments(entering)
    packed = []
    for i in range(count):
        value = jnp.where(at < 6, pres[i], 0.0)
        value = jnp.where(at == 6, stats[i][0], jnp.where(at == 7, stats[i][2], value))
        packed.append(jnp.where(at == 8, mean, jnp.where(at == 9, scale, value)))
    return centred * scale, coefficients, packed


def mix_carry(streams, coefficients, j):
    return sum(column(c, 1 + j) * y for c, y in zip(coefficients, streams))


def mix_backward(streams, packed, static, grad_entering, grad_carried, grad_beta, weight_rows, weight_mean):
    count = len(streams)
    rows, width = streams[0].shape
    at = lane((rows, LANES))
    tanhs = [jnp.where(at < 6, jnp.tanh(p), 0.0) for p in packed]
    coefficients = [static[i : i + 1] + tanhs[i] for i in range(count)]
    mean, scale = column(packed[0], 8), column(packed[0], 9)
    entering = (sum(column(c, 0) * y for c, y in zip(coefficients, streams)) - mean) * scale
    inner = jnp.mean(grad_entering * entering, axis=-1, keepdims=True)
    outer = jnp.mean(grad_entering, axis=-1, keepdims=True)
    grad_sum = scale * (grad_entering - outer - entering * inner)
    grads, both, normed, scalars = [], [], [], []
    for i in range(count):
        y = streams[i]
        value = jnp.where(at == 0, jnp.sum(grad_sum * y, axis=-1, keepdims=True), 0.0)
        for j in range(count):
            value = jnp.where(at == 1 + j, jnp.sum(grad_carried[j] * y, axis=-1, keepdims=True), value)
        value = jnp.where(at == 1 + count, grad_beta[i], value)
        grad_pre = value * (1.0 - tanhs[i] * tanhs[i])
        high = grad_pre.astype(BF16).astype(F32)
        low = grad_pre - high
        both.append((high + pltpu.roll(low, 8, 1)).astype(BF16))
        grads.append(value)
        normed.append((y - column(packed[i], 6)) * column(packed[i], 7))
        scalars.append((
            jnp.sum(grad_pre * weight_mean, axis=-1, keepdims=True),
            jnp.sum(jnp.where(at < 6, grad_pre * packed[i], 0.0), axis=-1, keepdims=True) / width,
        ))
    both = jnp.concatenate(both, axis=0)
    grad_normed = dot(both, weight_rows)
    mixing_sum = dot(both, jnp.concatenate([n.astype(BF16) for n in normed], axis=0), TN)
    out = []
    for i in range(count):
        value = column(coefficients[i], 0) * grad_sum
        for j in range(count):
            value = value + column(coefficients[i], 1 + j) * grad_carried[j]
        a, b = scalars[i]
        out.append(
            value + column(packed[i], 7) * (grad_normed[i * rows : (i + 1) * rows] - a - normed[i] * b)
        )
    return out, mixing_sum, grads


def load_streams(ref):
    return [ref[i].astype(F32) for i in range(ref.shape[0])]


def coefficients_of(packed, static):
    return [static[i : i + 1] + jnp.tanh(packed[i]) for i in range(len(packed))]


def first_kernel(x_ref, weight_ref, static_ref, entering_ref, packed_ref, turned_ref):
    streams = [x_ref[:, i, :] for i in range(x_ref.shape[1])]
    for i, stream in enumerate(streams):
        turned_ref[i] = stream
    entering, _, packed = mix_forward([v.astype(F32) for v in streams], weight_ref[...], static_ref[...])
    entering_ref[...] = entering.astype(BF16)
    for i, value in enumerate(packed):
        packed_ref[i] = value


def middle_kernel(
    x_ref, packed_ref, static_ref, branch_ref, w_ref, weight_ref, static_next_ref,
    m_ref, entering_ref, down_ref, packed_next_ref,
):
    streams = load_streams(x_ref)
    count = len(streams)
    coefficients = coefficients_of([packed_ref[i] for i in range(count)], static_ref[...])
    branch = branch_ref[...]
    middle = []
    for j in range(count):
        middle.append(mix_carry(streams, coefficients, j) + column(coefficients[j], 5) * branch)
        m_ref[j] = middle[j]
    entering, following, packed = mix_forward(middle, weight_ref[...], static_next_ref[...])
    entering_ref[...] = entering.astype(BF16)
    for i, value in enumerate(packed):
        packed_next_ref[i] = value
    down_ref[...] = sum(column(following[j], 5) * w_ref[j].astype(F32) for j in range(count)).astype(BF16)


def total(refs):
    return sum(ref[...].astype(F32) for ref in refs)


def out_kernel(m_ref, packed_ref, static_ref, *refs):
    out_ref = refs[-1]
    streams = load_streams(m_ref)
    count = len(streams)
    coefficients = coefficients_of([packed_ref[i] for i in range(count)], static_ref[...])
    z = total(refs[:-1])
    for j in range(count):
        out_ref[:, j, :] = (mix_carry(streams, coefficients, j) + column(coefficients[j], 5) * z).astype(BF16)


def accumulate(step, mixing_ref, static_ref, mixing_sum, grads):
    @pl.when(step == 0)
    def _():
        mixing_ref[...] = jnp.zeros_like(mixing_ref)
        static_ref[...] = jnp.zeros_like(static_ref)

    mixing_ref[...] += mixing_sum
    at = lax.broadcasted_iota(jnp.int32, static_ref.shape, 0)
    sums = jnp.zeros(static_ref.shape, F32)
    for i, grad in enumerate(grads):
        sums = jnp.where(at == i, jnp.sum(grad, axis=0, keepdims=True), sums)
    static_ref[...] += sums


def middle_back_kernel(
    terms, m_ref, packed_ref, static_ref, packed_first_ref, static_first_ref, w_ref, branch_ref,
    weight_rows_ref, weight_mean_ref, *refs,
):
    grad_m_ref, grad_branch_ref, grad_beta_ref, mixing_ref, static_sum_ref = refs[2 * terms :]
    streams = load_streams(m_ref)
    count = len(streams)
    cotangent = load_streams(w_ref)
    z = total(refs[:terms])
    grad_entering = total(refs[terms : 2 * terms])
    grad_beta = [jnp.sum(w * z, axis=-1, keepdims=True) for w in cotangent]
    grads, mixing_sum, grad_pres = mix_backward(
        streams, [packed_ref[i] for i in range(count)], static_ref[...], grad_entering, cotangent, grad_beta,
        weight_rows_ref[...], weight_mean_ref[...],
    )
    accumulate(pl.program_id(0), mixing_ref, static_sum_ref, mixing_sum, grad_pres)
    first = coefficients_of([packed_first_ref[i] for i in range(count)], static_first_ref[...])
    branch = branch_ref[...]
    at = lane(grad_beta_ref.shape)
    beta = jnp.zeros(grad_beta_ref.shape, F32)
    for j in range(count):
        grad_m_ref[j] = grads[j]
        beta = jnp.where(at == j, jnp.sum(grads[j] * branch, axis=-1, keepdims=True), beta)
    grad_beta_ref[...] = beta
    grad_branch_ref[...] = sum(column(first[j], 5) * grads[j] for j in range(count)).astype(BF16)


def first_back_kernel(
    x_ref, packed_ref, static_ref, grad_m_ref, grad_beta_ref, weight_rows_ref, weight_mean_ref, *refs
):
    grad_ref, mixing_ref, static_sum_ref = refs[-3:]
    streams = load_streams(x_ref)
    count = len(streams)
    grad_entering = total(refs[:-3])
    beta = grad_beta_ref[...]
    grads, mixing_sum, grad_pres = mix_backward(
        streams, [packed_ref[i] for i in range(count)], static_ref[...], grad_entering,
        [grad_m_ref[i] for i in range(count)], [column(beta, i) for i in range(count)],
        weight_rows_ref[...], weight_mean_ref[...],
    )
    accumulate(pl.program_id(0), mixing_ref, static_sum_ref, mixing_sum, grad_pres)
    for i in range(count):
        grad_ref[:, i, :] = grads[i]


def token_call(kernel, tokens, operands, outputs, block=None, mib=40):
    block = block or (32 if tokens % 32 == 0 else tokens)

    def spec(shape):
        if tokens not in shape[:-1]:
            return pl.BlockSpec(shape, lambda i, n=len(shape): (0,) * n)
        axis = shape.index(tokens)
        cut = tuple(block if d == axis else s for d, s in enumerate(shape))
        return pl.BlockSpec(cut, lambda i, axis=axis, n=len(shape): tuple(i if d == axis else 0 for d in range(n)))

    size = sum(math.prod(o.shape) * o.dtype.itemsize for o in list(operands) + list(outputs))
    return pl.pallas_call(
        kernel,
        grid=(tokens // block,),
        in_specs=[spec(o.shape) for o in operands],
        out_specs=[spec(o.shape) for o in outputs],
        out_shape=list(outputs),
        compiler_params=params(mib),
        cost_estimate=NO_COST,
    )(*operands)


def rows_of(operand):
    return operand[0].shape[0] // 2 if isinstance(operand, tuple) else operand.shape[0]


def whole_of(operand):
    return operand[0] if isinstance(operand, tuple) else operand


def half_of(operand):
    return operand[1] if isinstance(operand, tuple) else 0


def tile_of(size):
    return next((t for t in (512, 384, 256, 128) if size % t == 0), size)


def product_kernel(dims, added, a_ref, b_ref, *refs):
    out = dot(a_ref[...], b_ref[...], dims)
    if added:
        out = out + refs[0][...].astype(F32)
    refs[-1][...] = out.astype(refs[-1].dtype)


def product(a, b, dims=NN, add=None, into=None, filled=()):
    rows, depth = rows_of(a), whole_of(a).shape[1]
    half, columns = half_of(a), b.shape[0] if dims == NT else b.shape[1]
    tile = tile_of(columns)
    operands = [whole_of(a), b] + ([] if add is None else [add]) + list(filled)
    specs = [
        pl.BlockSpec((rows, depth), lambda j: (half, 0)),
        pl.BlockSpec((tile, depth), lambda j: (j, 0)) if dims == NT else pl.BlockSpec((depth, tile), lambda j: (0, j)),
    ]
    if add is not None:
        specs.append(pl.BlockSpec((rows, tile), lambda j: (0, j)))
    specs += [pl.BlockSpec(memory_space=pl.ANY)] * len(filled)
    at = into or 0
    return pl.pallas_call(
        functools.partial(product_kernel, dims, add is not None),
        grid=(columns // tile,),
        in_specs=specs,
        out_specs=pl.BlockSpec((rows, tile), lambda j: (at, j)),
        out_shape=jax.ShapeDtypeStruct((rows if into is None else 2 * rows, columns), BF16),
        input_output_aliases={len(operands) - 1: 0} if filled else {},
        compiler_params=params(40),
        cost_estimate=NO_COST,
    )(*operands)


def columns_product_kernel(units, reps, me_ref, x0, x1, y0, y1, *refs):
    outs, sums = refs[:-1], refs[-1]
    sums[...] = dot(x0[...], y0[...], TN) + dot(x1[...], y1[...], TN)
    step = pl.program_id(0)
    size = pl.num_programs(0) // units
    part = sums.shape[0] // reps
    for u in range(units):
        @pl.when(step // size == u)
        def _(u=u):
            for m in range(reps):
                row = pl.multiple_of((me_ref[0] ^ m) * part, part)
                outs[u * reps + m][0] = sums[pl.ds(row, part), :].astype(BF16)


def columns_product(xs, ys, units):
    shards, reps = lax.axis_size("shard"), lax.axis_size("rep")
    tokens, columns = rows_of(ys[0]), whole_of(ys[0]).shape[1]
    rows = whole_of(xs[0]).shape[1] // shards
    size, part = shards // units, rows // reps
    x_specs = [pl.BlockSpec((tokens, rows), lambda s, me, h=half_of(x): (h, s)) for x in xs]
    y_specs = [pl.BlockSpec((tokens, columns), lambda s, me, h=half_of(y): (h, 0)) for y in ys]
    out = pl.pallas_call(
        functools.partial(columns_product_kernel, units, reps),
        grid_spec=pltpu.PrefetchScalarGridSpec(
            num_scalar_prefetch=1,
            grid=(shards,),
            in_specs=x_specs + y_specs,
            out_specs=[
                pl.BlockSpec((1, part, columns), lambda s, me, u=u: (jnp.clip(s - u * size, 0, size - 1), 0, 0))
                for u in range(units) for _ in range(reps)
            ],
            scratch_shapes=[pltpu.VMEM((rows, columns), F32)],
        ),
        out_shape=[jax.ShapeDtypeStruct((size, part, columns), BF16)] * (units * reps),
        compiler_params=params(48),
        cost_estimate=NO_COST,
    )(lax.axis_index("rep").astype(jnp.int32)[None], *[whole_of(v) for v in [*xs, *ys]])
    return [out[u * reps : (u + 1) * reps] for u in range(units)]


def rows_product_kernel(units, reps, me_ref, x0, x1, y0, y1, *refs):
    outs, sums = refs[:-1], refs[-1]
    sums[...] = dot(x0[...], y0[...], TN) + dot(x1[...], y1[...], TN)
    part = outs[0].shape[0]
    for u in range(units):
        for m in range(reps):
            row = pl.multiple_of((me_ref[0] ^ m) * (units * part) + u * part, part)
            outs[u * reps + m][...] = sums[pl.ds(row, part), :].astype(BF16)


def rows_product(xs, ys, units):
    reps = lax.axis_size("rep")
    tokens, columns = rows_of(ys[0]), whole_of(ys[0]).shape[1]
    rows = whole_of(xs[0]).shape[1]
    part, tile = rows // (units * reps), tile_of(columns)
    x_specs = [pl.BlockSpec((tokens, rows), lambda j, me, h=half_of(x): (h, 0)) for x in xs]
    y_specs = [pl.BlockSpec((tokens, tile), lambda j, me, h=half_of(y): (h, j)) for y in ys]
    out = pl.pallas_call(
        functools.partial(rows_product_kernel, units, reps),
        grid_spec=pltpu.PrefetchScalarGridSpec(
            num_scalar_prefetch=1,
            grid=(columns // tile,),
            in_specs=x_specs + y_specs,
            out_specs=[pl.BlockSpec((part, tile), lambda j, me: (0, j))] * (units * reps),
            scratch_shapes=[pltpu.VMEM((rows, tile), F32)],
        ),
        out_shape=[jax.ShapeDtypeStruct((part, columns), BF16)] * (units * reps),
        compiler_params=params(48),
        cost_estimate=NO_COST,
    )(lax.axis_index("rep").astype(jnp.int32)[None], *[whole_of(v) for v in [*xs, *ys]])
    return [out[u * reps : (u + 1) * reps] for u in range(units)]


def ffn_tile(hidden):
    return 256 if hidden % 256 == 0 else hidden


def chunks(rows):
    step = 320 if rows % 320 == 0 else rows
    return [slice(i, i + step) for i in range(0, rows, step)]


def ffn_kernel(x_ref, gate_ref, up_ref, *refs):
    active_ref, by_gate_ref, by_up_ref = refs[-3:]
    for cut in chunks(x_ref.shape[0]):
        gate = dot(x_ref[cut, :], gate_ref[...])
        up = dot(x_ref[cut, :], up_ref[...])
        sigmoid = 1.0 / (1.0 + jnp.exp2(gate * -LOG2E))
        swish = gate * sigmoid
        active_ref[cut, :] = (swish * up).astype(BF16)
        by_gate_ref[cut, :] = (up * sigmoid * (1.0 + gate - swish)).astype(BF16)
        by_up_ref[cut, :] = swish.astype(BF16)


def ffn_forward(x, weight, half, filled=()):
    rows, width = x.shape
    hidden = weight.shape[1] // 2
    tile = ffn_tile(hidden)
    tiles = hidden // tile
    return pl.pallas_call(
        ffn_kernel,
        grid=(tiles,),
        in_specs=[
            pl.BlockSpec((rows, width), lambda j: (0, 0)),
            pl.BlockSpec((width, tile), lambda j: (0, j)),
            pl.BlockSpec((width, tile), lambda j: (0, j + tiles)),
        ] + [pl.BlockSpec(memory_space=pl.ANY)] * len(filled),
        out_specs=[pl.BlockSpec((rows, tile), lambda j: (half, j))] * 3,
        out_shape=[jax.ShapeDtypeStruct((2 * rows, hidden), BF16)] * 3,
        input_output_aliases={3 + i: i for i in range(len(filled))},
        compiler_params=params(40),
        cost_estimate=NO_COST,
    )(x, weight, weight, *filled)


def ffn_back_kernel(tiles, x_ref, down_ref, by_gate_ref, by_up_ref, *refs):
    out_ref = refs[-1]
    step = pl.program_id(0)
    tile = down_ref.shape[0]
    for cut in chunks(x_ref.shape[0]):
        grad = dot(x_ref[cut, :], down_ref[...], NT)
        first = pl.multiple_of(step * tile, tile)
        second = pl.multiple_of((step + tiles) * tile, tile)
        out_ref[cut, pl.ds(first, tile)] = (grad * by_gate_ref[cut, :].astype(F32)).astype(BF16)
        out_ref[cut, pl.ds(second, tile)] = (grad * by_up_ref[cut, :].astype(F32)).astype(BF16)


def ffn_backward(x, down, by_gate, by_up, half, filled=()):
    rows, width = x.shape
    hidden = down.shape[0]
    tile = ffn_tile(hidden)
    tiles = hidden // tile
    return pl.pallas_call(
        functools.partial(ffn_back_kernel, tiles),
        grid=(tiles,),
        in_specs=[
            pl.BlockSpec((rows, width), lambda j: (0, 0)),
            pl.BlockSpec((tile, width), lambda j: (j, 0)),
            pl.BlockSpec((rows, tile), lambda j: (half, j)),
            pl.BlockSpec((rows, tile), lambda j: (half, j)),
        ] + [pl.BlockSpec(memory_space=pl.ANY)] * len(filled),
        out_specs=pl.BlockSpec((rows, 2 * hidden), lambda j: (half, 0)),
        out_shape=jax.ShapeDtypeStruct((2 * rows, 2 * hidden), BF16),
        input_output_aliases={4 + i: i for i in range(len(filled))},
        compiler_params=params(40),
        cost_estimate=NO_COST,
    )(x, down, by_gate, by_up, *filled)


def turn(values):
    return pltpu.roll(values, values.shape[-1] // 2, 1)


def allowed(places, query_place, query_start):
    return (places <= query_place) & (places >= query_start)


def key_chunks(tokens):
    step = 128 if tokens % 128 == 0 else tokens
    return [slice(i, i + step) for i in range(0, tokens, step)]


def attend_kernel(
    heads, width, q_ref, k_ref, v_ref, cos_q, sin_q, cos_k, sin_k, key_place, query_place, query_start,
    out_ref, rot_q_ref, rot_k_ref, log_ref, value_t, scores, weights,
):
    scale = width ** (-0.5)

    @pl.when(pl.program_id(0) == 0)
    def _():
        for h in range(heads):
            cut = slice(h * width, (h + 1) * width)
            key = k_ref[:, cut].astype(F32)
            rot_k_ref[:, cut] = (key * cos_k[...] + turn(key) * sin_k[...]).astype(BF16)
            value_t[cut, :] = v_ref[:, cut].T

    chunks_here = key_chunks(k_ref.shape[0])
    tops = []
    for h in range(heads):
        cut = slice(h * width, (h + 1) * width)
        query = q_ref[:, cut].astype(F32)
        query = (query * cos_q[...] + turn(query) * sin_q[...]).astype(BF16)
        rot_q_ref[:, cut] = query
        tops.append(jnp.full((8, query.shape[0]), NEGATIVE, F32))
        scores[h] = dot(rot_k_ref[:, cut], query, NT)
    for keys in chunks_here:
        mask = allowed(key_place[keys, :], query_place[...], query_start[...])
        for h in range(heads):
            part = jnp.where(mask, scores[h, keys, :], NEGATIVE)
            scores[h, keys, :] = part
            tops[h] = jnp.maximum(tops[h], jnp.max(part.reshape(-1, 8, part.shape[1]), axis=0))
    for h in range(heads):
        cut = slice(h * width, (h + 1) * width)
        top = jnp.max(tops[h], axis=0, keepdims=True) * (scale * LOG2E)
        total = jnp.zeros((8, top.shape[1]), F32)
        for keys in chunks_here:
            part = jnp.exp2(scores[h, keys, :] * (scale * LOG2E) - top)
            total = total + jnp.sum(part.reshape(-1, 8, part.shape[1]), axis=0)
            weights[keys, :] = part.astype(BF16)
        total = jnp.sum(total, axis=0, keepdims=True)
        out_ref[:, cut] = (dot(value_t[cut, :], weights[...]) * (1.0 / total)).T.astype(BF16)
        log_ref[h : h + 1] = top + jnp.log2(total)


def attend_back_kernel(
    heads, width, q_ref, k_ref, v_ref, grad_ref, log_ref, cos_q, sin_q, cos_k, sin_k, key_place,
    query_place, query_start, out_ref, key_t, sum_k, sum_v, scores, grads, low_weights, low_grads,
):
    scale = width ** (-0.5)
    step = pl.program_id(0)
    block = q_ref.shape[0]
    here = pl.ds(pl.multiple_of(step * block, block), block)

    @pl.when(step == 0)
    def _():
        for h in range(heads):
            cut = slice(h * width, (h + 1) * width)
            key_t[cut, :] = k_ref[:, cut].T
        sum_k[...] = jnp.zeros_like(sum_k)
        sum_v[...] = jnp.zeros_like(sum_v)

    for h in range(heads):
        cut = slice(h * width, (h + 1) * width)
        query, grad = q_ref[:, cut], grad_ref[:, cut]
        centre = jnp.zeros((8, block), F32)
        scores[...] = dot(k_ref[:, cut], query, NT)
        grads[...] = dot(v_ref[:, cut], grad, NT)
        for keys in key_chunks(k_ref.shape[0]):
            mask = allowed(key_place[keys, :], query_place[...], query_start[...])
            part = scores[keys, :] * (scale * LOG2E) - log_ref[h : h + 1]
            weights = jnp.exp2(jnp.where(mask, part, NEGATIVE))
            scores[keys, :] = weights
            low_weights[keys, :] = weights.astype(BF16)
            centre = centre + jnp.sum((weights * grads[keys, :]).reshape(-1, 8, block), axis=0)
        centre = jnp.sum(centre, axis=0, keepdims=True)
        for keys in key_chunks(k_ref.shape[0]):
            low_grads[keys, :] = (scores[keys, :] * (grads[keys, :] - centre)).astype(BF16)
        sum_v[:, cut] += dot(low_weights[...], grad)
        sum_k[:, cut] += dot(low_grads[...], query)
        grad_query = (dot(key_t[cut, :], low_grads[...]) * scale).T
        out_ref[here, cut] = (grad_query * cos_q[...] - turn(grad_query) * sin_q[...]).astype(BF16)

    @pl.when(step == pl.num_programs(0) - 1)
    def _():
        for h in range(heads):
            cut = slice(h * width, (h + 1) * width)
            key = sum_k[:, cut] * scale
            second = slice((heads + h) * width, (heads + h + 1) * width)
            third = slice((2 * heads + h) * width, (2 * heads + h + 1) * width)
            out_ref[:, second] = (key * cos_k[...] - turn(key) * sin_k[...]).astype(BF16)
            out_ref[:, third] = sum_v[:, cut].astype(BF16)


def attention(qkv, cosine, sine, place, start, heads):
    tokens, width = qkv.shape[0], qkv.shape[1] // 3
    head_width = width // heads
    block = 256 if tokens % 256 == 0 else tokens
    row = lambda i: (i, 0)
    whole = lambda i: (0, 0)
    along = lambda i: (0, i)
    key_place = jnp.broadcast_to(place[:, None], (tokens, block))
    blocks = tokens // block
    return pl.pallas_call(
        functools.partial(attend_kernel, heads, head_width),
        grid=(blocks,),
        in_specs=[
            pl.BlockSpec((block, width), row),
            pl.BlockSpec((tokens, width), lambda i: (0, 1)),
            pl.BlockSpec((tokens, width), lambda i: (0, 2)),
            pl.BlockSpec((block, head_width), row),
            pl.BlockSpec((block, head_width), row),
            pl.BlockSpec((tokens, head_width), whole),
            pl.BlockSpec((tokens, head_width), whole),
            pl.BlockSpec((tokens, block), whole),
            pl.BlockSpec((1, block), along),
            pl.BlockSpec((1, block), along),
        ],
        out_specs=[
            pl.BlockSpec((block, width), row),
            pl.BlockSpec((block, width), row),
            pl.BlockSpec((tokens, width), whole),
            pl.BlockSpec((heads, block), along),
        ],
        out_shape=[
            jax.ShapeDtypeStruct((tokens, width), BF16),
            jax.ShapeDtypeStruct((tokens, width), BF16),
            jax.ShapeDtypeStruct((tokens, width), BF16),
            jax.ShapeDtypeStruct((heads, tokens), F32),
        ],
        scratch_shapes=[pltpu.VMEM((width, tokens), BF16), pltpu.VMEM((heads, tokens, block), F32),
            pltpu.VMEM((tokens, block), BF16),
        ],
        compiler_params=params(48),
        cost_estimate=NO_COST,
    )(qkv, qkv, qkv, cosine, sine, cosine, sine, key_place, place[None], start[None])


def attention_back(qkv, rot_q, rot_k, grad, logs, cosine, sine, place, start, heads):
    tokens, width = rot_q.shape
    head_width = width // heads
    block = 256 if tokens % 256 == 0 else tokens
    row = lambda i: (i, 0)
    whole = lambda i: (0, 0)
    along = lambda i: (0, i)
    key_place = jnp.broadcast_to(place[:, None], (tokens, block))
    return pl.pallas_call(
        functools.partial(attend_back_kernel, heads, head_width),
        grid=(tokens // block,),
        in_specs=[
            pl.BlockSpec((block, width), row),
            pl.BlockSpec((tokens, width), whole),
            pl.BlockSpec((tokens, width), lambda i: (0, 2)),
            pl.BlockSpec((block, width), row),
            pl.BlockSpec((heads, block), along),
            pl.BlockSpec((block, head_width), row),
            pl.BlockSpec((block, head_width), row),
            pl.BlockSpec((tokens, head_width), whole),
            pl.BlockSpec((tokens, head_width), whole),
            pl.BlockSpec((tokens, block), whole),
            pl.BlockSpec((1, block), along),
            pl.BlockSpec((1, block), along),
        ],
        out_specs=pl.BlockSpec((tokens, 3 * width), whole),
        out_shape=jax.ShapeDtypeStruct((tokens, 3 * width), BF16),
        scratch_shapes=[
            pltpu.VMEM((width, tokens), BF16),
            pltpu.VMEM((tokens, width), F32),
            pltpu.VMEM((tokens, width), F32),
            pltpu.VMEM((tokens, block), F32),
            pltpu.VMEM((tokens, block), F32),
            pltpu.VMEM((tokens, block), BF16),
            pltpu.VMEM((tokens, block), BF16),
        ],
        compiler_params=params(56),
        cost_estimate=NO_COST,
    )(rot_q, rot_k, qkv, grad, logs, cosine, sine, cosine, sine, key_place, place[None], start[None])


def sequence_places(ordering, lengths):
    ending = jnp.cumsum(lengths)
    segment = jnp.sum((ordering[:, None] >= ending[None, :]).astype(jnp.int32), axis=1)
    opening = ending - lengths
    chosen = segment[:, None] == jnp.arange(lengths.shape[0], dtype=jnp.int32)[None, :]
    return jnp.sum(jnp.where(chosen, opening[None, :], 0), axis=1)


def rope_tables(position, head_width):
    middle = head_width // 2
    frequency = jnp.exp(
        jnp.arange(middle, dtype=F32) * (-2.0 * math.log(10000.0) / head_width)
    )
    angles = position.astype(F32)[:, None] * frequency[None, :]
    sine = jnp.sin(angles)
    cosine = jnp.cos(angles)
    return jnp.concatenate([cosine, cosine], axis=1), jnp.concatenate([-sine, sine], axis=1)


def per_device(
    streams, cotangent, lengths, packed_at, query_weight, key_weight, value_weight, output_weight,
    gate_weight, up_weight, down_weight, mixing_weight, mixing_static,
):
    shards = lax.axis_size("shard")
    line = shards // 2
    me = lax.axis_index("shard")
    spot, core = me // 2, me % 2
    tokens, count, width = streams.shape
    head_width = width // HEADS
    heads = HEADS // shards
    local = heads * head_width
    shape = jax.ShapeDtypeStruct

    rounds = Rounds()
    run, also, then, tie, hold, finish = (
        rounds.run, rounds.also, rounds.then, rounds.tie, rounds.hold, rounds.finish
    )
    me_rep = lax.axis_index("rep")

    gather_mixing = Task(mixing_gather(mixing_weight))
    recut_qkv = Task(chip_exchange(recut_piece([query_weight, key_weight, value_weight])))
    run(gather_mixing, recut_qkv)
    run(gather_mixing, recut_qkv)
    finish(gather_mixing)
    mixing_rows = gather_mixing.value
    mixing_mean = jnp.sum(mixing_rows.astype(F32), axis=2)[:, None, :] / width
    static = jnp.pad(mixing_static, ((0, 0), (0, 0), (0, LANES - 6)))
    entering, packed, x = token_call(
        first_kernel, tokens, [streams, mixing_rows[0], static[0]],
        [
            shape((tokens, width), BF16), shape((count, tokens, LANES), F32),
            shape((count, tokens, width), BF16),
        ],
    )
    part = output_weight.shape[0] // lax.axis_size("rep")
    output_part = lax.dynamic_slice_in_dim(output_weight, me_rep * part, part, 0)
    gather_in = Task(line_gather(jnp.concatenate([entering, output_part], axis=0)))
    finish(recut_qkv)
    gather_qkv = Task(rep_gather(stack_units(recut_qkv.value, 2), True))
    run(gather_in, gather_qkv)
    gate_up_piece = recut_piece([tie(gate_weight), up_weight])
    run(gather_in, gather_qkv)
    hold(gate_up_piece)

    places = tie(packed_at)[0].reshape(line, 2, tokens)
    turned = jnp.roll(places, -spot, axis=0)
    place = jnp.concatenate(
        [
            lax.dynamic_index_in_dim(turned, core, 1, keepdims=False).reshape(-1),
            lax.dynamic_index_in_dim(turned, 1 - core, 1, keepdims=False).reshape(-1),
        ]
    )
    start = sequence_places(place, lengths[0])
    cosine, sine = rope_tables(place - start, head_width)
    w = tie(cotangent).transpose(1, 0, 2)
    gate_up_blocks = []
    recut_gate_up = Task(chip_exchange(gate_up_piece, (line // 4, line // 4, line // 4), gate_up_blocks, line - 1))
    run(gather_in, recut_gate_up)
    hold(cosine, sine, w)
    finish(gather_in, gather_qkv)
    gathered = gather_in.value.reshape(line, tokens + part, width)
    mine_in = gathered[:, :tokens].reshape(line * tokens, width)
    swap = Task(other_core(mine_in))
    gather_output = Task(rep_gather(cut_units(gathered[:, tokens:], 2), True))
    run(swap, recut_gate_up, gather_output)
    attention_weight = recut_join(gather_qkv.value)
    hold(attention_weight)
    mine_qkv = product(mine_in, attention_weight, into=0)
    other_in = swap.value
    run(recut_gate_up, gather_output)
    qkv = product(other_in, attention_weight, into=1, filled=(mine_qkv,))
    attended, rot_q, rot_k, logs = attention(qkv, cosine, sine, place, start, heads)
    finish(gather_output)
    hold(attended)
    gather_low = Task(rep_gather(stack_units(gate_up_blocks[: shards // 2], 2), True))
    tokens_out = Task(to_tokens(attended.reshape(2, line, tokens, local)))
    run(tokens_out, recut_gate_up, gather_low)
    output_mine = rows_in_order(gather_output.value)
    swap = Task(other_core(output_mine))
    run(tokens_out, swap)
    branch = dot(tokens_out.value[0], output_mine) + dot(tokens_out.value[1], swap.value)
    hold(branch)
    run(recut_gate_up)

    middle, entering_next, down_in, packed_next = token_call(
        middle_kernel, tokens,
        [x, packed, static[0], branch, w, mixing_rows[1], static[1]],
        [
            shape((count, tokens, width), F32), shape((tokens, width), BF16),
            shape((tokens, width), BF16), shape((count, tokens, LANES), F32),
        ],
    )
    finish(recut_gate_up)
    hold(entering_next)
    gather_high = Task(rep_gather(stack_units(gate_up_blocks[shards // 2 :], 2), True))
    gather_ffn, gather_down = Task(direct_gather(entering_next, 2)), Task(direct_gather(down_in, 2))
    run(gather_ffn, gather_low)
    finish(gather_low)
    gate_up = recut_join(gather_low.value)
    run(gather_ffn, gather_high)
    finish(gather_ffn)
    mine_ffn = gather_ffn.value
    swap = Task(other_core(mine_ffn))
    run(gather_down, swap, gather_high)
    finish(gather_high)
    gate_up = recut_join(gather_high.value, shards // 2, (gate_up,))
    hidden = gate_up.shape[1] // 2
    filled = ffn_forward(mine_ffn, gate_up, 0)
    other_ffn = swap.value
    run(gather_down)
    active, by_gate, by_up = ffn_forward(other_ffn, gate_up, 1, filled)
    theirs = product((active, 1), down_weight)
    finish(gather_down)
    mine_down = gather_down.value
    swap_z, swap = Task(other_core(theirs)), Task(other_core(mine_down))
    run(swap_z, swap)
    filled = ffn_backward(mine_down, down_weight, by_gate, by_up, 0)
    other_down = swap.value
    scatter_z = Task(direct_scatter(product((active, 0), down_weight, add=swap_z.value), 2))
    run(scatter_z)
    grad_both = ffn_backward(other_down, down_weight, by_gate, by_up, 1, (filled,))
    theirs = product((grad_both, 1), gate_up, NT)
    down_blocks = rows_product([(active, 0), (active, 1)], [mine_down, other_down], 2)
    hold(theirs, *down_blocks[0])
    swap = Task(other_core(theirs))
    scatter_down = Task(rep_scatter(down_blocks, True))
    run(scatter_z, swap, scatter_down)
    f_mine = product((grad_both, 0), gate_up, NT, add=swap.value)
    ready = after(grad_both, f_mine)
    gate_up_blocks = columns_product([mine_ffn, other_ffn], [(ready, 0), (ready, 1)], 2)
    finish(scatter_z)
    scatter_f = Task(direct_scatter(f_mine, 2))
    scatter_gate_up = Task(rep_scatter(gate_up_blocks))
    run(scatter_f, (scatter_gate_up, 1))
    run(scatter_f, scatter_gate_up)
    finish(scatter_f)

    grad_middle, grad_branch, grad_beta, mixing_sum_next, static_sum_next = token_call(
        functools.partial(middle_back_kernel, line), tokens,
        [
            middle, packed_next, static[1], packed, static[0], w, branch, mixing_rows[1], mixing_mean[1],
            *scatter_z.value, *scatter_f.value,
        ],
        [
            shape((count, tokens, width), F32), shape((tokens, width), BF16), shape((tokens, LANES), F32),
            shape((LANES, width), F32), shape((8, LANES), F32),
        ],
    )
    gather_branch = Task(direct_gather(grad_branch, 2))
    run(gather_branch, scatter_gate_up)
    finish(scatter_gate_up)
    low = []
    recut_grad = Task(chip_exchange(jnp.concatenate(scatter_gate_up.value, axis=0), (line // 4, line // 4), low))
    (result,) = token_call(
        out_kernel, tokens, [tie(middle), packed_next, static[1], *scatter_z.value],
        [shape((tokens, count, width), BF16)],
    )
    run(gather_branch, scatter_down)
    hold(result)
    finish(gather_branch)
    mine_branch = gather_branch.value
    swap = Task(other_core(mine_branch))
    run(swap, recut_grad)
    finish(scatter_down)
    gather_down_rows = Task(rep_gather(scatter_down.value, True))
    grad_mine = product(mine_branch, output_weight, NT, into=0)
    other_branch = swap.value
    run(recut_grad, gather_down_rows)
    output_blocks = rows_product([(attended, 0), (attended, 1)], [mine_branch, other_branch], 2)
    hold(*output_blocks[0])
    grad_attended = product(other_branch, output_weight, NT, into=1, filled=(grad_mine,))
    hold(grad_attended)
    grad_qkv = attention_back(qkv, rot_q, rot_k, grad_attended, logs, cosine, sine, place, start, heads)
    theirs = product((grad_qkv, 1), attention_weight, NT)
    run(recut_grad, gather_down_rows)
    hold(theirs)
    gather_low = Task(rep_gather(stack_units(low[: shards // 2], 2), True))
    scatter_output = Task(rep_scatter(output_blocks, True))
    run(recut_grad, gather_low, scatter_output)
    finish(recut_grad, gather_down_rows)
    qkv_blocks = columns_product([mine_in, other_in], [(grad_qkv, 0), (grad_qkv, 1)], 2)
    hold(*qkv_blocks[0])
    gather_high = Task(rep_gather(stack_units(low[shards // 2 :], 2), True))
    swap = Task(other_core(theirs))
    run(swap)
    scatter_a = Task(direct_scatter(product((grad_qkv, 0), attention_weight, NT, add=swap.value), 2))
    scatter_qkv = Task(rep_scatter(qkv_blocks, True))
    run(scatter_a, scatter_qkv)
    run(scatter_a, scatter_qkv, gather_low)
    finish(scatter_qkv, scatter_a, gather_low)
    recut_qkv_grad = Task(chip_exchange(jnp.concatenate(scatter_qkv.value, axis=0)))
    run(recut_qkv_grad, gather_high, scatter_output)
    finish(scatter_output)
    gather_output = Task(rep_gather(scatter_output.value, True))
    grad_streams, mixing_sum, static_sum = token_call(
        first_back_kernel, tokens,
        [x, packed, static[0], tie(grad_middle), grad_beta, mixing_rows[0], mixing_mean[0], *scatter_a.value],
        [shape((tokens, count, width), F32), shape((LANES, width), F32), shape((8, LANES), F32)],
    )
    run(recut_qkv_grad, gather_high)
    hold(grad_streams)
    finish(recut_qkv_grad, gather_high)
    gather_qkv_grad = Task(rep_gather(stack_units(recut_qkv_grad.value, 2), True))
    mixing_sums = jnp.stack([mixing_sum, mixing_sum_next])
    mixing_sums = (mixing_sums[:, :6] + mixing_sums[:, 8:14]).reshape(12, shards, -1)
    small = jnp.concatenate(
        [
            jnp.pad(mixing_sums.transpose(1, 0, 2), ((0, 0), (0, 4), (0, 0))),
            jnp.broadcast_to(jnp.concatenate([static_sum, static_sum_next])[None], (shards, 16, LANES)),
        ],
        axis=2,
    )
    sum_last = Task(sum_small(small))
    run(sum_last, gather_qkv_grad, gather_output)
    gate_rows, up_rows = columns_join([[tie(v) for v in u] for u in gather_low.value + gather_high.value], 2)
    down_rows = rows_join([[tie(v) for v in u] for u in gather_down_rows.value])
    run(sum_last, gather_qkv_grad)
    hold(gate_rows, down_rows)
    run(sum_last, gather_output)
    finish(gather_qkv_grad, sum_last, gather_output)
    output_rows = rows_join(gather_output.value)
    small = sum_last.value
    rows = width // shards
    own_mixing = jnp.swapaxes(small[:12, :rows].reshape(2, 6, rows), 1, 2)
    static_sums = jnp.stack([small[0:count, rows : rows + 6], small[8 : 8 + count, rows : rows + 6]])
    query_rows, key_rows, value_rows = columns_join(gather_qkv_grad.value, 3)
    return (
        result, grad_streams, query_rows, key_rows, value_rows, output_rows,
        gate_rows, up_rows, down_rows, own_mixing, static_sums,
    )


def solution(mesh):
    tokens = P(("rep", "shard"), None, None)
    rows = P("shard", None)
    return jax.shard_map(
        per_device,
        mesh=mesh,
        in_specs=(tokens, tokens, P("rep", None), P("rep", None)) + (rows,) * 7 + (P(None, "shard", None), P()),
        out_specs=(tokens, tokens) + (rows,) * 7 + (P(None, "shard", None), P()),
        check_vma=False,
    )
```
